32 devices in a mesh: parts: 2 (over y), branch: 4 (over x, core), tensor: 4 (over z).
Axes of the slice: x: 2, y: 2, z: 4, core: 2. Of those that a mesh axis runs over, the one named last changes fastest.
Arguments:
- layer_input: bfloat16 [2048, 3584], P(('parts', 'branch')), parts along dimension 0
- norm_gain: float32 [3584], replicated, may hold values from -2.5 to 2.5
- w_query: bfloat16 [3584, 4096], P(None, 'tensor'), may hold values from -0.09375 to 0.09375
- w_key: bfloat16 [3584, 2048], P(None, 'tensor'), may hold values from -0.09375 to 0.09375
- w_value: bfloat16 [3584, 2048], P(None, 'tensor'), may hold values from -0.09375 to 0.09375
- head_grad: bfloat16 [2048, 4096], P(('parts', 'branch'), 'tensor'), parts along dimension 0, may hold values from -6 to 6
- parents: int32 [2048], P(('parts', 'branch')), parts along dimension 0, may hold values from -1 to 126, as said below
- row_counts: int32 [16], P('parts'), parts along dimension 0, may hold values from 0 to 128, as said below
Outputs:
- grad_input: bfloat16 [2048, 3584], P(('parts', 'branch'), 'tensor'), parts along dimension 0
- grad_query: float32 [7168, 4096], P(('parts', 'branch'), 'tensor'), parts along dimension 0
- grad_key: float32 [7168, 2048], P(('parts', 'branch'), 'tensor'), parts along dimension 0
- grad_value: float32 [7168, 2048], P(('parts', 'branch'), 'tensor'), parts along dimension 0
- grad_gain: float32 [7168], P(('parts', 'tensor')), parts along dimension 0
The draws below stay inside these ranges and needn't reach their ends.
There are 2 independent parts, one for each index of `parts`. The reference program is written for one: setup_inputs(seed, part) draws one part's arguments, and reference() takes and returns one part's arrays. A program takes and returns all parts, laid end to end along the dimension named above; an argument that names none is the same for every part. Nothing has to cross between parts.
Inputs may be any that keep to these rules, and one draw needn't show every extreme that they name: `row_counts`: the 2 blocks of one branch index (blocks b * 2 to b * 2 + 1) hold their live trees first; a live tree has 32 to 128 rows, an empty block 0. `parents`: inside its block a row's parent is an earlier row of that block; the first row of every block has parent -1.
All inputs are finite; a program needn't handle non-finite values.
Results may differ from the reference program's by a relative error of at most 0.011.
Values may be sent and summed in bfloat16 or wider, within the bound.
No kernel may reach another device: no remote copies, remote signals or barrier semaphores. Data moves between devices by JAX's collectives and lax.ppermute only.
A program may use at most 128 MiB of HBM per device.

```python
import math
import jax
import jax.numpy as jnp
from jax import lax

D = 3584
HEADS = 16
KV_HEADS = 8
HEAD_DIM = 256
BLOCK = 128
SLOTS = 2
TREES = 8
TOKENS = 1024


def draw_layer_input(key, part):
    key = jax.random.fold_in(key, 11)
    noise_key, row_key, column_key = jax.random.split(key, 3)
    noise = jax.random.normal(noise_key, (TOKENS, D), jnp.float32)
    top_scale = 10.0
    row_scale = jnp.exp(jax.random.uniform(row_key, (TOKENS, 1), jnp.float32, 0.0, 1.0) * math.log(top_scale))
    column_scale = jnp.exp(jax.random.uniform(column_key, (1, D), jnp.float32, 0.0, 1.0) * math.log(10.0))
    return (0.2 * noise * row_scale * column_scale).astype(jnp.bfloat16)


def draw_parents(key, part):
    key = jax.random.fold_in(key, 23)
    jump_key, choose_key = jax.random.split(key)
    position = jnp.arange(TOKENS, dtype=jnp.int32) % BLOCK
    jumped = jax.random.randint(jump_key, (TOKENS,), 0, jnp.maximum(position, 1), dtype=jnp.int32)
    chooser = jax.random.randint(choose_key, (TOKENS,), 0, 4, dtype=jnp.int32)
    parent_rows = jnp.where(chooser == 0, jumped, position - 1)
    return jnp.where(position == 0, -1, parent_rows).astype(jnp.int32)


def draw_row_counts(key, part):
    key = jax.random.fold_in(key, 37)
    load_key, rows_key = jax.random.split(key)
    groups = TREES // SLOTS
    live_trees = jax.random.randint(load_key, (groups, 1), 0, SLOTS + 1, dtype=jnp.int32)
    tree_rows = jax.random.randint(rows_key, (groups, SLOTS), BLOCK // 4, BLOCK + BLOCK // 2, dtype=jnp.int32)
    tree_rows = jnp.minimum(tree_rows, BLOCK)
    slot_index = jnp.arange(SLOTS, dtype=jnp.int32)[None, :]
    return jnp.where(slot_index < live_trees, tree_rows, 0).reshape(TREES).astype(jnp.int32)


def block_scale(stream_key, extent, cuts, least, largest):
    gain = 1.0
    for dim, parts in cuts:
        draws = jax.random.uniform(jax.random.fold_in(jax.random.fold_in(stream_key, 6), dim), (parts,), jnp.float32, least / len(cuts), largest / len(cuts))
        gain = gain * jnp.repeat(jnp.exp(draws), extent[dim] // parts).reshape((-1,) + (1,) * (len(extent) - 1 - dim))
    return gain


def gaussian(key, dims, width, most, cuts=(), kind=jnp.bfloat16):
    array = width * jax.random.normal(key, dims, jnp.float32)
    if cuts:
        array = array * block_scale(key, dims, cuts, -0.22, 0.18)
    return jnp.clip(array, -most, most).astype(kind)


def setup_inputs(seed: int = 0, part: int = 0) -> dict:
    splits = jax.random.split(jax.random.key(seed), 9)
    part_splits = jax.random.split(jax.random.fold_in(splits[8], part), 9)
    return {
        "layer_input": draw_layer_input(jax.random.fold_in(jax.random.fold_in(splits[8], part), 71), part),
        "norm_gain": gaussian(splits[1], (D,), 0.5, 2.5, (), jnp.float32),
        "w_query": gaussian(splits[2], (D, HEADS * HEAD_DIM), D ** -0.5, 0.09375, ((1, 4),)),
        "w_key": gaussian(splits[3], (D, KV_HEADS * HEAD_DIM), D ** -0.5, 0.09375, ((1, 4),)),
        "w_value": gaussian(splits[4], (D, KV_HEADS * HEAD_DIM), D ** -0.5, 0.09375, ((1, 4),)),
        "head_grad": gaussian(part_splits[5], (TOKENS, HEADS * HEAD_DIM), 1.0, 6.0, ((0, 4), (1, 4))),
        "parents": draw_parents(jax.random.fold_in(jax.random.fold_in(splits[8], part), 71), part),
        "row_counts": draw_row_counts(jax.random.fold_in(jax.random.fold_in(splits[8], part), 71), part),
    }


epsilon = 1e-06
softcap_limit = 50.0

def ancestor_mask(parent_rows):
    row_total = parent_rows.shape[0]
    position = jnp.arange(row_total, dtype=jnp.int32)
    reached = (parent_rows[:, None] == position[None, :]).astype(jnp.float32)
    reached = reached + (position[:, None] == position[None, :]).astype(jnp.float32)
    for squaring in range(row_total.bit_length() - 1):
        halfway = reached.astype(jnp.bfloat16)
        reached = jnp.minimum(jnp.dot(halfway, halfway, preferred_element_type=jnp.float32), 1.0)
    return reached > 0.5

def normalize(tree_input, norm_gain):
    values = tree_input.astype(jnp.float32)
    inverse = lax.rsqrt(lax.optimization_barrier(jnp.mean(values * values, axis=-1, keepdims=True)) + epsilon)
    scaled = values * inverse
    normed = (scaled * (1.0 + norm_gain)).astype(jnp.bfloat16)
    return (inverse, scaled, normed)

def attention_backward(normed, tree_grad, parent_rows, row_count, w_query, w_key, w_value, kv_heads, head_dim):
    row_total = normed.shape[0]
    queries = jnp.dot(normed, w_query, preferred_element_type=jnp.float32).astype(jnp.bfloat16)
    key_rows = jnp.dot(normed, w_key, preferred_element_type=jnp.float32).astype(jnp.bfloat16)
    value_rows = jnp.dot(normed, w_value, preferred_element_type=jnp.float32).astype(jnp.bfloat16)
    group_size = queries.shape[1] // head_dim // kv_heads
    query_four = queries.reshape(row_total, kv_heads, group_size, head_dim).astype(jnp.float32)
    key_three = key_rows.reshape(row_total, kv_heads, head_dim).astype(jnp.float32)
    value_three = value_rows.reshape(row_total, kv_heads, head_dim).astype(jnp.float32)
    live_rows = jnp.arange(row_total, dtype=jnp.int32) < row_count
    grad_live = jnp.where(live_rows[:, None], tree_grad, jnp.zeros_like(tree_grad))
    grad_four = grad_live.reshape(row_total, kv_heads, group_size, head_dim).astype(jnp.float32)
    scale_factor = head_dim ** (-0.5)
    scores = jnp.einsum('ikgd,jkd->kgij', query_four, key_three) * scale_factor
    bounded = jnp.tanh(scores / softcap_limit)
    allowed = ancestor_mask(parent_rows)
    weights = jnp.where(allowed[None, None], jnp.exp(softcap_limit * bounded), 0.0)
    probabilities = weights / lax.optimization_barrier(jnp.sum(weights, axis=-1, keepdims=True))
    d_probs = jnp.einsum('ikgd,jkd->kgij', grad_four, value_three)
    d_scores = probabilities * (d_probs - lax.optimization_barrier(jnp.sum(probabilities * d_probs, axis=-1, keepdims=True)))
    d_raw = (d_scores * (1.0 - bounded * bounded) * scale_factor).astype(jnp.bfloat16).astype(jnp.float32)
    prob_half = probabilities.astype(jnp.bfloat16).astype(jnp.float32)
    d_query = jnp.einsum('kgij,jkd->ikgd', d_raw, key_three).reshape(row_total, -1).astype(jnp.bfloat16)
    d_key = jnp.einsum('kgij,ikgd->jkd', d_raw, query_four).reshape(row_total, -1).astype(jnp.bfloat16)
    d_value = jnp.einsum('kgij,ikgd->jkd', prob_half, grad_four).reshape(row_total, -1).astype(jnp.bfloat16)
    return (d_query, d_key, d_value)

def transpose_dot(left, right):
    return lax.dot_general(left, right, (((0,), (0,)), ((), ())), preferred_element_type=jnp.float32)

def back_dot(left, right):
    return lax.dot_general(left, right, (((1,), (1,)), ((), ())), preferred_element_type=jnp.float32)

def reference(layer_input, norm_gain, w_query, w_key, w_value, head_grad, parents, row_counts):
    inputs_t = layer_input.reshape(TREES, BLOCK, D)
    grads_t = head_grad.reshape(TREES, BLOCK, HEADS * HEAD_DIM)
    parents_t = parents.reshape(TREES, BLOCK)

    def one_tree(carried_state, pieces):
        acc_query, acc_key, acc_value, acc_gain = carried_state
        tree_input, tree_grad, parent_rows, row_count = pieces
        inverse, scaled, normed = normalize(tree_input, norm_gain)
        d_query, d_key, d_value = attention_backward(normed, tree_grad, parent_rows, row_count, w_query, w_key, w_value, KV_HEADS, HEAD_DIM)
        d_normed = back_dot(d_query, w_query) + back_dot(d_key, w_key) + back_dot(d_value, w_value)
        adjusted = (1.0 + norm_gain) * d_normed
        centred = lax.optimization_barrier(jnp.mean(scaled * adjusted, axis=-1, keepdims=True))
        grad_input = (inverse * (adjusted - scaled * centred)).astype(jnp.bfloat16)
        acc_query = acc_query + transpose_dot(normed, d_query)
        acc_key = acc_key + transpose_dot(normed, d_key)
        acc_value = acc_value + transpose_dot(normed, d_value)
        acc_gain = acc_gain + lax.optimization_barrier(jnp.sum(d_normed * scaled, axis=0))
        return ((acc_query, acc_key, acc_value, acc_gain), grad_input)
    initial = (jnp.zeros((D, HEADS * HEAD_DIM), jnp.float32), jnp.zeros((D, KV_HEADS * HEAD_DIM), jnp.float32), jnp.zeros((D, KV_HEADS * HEAD_DIM), jnp.float32), jnp.zeros((D,), jnp.float32))
    finals, grad_rows = lax.scan(one_tree, initial, (inputs_t, grads_t, parents_t, row_counts))
    return (grad_rows.reshape(TOKENS, D), finals[0], finals[1], finals[2], finals[3])
```

```python
import functools

import jax
import jax.numpy as jnp
from jax import lax
from jax.experimental import pallas as pl
from jax.experimental.pallas import tpu as pltpu
from jax.sharding import PartitionSpec as P

HEAD_DIM = 256
MIB = 1024 * 1024

epsilon = 1e-06
softcap_limit = 50.0


def nn_dot(left, right):
    return lax.dot_general(
        left, right, (((1,), (0,)), ((), ())), preferred_element_type=jnp.float32
    )


def nt_dot(left, right):
    return lax.dot_general(
        left, right, (((1,), (1,)), ((), ())), preferred_element_type=jnp.float32
    )


def tn_dot(left, right):
    return lax.dot_general(
        left, right, (((0,), (0,)), ((), ())), preferred_element_type=jnp.float32
    )


def norm_kernel(targets, input_ref, gain_ref, normed_ref, inverse_ref, *rest):
    piece_refs, turned = rest[:-1], rest[-1]
    rows, width = input_ref.shape
    values = input_ref[...].astype(jnp.float32)
    inverse = lax.rsqrt(jnp.mean(values * values, axis=-1, keepdims=True) + epsilon)
    inverse_ref[...] = inverse
    normed = (values * inverse * (1.0 + gain_ref[...])).astype(jnp.bfloat16)
    normed_ref[...] = normed
    turned[...] = normed.T
    depth = width // len(piece_refs)
    for target, piece_ref in zip(targets(), piece_refs):
        start = pl.multiple_of(target * depth, 16)
        piece_ref[...] = turned[pl.ds(start, depth), :]


def normalize(layer_input, norm_gain, targets, pieces):
    rows, width = layer_input.shape
    vmem = pl.BlockSpec(memory_space=pltpu.VMEM)
    out = pl.pallas_call(
        functools.partial(norm_kernel, targets),
        out_shape=(
            jax.ShapeDtypeStruct((rows, width), jnp.bfloat16),
            jax.ShapeDtypeStruct((rows, 1), jnp.float32),
        )
        + (jax.ShapeDtypeStruct((width // pieces, rows), jnp.bfloat16),) * pieces,
        in_specs=[vmem, vmem],
        out_specs=(vmem,) * (2 + pieces),
        scratch_shapes=[pltpu.VMEM((width, rows), jnp.bfloat16)],
        compiler_params=pltpu.CompilerParams(vmem_limit_bytes=40 * MIB),
        name="norm",
    )(layer_input, norm_gain.reshape(1, width))
    return out[0], out[1], out[2:]


def ancestor_mask(parent_column):
    rows = parent_column.shape[0]
    row = lax.broadcasted_iota(jnp.int32, (rows, rows), 0)
    column = lax.broadcasted_iota(jnp.int32, (rows, rows), 1)
    reached = jnp.where((parent_column == column) | (row == column), 1.0, 0.0)
    for squaring in range(rows.bit_length() - 1):
        halfway = reached.astype(jnp.bfloat16)
        reached = jnp.minimum(nn_dot(halfway, halfway), 1.0)
    return reached


def attention_kernel(
    slots,
    count_ref,
    normed_ref,
    query_ref,
    key_ref,
    value_ref,
    grad_ref,
    parent_ref,
    delta_ref,
    centre_ref,
    allowed_ref,
):
    head_dim = HEAD_DIM
    block = normed_ref.shape[0] // slots
    group = query_ref.shape[1] // head_dim
    step = pl.program_id(0)

    @pl.when(step == 0)
    def _():
        centre_ref[...] = jnp.zeros_like(centre_ref)
        for slot in range(slots):
            allowed_ref[slot] = ancestor_mask(parent_ref[slot * block : (slot + 1) * block, :])

    normed = normed_ref[...]
    query_sum = nn_dot(normed, query_ref[...])
    key_sum = nn_dot(normed, key_ref[...])
    value_sum = nn_dot(normed, value_ref[...])
    scale = head_dim ** (-0.5)
    for slot in range(slots):
        rows = slice(slot * block, (slot + 1) * block)
        query_parts = [
            query_sum[rows, g * head_dim : (g + 1) * head_dim] for g in range(group)
        ]
        queries = jnp.concatenate(query_parts, axis=0).astype(jnp.bfloat16)
        keys = key_sum[rows].astype(jnp.bfloat16)
        values = value_sum[rows].astype(jnp.bfloat16)
        live = lax.broadcasted_iota(jnp.int32, (block, head_dim), 0) < count_ref[slot]
        grads = jnp.concatenate(
            [
                jnp.where(
                    live,
                    grad_ref[rows, g * head_dim : (g + 1) * head_dim].astype(jnp.float32),
                    0.0,
                )
                for g in range(group)
            ],
            axis=0,
        ).astype(jnp.bfloat16)
        allowed = jnp.concatenate([allowed_ref[slot]] * group, axis=0) > 0.5
        bounded = jnp.tanh(nt_dot(queries, keys) * (scale / softcap_limit))
        weights = jnp.where(allowed, jnp.exp(softcap_limit * bounded), 0.0)
        probabilities = weights / jnp.sum(weights, axis=-1, keepdims=True)
        d_probs = nt_dot(grads, values)
        d_scores = probabilities * (
            d_probs - jnp.sum(probabilities * d_probs, axis=-1, keepdims=True)
        )
        d_raw = (d_scores * (1.0 - bounded * bounded) * scale).astype(jnp.bfloat16)
        prob_half = probabilities.astype(jnp.bfloat16)
        d_query = nn_dot(d_raw, keys).astype(jnp.bfloat16)
        d_key = tn_dot(d_raw, queries).astype(jnp.bfloat16)
        d_value = tn_dot(prob_half, grads).astype(jnp.bfloat16)
        centre = jnp.sum(
            d_key.astype(jnp.float32) * key_sum[rows]
            + d_value.astype(jnp.float32) * value_sum[rows],
            axis=-1,
            keepdims=True,
        )
        for g in range(group):
            part = d_query[g * block : (g + 1) * block]
            delta_ref[rows, g * head_dim : (g + 1) * head_dim] = part
            centre += jnp.sum(
                part.astype(jnp.float32) * query_parts[g], axis=-1, keepdims=True
            )
        delta_ref[rows, group * head_dim : (group + 1) * head_dim] = d_key
        delta_ref[rows, (group + 1) * head_dim : (group + 2) * head_dim] = d_value
        centre_ref[rows, :] += centre


def attention_backward(normed, w_query, w_key, w_value, head_grad, parents, counts):
    rows, width = normed.shape
    slots = counts.shape[0]
    kv_local = w_key.shape[1] // HEAD_DIM
    group = w_query.shape[1] // w_key.shape[1]
    delta_width = (group + 2) * HEAD_DIM
    block = rows // slots
    whole = lambda h: (0, 0)
    by_head = lambda h: (0, h)
    return pl.pallas_call(
        functools.partial(attention_kernel, slots),
        out_shape=(
            jax.ShapeDtypeStruct((rows, kv_local * delta_width), jnp.bfloat16),
            jax.ShapeDtypeStruct((rows, 1), jnp.float32),
        ),
        grid=(kv_local,),
        in_specs=[
            pl.BlockSpec(memory_space=pltpu.SMEM),
            pl.BlockSpec((rows, width), whole),
            pl.BlockSpec((width, group * HEAD_DIM), by_head),
            pl.BlockSpec((width, HEAD_DIM), by_head),
            pl.BlockSpec((width, HEAD_DIM), by_head),
            pl.BlockSpec((rows, group * HEAD_DIM), by_head),
            pl.BlockSpec((rows, 1), whole),
        ],
        out_specs=(
            pl.BlockSpec((rows, delta_width), by_head),
            pl.BlockSpec((rows, 1), whole),
        ),
        scratch_shapes=[pltpu.VMEM((slots, block, block), jnp.float32)],
        compiler_params=pltpu.CompilerParams(vmem_limit_bytes=48 * MIB),
        name="attention",
    )(counts, normed, w_query, w_key, w_value, head_grad, parents.reshape(rows, 1))


def back_kernel(order_ref, delta_ref, query_ref, key_ref, value_ref, *out_refs):
    del order_ref
    step = pl.program_id(0)
    head_dim = HEAD_DIM
    kv_local = key_ref.shape[1] // head_dim
    group = query_ref.shape[1] // key_ref.shape[1]
    span = (group + 2) * head_dim
    total = None
    for h in range(kv_local):
        base = h * span
        mid = base + group * head_dim
        term = nt_dot(
            delta_ref[:, base:mid],
            query_ref[:, h * group * head_dim : (h + 1) * group * head_dim],
        )
        term += nt_dot(
            delta_ref[:, mid : mid + head_dim], key_ref[:, h * head_dim : (h + 1) * head_dim]
        )
        term += nt_dot(
            delta_ref[:, mid + head_dim : mid + 2 * head_dim],
            value_ref[:, h * head_dim : (h + 1) * head_dim],
        )
        total = term if total is None else total + term
    total = total.astype(jnp.bfloat16)
    for place, out_ref in enumerate(out_refs):

        @pl.when(step == place)
        def _():
            out_ref[...] = total


def back_project(order, delta, w_query, w_key, w_value):
    rows = delta.shape[0]
    pieces = order.shape[0]
    depth = w_query.shape[0] // pieces
    picked = lambda i, order: (order[i], 0)
    whole = lambda i, order: (0, 0)
    return pl.pallas_call(
        back_kernel,
        out_shape=(jax.ShapeDtypeStruct((rows, depth), jnp.bfloat16),) * pieces,
        grid_spec=pltpu.PrefetchScalarGridSpec(
            num_scalar_prefetch=1,
            grid=(pieces,),
            in_specs=[
                pl.BlockSpec(delta.shape, whole),
                pl.BlockSpec((depth, w_query.shape[1]), picked),
                pl.BlockSpec((depth, w_key.shape[1]), picked),
                pl.BlockSpec((depth, w_value.shape[1]), picked),
            ],
            out_specs=(pl.BlockSpec((rows, depth), whole),) * pieces,
        ),
        compiler_params=pltpu.CompilerParams(vmem_limit_bytes=48 * MIB),
        name="back",
    )(order, delta, w_query, w_key, w_value)


def weight_kernel(group, *refs):
    sources = (len(refs) - 3) // 2
    turned_refs, delta_refs = refs[:sources], refs[sources : 2 * sources]
    query_ref, key_ref, value_ref = refs[2 * sources :]
    total = None
    for turned_ref, delta_ref in zip(turned_refs, delta_refs):
        term = nn_dot(turned_ref[...], delta_ref[...])
        total = term if total is None else total + term
    mid = group * HEAD_DIM
    query_ref[...] = total[:, :mid]
    key_ref[...] = total[:, mid : mid + HEAD_DIM]
    value_ref[...] = total[:, mid + HEAD_DIM :]


def weight_gradients(turned, deltas, group):
    depth, rows = turned[0].shape
    span = (group + 2) * HEAD_DIM
    kv_local = deltas[0].shape[1] // span
    cuts = 2
    cut = depth // cuts
    out_block = lambda h, i: (i, h)
    return pl.pallas_call(
        functools.partial(weight_kernel, group),
        out_shape=(
            jax.ShapeDtypeStruct((depth, kv_local * group * HEAD_DIM), jnp.float32),
            jax.ShapeDtypeStruct((depth, kv_local * HEAD_DIM), jnp.float32),
            jax.ShapeDtypeStruct((depth, kv_local * HEAD_DIM), jnp.float32),
        ),
        grid=(kv_local, cuts),
        in_specs=[pl.BlockSpec((cut, rows), lambda h, i: (i, 0))] * len(turned)
        + [pl.BlockSpec((rows, span), lambda h, i: (0, h))] * len(deltas),
        out_specs=(
            pl.BlockSpec((cut, group * HEAD_DIM), out_block),
            pl.BlockSpec((cut, HEAD_DIM), out_block),
            pl.BlockSpec((cut, HEAD_DIM), out_block),
        ),
        compiler_params=pltpu.CompilerParams(vmem_limit_bytes=48 * MIB),
        name="weights",
    )(*turned, *deltas)


def branch_send(array, chips, shift, swap):
    pairs = [
        (c * 2 + k, ((c + shift) % chips) * 2 + (k ^ swap)) for c in range(chips) for k in range(2)
    ]
    return lax.ppermute(array, "branch", pairs)


def local(layer_input, norm_gain, w_query, w_key, w_value, head_grad, parents, row_counts):
    branch_total = lax.axis_size("branch")
    branch_index = lax.axis_index("branch")
    tensor_total = lax.axis_size("tensor")
    tensor_index = lax.axis_index("tensor")
    slots = row_counts.shape[0] // branch_total
    rows, width = layer_input.shape
    column_width = width // tensor_total
    chips = branch_total // 2
    group = w_query.shape[1] // w_key.shape[1]
    own_counts = lax.dynamic_slice_in_dim(row_counts, branch_index * slots, slots, 0)
    offsets = [(shift, swap) for shift in range(chips) for swap in range(2)]

    def targets():
        index = lax.axis_index("branch")
        chip, core = index // 2, index % 2
        return [lax.rem(chip + s, chips) * 2 + lax.rem(core + e, 2) for s, e in offsets]

    normed, inverse, pieces = normalize(layer_input, norm_gain, targets, branch_total)
    turned = [
        piece if (s, e) == (0, 0) else branch_send(piece, chips, s, e)
        for piece, (s, e) in zip(pieces, offsets)
    ]
    delta, centre_part = attention_backward(
        normed, w_query, w_key, w_value, head_grad, parents, own_counts
    )
    direct = [delta] + [branch_send(delta, chips, s, 0) for s in range(1, chips)]
    deltas = []
    for part in direct:
        deltas += [part, branch_send(part, chips, 0, 1)]
    centre = lax.psum(centre_part, "tensor") * (1.0 / width)

    shifts = list(range(1, tensor_total)) + [0]
    order = lax.rem(tensor_index + jnp.array(shifts, jnp.int32), tensor_total)
    partials = back_project(order, delta, w_query, w_key, w_value)
    d_normed = partials[-1].astype(jnp.float32)
    for shift, partial in zip(shifts[:-1], partials[:-1]):
        pairs = [(t, (t + shift) % tensor_total) for t in range(tensor_total)]
        d_normed = d_normed + lax.ppermute(partial, "tensor", pairs).astype(jnp.float32)

    column_start = tensor_index * column_width
    input_columns = lax.dynamic_slice_in_dim(layer_input, column_start, column_width, 1)
    gain_columns = lax.dynamic_slice_in_dim(norm_gain, column_start, column_width, 0)
    scaled = input_columns.astype(jnp.float32) * inverse
    grad_input = (inverse * ((1.0 + gain_columns) * d_normed - scaled * centre)).astype(
        jnp.bfloat16
    )
    grad_gain = lax.psum(jnp.sum(d_normed * scaled, axis=0), "branch")
    grad_query, grad_key, grad_value = weight_gradients(turned, deltas, group)
    return (grad_input, grad_query, grad_key, grad_value, grad_gain)


def solution(mesh):
    placed = (
        P(("parts", "branch"), None),
        P(),
        P(None, "tensor"),
        P(None, "tensor"),
        P(None, "tensor"),
        P(("parts", "branch"), "tensor"),
        P(("parts", "branch")),
        P("parts"),
    )
    return jax.shard_map(
        local,
        mesh=mesh,
        in_specs=placed,
        out_specs=(
            P(("parts", "branch"), "tensor"),
            P(("parts", "branch"), "tensor"),
            P(("parts", "branch"), "tensor"),
            P(("parts", "branch"), "tensor"),
            P(("parts", "tensor")),
        ),
        check_vma=False,
    )
```

```python
import functools

import jax
import jax.numpy as jnp
from jax import lax
from jax.experimental import pallas as pl
from jax.experimental.pallas import tpu as pltpu
from jax.sharding import PartitionSpec as P

HEAD_DIM = 256
MIB = 1024 * 1024
CENTRE_ROWS = 16


epsilon = 1e-06
softcap_limit = 50.0


def nn_dot(left, right):
    return lax.dot_general(
        left, right, (((1,), (0,)), ((), ())), preferred_element_type=jnp.float32
    )


def nt_dot(left, right):
    return lax.dot_general(
        left, right, (((1,), (1,)), ((), ())), preferred_element_type=jnp.float32
    )


def tn_dot(left, right):
    return lax.dot_general(
        left, right, (((0,), (0,)), ((), ())), preferred_element_type=jnp.float32
    )


def cost(flops, count):
    return pl.CostEstimate(flops=flops, bytes_accessed=count, transcendentals=0)


def norm_kernel(targets, input_ref, gain_ref, normed_ref, inverse_ref, *rest):
    piece_refs, turned = rest[:-1], rest[-1]
    rows, width = input_ref.shape
    values = input_ref[...].astype(jnp.float32)
    inverse = lax.rsqrt(jnp.mean(values * values, axis=-1, keepdims=True) + epsilon)
    inverse_ref[...] = inverse
    gain = gain_ref[...].reshape(1, width)
    normed = (values * inverse * (1.0 + gain)).astype(jnp.bfloat16)
    normed_ref[...] = normed
    turned[...] = normed.T
    depth = width // len(piece_refs)
    for target, piece_ref in zip(targets(), piece_refs):
        start = pl.multiple_of(target * depth, 16)
        piece_ref[...] = turned[pl.ds(start, depth), :]


def normalize(layer_input, norm_gain, targets, pieces, block):
    rows, width = layer_input.shape
    depth = width // pieces
    out = pl.pallas_call(
        functools.partial(norm_kernel, targets),
        out_shape=(
            jax.ShapeDtypeStruct((rows, width), jnp.bfloat16),
            jax.ShapeDtypeStruct((rows, 1), jnp.float32),
        )
        + (jax.ShapeDtypeStruct((depth, rows), jnp.bfloat16),) * pieces,
        grid=(rows // block,),
        in_specs=[
            pl.BlockSpec((block, width), lambda i: (i, 0)),
            pl.BlockSpec((width,), lambda i: (0,)),
        ],
        out_specs=(
            pl.BlockSpec((block, width), lambda i: (i, 0)),
            pl.BlockSpec((block, 1), lambda i: (i, 0)),
        )
        + (pl.BlockSpec((depth, block), lambda i: (0, i)),) * pieces,
        scratch_shapes=[pltpu.VMEM((width, block), jnp.bfloat16)],
        compiler_params=pltpu.CompilerParams(vmem_limit_bytes=40 * MIB),
        cost_estimate=cost(10 * rows * width, 6 * rows * width),
        name="norm",
    )(layer_input, norm_gain)
    return out[0], out[1], out[2:]


def ancestor_mask(parent_row):
    rows = parent_row.shape[1]
    row = lax.broadcasted_iota(jnp.int32, (rows, rows), 0)
    column = lax.broadcasted_iota(jnp.int32, (rows, rows), 1)
    reached = jnp.where((parent_row == row) | (row == column), 1.0, 0.0)
    for squaring in range(rows.bit_length() - 1):
        halfway = reached.astype(jnp.bfloat16)
        reached = jnp.minimum(nn_dot(halfway, halfway), 1.0)
    return reached.T


def attention_kernel(
    slots,
    kv_local,
    cuts,
    count_ref,
    parent_ref,
    normed_hbm,
    query_hbm,
    key_hbm,
    value_hbm,
    grad_hbm,
    *rest,
):
    delta_hbm = rest[:kv_local]
    turned_hbm, centre_ref, normed_ref, query_ref, key_ref, value_ref, grad_ref = rest[
        kv_local : kv_local + 7
    ]
    delta_ref, turned_ref, load_sem, weight_sem, store_sem = rest[kv_local + 7 :]
    head_dim = HEAD_DIM
    rows, width = normed_ref.shape
    block = rows // slots
    group = query_ref.shape[2] // head_dim
    span = (group + 2) * head_dim
    depth = width // cuts

    def fetch(h, cut, which):
        source, kept = ((query_hbm, query_ref), (key_hbm, key_ref), (value_hbm, value_ref))[which]
        wide = kept.shape[2]
        lines = pl.ds(cut * depth, depth)
        return pltpu.make_async_copy(
            source.at[lines, pl.ds(h * wide, wide)],
            kept.at[h, lines, :],
            weight_sem.at[h, cut, which],
        )

    loads = [
        pltpu.make_async_copy(normed_hbm, normed_ref, load_sem.at[0]),
        pltpu.make_async_copy(grad_hbm, grad_ref, load_sem.at[1]),
    ]
    loads[0].start()
    for cut in range(cuts):
        for which in range(3):
            fetch(0, cut, which).start()
    loads[1].start()
    for h in range(1, kv_local):
        for cut in range(cuts):
            for which in range(3):
                fetch(h, cut, which).start()

    first_count = lax.axis_index("branch") * slots
    parents = parent_ref[...].reshape(1, rows)
    allowed_slots = [
        ancestor_mask(parents[:, slot * block : (slot + 1) * block]) for slot in range(slots)
    ]
    scale = head_dim ** (-0.5)
    centre_parts = [jnp.zeros((block, 1), jnp.float32) for _ in range(slots)]
    stores = []
    for h in range(kv_local):
        sums = [None, None, None]
        for cut in range(cuts):
            if h == 0 and cut == 0:
                loads[0].wait()
            lines = slice(cut * depth, (cut + 1) * depth)
            for which, kept in enumerate((query_ref, key_ref, value_ref)):
                fetch(h, cut, which).wait()
                term = nn_dot(normed_ref[:, lines], kept[h, lines, :])
                sums[which] = term if sums[which] is None else sums[which] + term
        query_sum, key_sum, value_sum = sums
        if h == 0:
            loads[1].wait()
        for slot in range(slots):
            lines = slice(slot * block, (slot + 1) * block)
            query_parts = [
                query_sum[lines, g * head_dim : (g + 1) * head_dim] for g in range(group)
            ]
            queries = jnp.concatenate(query_parts, axis=0).astype(jnp.bfloat16)
            keys = key_sum[lines].astype(jnp.bfloat16)
            values = value_sum[lines].astype(jnp.bfloat16)
            live = (
                lax.broadcasted_iota(jnp.int32, (block, head_dim), 0)
                < count_ref[first_count + slot]
            )
            base = h * group * head_dim
            grads = jnp.concatenate(
                [
                    jnp.where(
                        live,
                        grad_ref[
                            lines, base + g * head_dim : base + (g + 1) * head_dim
                        ].astype(jnp.float32),
                        0.0,
                    )
                    for g in range(group)
                ],
                axis=0,
            ).astype(jnp.bfloat16)
            allowed = jnp.concatenate([allowed_slots[slot]] * group, axis=0)
            bounded = jnp.tanh(nt_dot(queries, keys) * (scale / softcap_limit))
            weights = allowed * jnp.exp(softcap_limit * bounded)
            probabilities = weights * (1.0 / jnp.sum(weights, axis=-1, keepdims=True))
            d_probs = nt_dot(grads, values)
            d_scores = probabilities * (
                d_probs - jnp.sum(probabilities * d_probs, axis=-1, keepdims=True)
            )
            d_raw = (d_scores * (1.0 - bounded * bounded) * scale).astype(jnp.bfloat16)
            prob_half = probabilities.astype(jnp.bfloat16)
            d_query = nn_dot(d_raw, keys).astype(jnp.bfloat16)
            d_key = tn_dot(d_raw, queries).astype(jnp.bfloat16)
            d_value = tn_dot(prob_half, grads).astype(jnp.bfloat16)
            product = d_key.astype(jnp.float32) * key_sum[lines]
            product += d_value.astype(jnp.float32) * value_sum[lines]
            for g in range(group):
                part = d_query[g * block : (g + 1) * block]
                delta_ref[h, lines, g * head_dim : (g + 1) * head_dim] = part
                product += part.astype(jnp.float32) * query_parts[g]
            delta_ref[h, lines, group * head_dim : (group + 1) * head_dim] = d_key
            delta_ref[h, lines, (group + 1) * head_dim :] = d_value
            centre_parts[slot] += jnp.sum(product, axis=-1, keepdims=True)
        stores.append(pltpu.make_async_copy(delta_ref.at[h], delta_hbm[h], store_sem.at[h, 0]))
        stores[-1].start()
        turned_ref[h] = delta_ref[h].T
        stores.append(
            pltpu.make_async_copy(
                turned_ref.at[h], turned_hbm.at[pl.ds(h * span, span), :], store_sem.at[h, 1]
            )
        )
        stores[-1].start()
    centre = jnp.concatenate(centre_parts, axis=0)
    centre_ref[...] = jnp.broadcast_to(centre, (rows, 128)).T[:CENTRE_ROWS]
    for store in stores:
        store.wait()


def attention_backward(normed, w_query, w_key, w_value, head_grad, parents, counts, slots):
    rows, width = normed.shape
    kv_local = w_key.shape[1] // HEAD_DIM
    group = w_query.shape[1] // w_key.shape[1]
    span = (group + 2) * HEAD_DIM
    cuts = 2 if width % 512 == 0 else 1
    hbm = pl.BlockSpec(memory_space=pl.ANY)
    vmem = pl.BlockSpec(memory_space=pltpu.VMEM)
    out = pl.pallas_call(
        functools.partial(attention_kernel, slots, kv_local, cuts),
        out_shape=(jax.ShapeDtypeStruct((rows, span), jnp.bfloat16),) * kv_local
        + (
            jax.ShapeDtypeStruct((kv_local * span, rows), jnp.bfloat16),
            jax.ShapeDtypeStruct((CENTRE_ROWS, rows), jnp.float32),
        ),
        in_specs=[pl.BlockSpec(memory_space=pltpu.SMEM), vmem] + [hbm] * 5,
        out_specs=(hbm,) * (kv_local + 1) + (vmem,),
        scratch_shapes=[
            pltpu.VMEM((rows, width), jnp.bfloat16),
            pltpu.VMEM((kv_local, width, group * HEAD_DIM), jnp.bfloat16),
            pltpu.VMEM((kv_local, width, HEAD_DIM), jnp.bfloat16),
            pltpu.VMEM((kv_local, width, HEAD_DIM), jnp.bfloat16),
            pltpu.VMEM(head_grad.shape, jnp.bfloat16),
            pltpu.VMEM((kv_local, rows, span), jnp.bfloat16),
            pltpu.VMEM((kv_local, span, rows), jnp.bfloat16),
            pltpu.SemaphoreType.DMA((2,)),
            pltpu.SemaphoreType.DMA((kv_local, cuts, 3)),
            pltpu.SemaphoreType.DMA((kv_local, 2)),
        ],
        compiler_params=pltpu.CompilerParams(vmem_limit_bytes=48 * MIB),
        cost_estimate=cost(
            2 * rows * width * kv_local * span, 2 * width * (kv_local * span + rows)
        ),
        name="attention",
    )(counts, parents, normed, w_query, w_key, w_value, head_grad)
    return out[:kv_local], out[kv_local], out[kv_local + 1]


def back_kernel(
    cuts, order_ref, turned_ref, centre_ref, query_ref, key_ref, value_ref, *rest
):
    del order_ref
    pieces = (len(rest) - 2) // 1
    out_hbm, kept, store_sem = rest[:pieces], rest[pieces], rest[pieces + 1]
    piece, cut = pl.program_id(0), pl.program_id(1)
    head_dim = HEAD_DIM
    kv_local = key_ref.shape[1] // head_dim
    group = query_ref.shape[1] // key_ref.shape[1]
    span = (group + 2) * head_dim
    lines = query_ref.shape[0]
    total = None
    for h in range(kv_local):
        base = h * span
        mid = base + group * head_dim
        term = nn_dot(
            query_ref[:, h * group * head_dim : (h + 1) * group * head_dim],
            turned_ref[base:mid, :],
        )
        term += nn_dot(
            key_ref[:, h * head_dim : (h + 1) * head_dim], turned_ref[mid : mid + head_dim, :]
        )
        term += nn_dot(
            value_ref[:, h * head_dim : (h + 1) * head_dim],
            turned_ref[mid + head_dim : mid + 2 * head_dim, :],
        )
        total = term if total is None else total + term
    start = pl.multiple_of(cut * lines, 16)
    kept[piece, pl.ds(start, lines), :] = total.astype(jnp.bfloat16)

    copies = [
        pltpu.make_async_copy(kept.at[place], out_hbm[place], store_sem.at[place])
        for place in range(pieces)
    ]
    for place, copy in enumerate(copies):

        @pl.when((piece == place) & (cut == cuts - 1))
        def _():
            kept[place, cuts * lines :, :] = centre_ref[...].astype(jnp.bfloat16)
            copy.start()

    @pl.when((piece == pieces - 1) & (cut == cuts - 1))
    def _():
        for copy in copies:
            copy.wait()


def back_project(order, turned, centre, w_query, w_key, w_value, blocks):
    rows = turned.shape[1]
    pieces = order.shape[0]
    depth = w_query.shape[0] // blocks
    cuts = 2
    cut = depth // cuts
    picked = lambda i, j, order: (order[i] * cuts + j, 0)
    whole = lambda i, j, order: (0, 0)
    return pl.pallas_call(
        functools.partial(back_kernel, cuts),
        out_shape=(jax.ShapeDtypeStruct((depth + CENTRE_ROWS, rows), jnp.bfloat16),) * pieces,
        grid_spec=pltpu.PrefetchScalarGridSpec(
            num_scalar_prefetch=1,
            grid=(pieces, cuts),
            in_specs=[
                pl.BlockSpec(turned.shape, whole),
                pl.BlockSpec(centre.shape, whole),
                pl.BlockSpec((cut, w_query.shape[1]), picked),
                pl.BlockSpec((cut, w_key.shape[1]), picked),
                pl.BlockSpec((cut, w_value.shape[1]), picked),
            ],
            out_specs=(pl.BlockSpec(memory_space=pl.ANY),) * pieces,
            scratch_shapes=[
                pltpu.VMEM((pieces, depth + CENTRE_ROWS, rows), jnp.bfloat16),
                pltpu.SemaphoreType.DMA((pieces,)),
            ],
        ),
        compiler_params=pltpu.CompilerParams(vmem_limit_bytes=48 * MIB),
        cost_estimate=cost(
            2 * pieces * depth * turned.shape[0] * rows, 2 * pieces * depth * turned.shape[0]
        ),
        name="back",
    )(order, turned, centre, w_query, w_key, w_value)


def weight_kernel(group, sources, *refs):
    turned_refs, delta_refs = refs[:sources], refs[sources : 2 * sources]
    query_ref, key_ref, value_ref = refs[-3:]
    total = None
    for turned_ref, delta_ref in zip(turned_refs, delta_refs):
        term = nn_dot(turned_ref[...], delta_ref[...])
        total = term if total is None else total + term
    mid = group * HEAD_DIM
    query_ref[...] = total[:, :mid]
    key_ref[...] = total[:, mid : mid + HEAD_DIM]
    value_ref[...] = total[:, mid + HEAD_DIM :]


def weight_gradients(turned, deltas, head, kv_local, group, before):
    depth, rows = turned[0].shape
    span = (group + 2) * HEAD_DIM
    cuts = 4 if depth % 64 == 0 else 2
    cut = depth // cuts
    sources = len(turned)
    out_block = lambda i: (i, head)
    kept = list(before) if before is not None else []
    return pl.pallas_call(
        functools.partial(weight_kernel, group, sources),
        out_shape=(
            jax.ShapeDtypeStruct((depth, kv_local * group * HEAD_DIM), jnp.float32),
            jax.ShapeDtypeStruct((depth, kv_local * HEAD_DIM), jnp.float32),
            jax.ShapeDtypeStruct((depth, kv_local * HEAD_DIM), jnp.float32),
        ),
        grid=(cuts,),
        in_specs=[pl.BlockSpec((cut, rows), lambda i: (i, 0))] * sources
        + [pl.BlockSpec((rows, span), lambda i: (0, 0))] * sources
        + [pl.BlockSpec(memory_space=pl.ANY)] * len(kept),
        out_specs=(
            pl.BlockSpec((cut, group * HEAD_DIM), out_block),
            pl.BlockSpec((cut, HEAD_DIM), out_block),
            pl.BlockSpec((cut, HEAD_DIM), out_block),
        ),
        input_output_aliases={2 * sources + i: i for i in range(len(kept))},
        compiler_params=pltpu.CompilerParams(vmem_limit_bytes=48 * MIB),
        cost_estimate=cost(
            2 * sources * rows * depth * span,
            4 * depth * span + 2 * sources * rows * (depth + span),
        ),
        name="weights",
    )(*turned, *deltas, *kept)


def finish_kernel(flag_ref, input_ref, gain_ref, inverse_ref, *refs):
    part_refs, (out_ref, sum_ref) = refs[:-2], refs[-2:]
    rows, wide = out_ref.shape
    total = part_refs[0][...].astype(jnp.float32)
    for place, part_ref in enumerate(part_refs[1:]):
        total += part_ref[...].astype(jnp.float32) * flag_ref[place].astype(jnp.float32)
    total = total.T
    d_normed = total[:, :wide]
    centre = (total[:, wide : wide + 1]) * (1.0 / flag_ref[len(part_refs) - 1].astype(jnp.float32))
    inverse = inverse_ref[...]
    scaled = input_ref[...].astype(jnp.float32) * inverse
    gain = gain_ref[...].reshape(1, wide)
    out_ref[...] = (inverse * ((1.0 + gain) * d_normed - scaled * centre)).astype(jnp.bfloat16)
    sum_ref[...] = jnp.sum(d_normed * scaled, axis=0, keepdims=True)


def finish(flags, input_columns, gain_columns, inverse, parts):
    rows, wide = input_columns.shape
    return pl.pallas_call(
        finish_kernel,
        out_shape=(
            jax.ShapeDtypeStruct((rows, wide), jnp.bfloat16),
            jax.ShapeDtypeStruct((1, wide), jnp.float32),
        ),
        grid=(1,),
        in_specs=[
            pl.BlockSpec(memory_space=pltpu.SMEM),
            pl.BlockSpec((rows, wide), lambda i: (0, 0)),
            pl.BlockSpec((wide,), lambda i: (0,)),
            pl.BlockSpec((rows, 1), lambda i: (0, 0)),
        ]
        + [pl.BlockSpec(part.shape, lambda i: (0, 0)) for part in parts],
        out_specs=(
            pl.BlockSpec((rows, wide), lambda i: (0, 0)),
            pl.BlockSpec((1, wide), lambda i: (0, 0)),
        ),
        compiler_params=pltpu.CompilerParams(vmem_limit_bytes=40 * MIB),
        cost_estimate=cost(20 * rows * wide, 2 * rows * wide * (len(parts) + 2)),
        name="finish",
    )(flags, input_columns, gain_columns, inverse, *parts)


def branch_send(array, chips, shift, swap):
    pairs = [
        (c * 2 + k, ((c + shift) % chips) * 2 + (k ^ swap)) for c in range(chips) for k in range(2)
    ]
    return lax.ppermute(array, "branch", pairs)


def tensor_scatter(project, index, total):
    if total != 4:
        shifts = list(range(1, total)) + [0]
        parts = project(lax.rem(index + jnp.array(shifts, jnp.int32), total))
        arrived = [
            lax.ppermute(part, "tensor", [(t, (t + shift) % total) for t in range(total)])
            for shift, part in zip(shifts, parts[:-1])
        ]
        return parts[-1], arrived, jnp.ones((total - 1,), jnp.int32)
    order = jnp.array([[3, 2, 1, 0], [0, 2, 3, 1], [3, 1, 0, 2], [0, 1, 2, 3]], jnp.int32)[index]
    first, second = project(order[:2])
    third, own = project(order[2:])
    inner = (index == 1) | (index == 2)
    from_first = lax.ppermute(first, "tensor", [(0, 1), (1, 0), (2, 3), (3, 2)])
    from_inner = lax.ppermute(second, "tensor", [(1, 2), (2, 1)])
    from_ends = lax.ppermute(second, "tensor", [(0, 2), (3, 1)])
    kept = jnp.where(inner, from_first.astype(jnp.float32), 0.0)
    joined = (third.astype(jnp.float32) + kept).astype(jnp.bfloat16)
    from_joined = lax.ppermute(joined, "tensor", [(1, 3), (2, 0), (0, 1), (3, 2)])
    flags = jnp.stack([jnp.where(inner, 0, 1), 1, 1, 1]).astype(jnp.int32)
    return own, [from_first, from_inner, from_ends, from_joined], flags


def local(layer_input, norm_gain, w_query, w_key, w_value, head_grad, parents, row_counts):
    branch_total = lax.axis_size("branch")
    tensor_total = lax.axis_size("tensor")
    tensor_index = lax.axis_index("tensor")
    slots = row_counts.shape[0] // branch_total
    rows, width = layer_input.shape
    column_width = width // tensor_total
    chips = branch_total // 2
    group = w_query.shape[1] // w_key.shape[1]
    kv_local = w_key.shape[1] // HEAD_DIM
    offsets = [(shift, swap) for shift in range(chips) for swap in range(2)]

    def targets():
        index = lax.axis_index("branch")
        chip, core = index // 2, index % 2
        return [lax.rem(chip + s, chips) * 2 + lax.rem(core + e, 2) for s, e in offsets]

    normed, inverse, pieces = normalize(
        layer_input, norm_gain, targets, branch_total, rows // slots
    )
    turned = [
        piece if (s, e) == (0, 0) else branch_send(piece, chips, s, e)
        for piece, (s, e) in zip(pieces, offsets)
    ]
    deltas, delta_turned, centre = attention_backward(
        normed, w_query, w_key, w_value, head_grad, parents, row_counts, slots
    )

    def project(order):
        return back_project(
            order, delta_turned, centre, w_query, w_key, w_value, tensor_total
        )

    own, arrived, flags = tensor_scatter(project, tensor_index, tensor_total)

    weights = None
    for head, delta in enumerate(deltas):
        direct = [delta] + [branch_send(delta, chips, s, 0) for s in range(1, chips)]
        gathered = []
        for part in direct:
            gathered += [part, branch_send(part, chips, 0, 1)]
        weights = weight_gradients(turned, gathered, head, kv_local, group, weights)

    column_start = tensor_index * column_width
    input_columns = lax.dynamic_slice_in_dim(layer_input, column_start, column_width, 1)
    gain_columns = lax.dynamic_slice_in_dim(norm_gain, column_start, column_width, 0)
    flags = jnp.concatenate([flags, jnp.array([width], jnp.int32)])
    grad_input, gain_sum = finish(flags, input_columns, gain_columns, inverse, [own] + arrived)
    if chips == 2:
        here = gain_sum + branch_send(gain_sum, chips, 0, 1)
        there = branch_send(gain_sum, chips, 1, 0) + branch_send(gain_sum, chips, 1, 1)
        grad_gain = here + there
    else:
        grad_gain = lax.psum(gain_sum, "branch")
    return (grad_input, *weights, grad_gain.reshape(column_width))


def solution(mesh):
    placed = (
        P(("parts", "branch"), None),
        P(),
        P(None, "tensor"),
        P(None, "tensor"),
        P(None, "tensor"),
        P(("parts", "branch"), "tensor"),
        P(("parts", "branch")),
        P("parts"),
    )
    return jax.shard_map(
        local,
        mesh=mesh,
        in_specs=placed,
        out_specs=(
            P(("parts", "branch"), "tensor"),
            P(("parts", "branch"), "tensor"),
            P(("parts", "branch"), "tensor"),
            P(("parts", "branch"), "tensor"),
            P(("parts", "tensor")),
        ),
        check_vma=False,
    )
```

```python
import functools

import jax
import jax.numpy as jnp
from jax import lax
from jax.experimental import pallas as pl
from jax.experimental.pallas import tpu as pltpu
from jax.sharding import PartitionSpec as P

HEAD_DIM = 256
MIB = 1024 * 1024
CENTRE_ROWS = 16
VMEM_LIMIT = 64 * MIB


epsilon = 1e-06
softcap_limit = 50.0


def nn_dot(left, right):
    return lax.dot_general(
        left, right, (((1,), (0,)), ((), ())), preferred_element_type=jnp.float32
    )


def nt_dot(left, right):
    return lax.dot_general(
        left, right, (((1,), (1,)), ((), ())), preferred_element_type=jnp.float32
    )


def tn_dot(left, right):
    return lax.dot_general(
        left, right, (((0,), (0,)), ((), ())), preferred_element_type=jnp.float32
    )


def small_cost():
    return pl.CostEstimate(flops=1000000, bytes_accessed=100000, transcendentals=0)


def norm_kernel(targets, cut, input_ref, gain_ref, normed_ref, inverse_ref, *rest):
    input_cut_ref, gain_cut_ref = rest[:2]
    piece_refs, (turned, gain_row) = rest[2:-2], rest[-2:]
    rows, width = input_ref.shape
    values = input_ref[...].astype(jnp.float32)
    inverse = lax.rsqrt(jnp.mean(values * values, axis=-1, keepdims=True) + epsilon)
    inverse_ref[...] = inverse
    gain = gain_ref[...].reshape(1, width)
    normed = (values * inverse * (1.0 + gain)).astype(jnp.bfloat16)
    normed_ref[...] = normed
    turned[...] = normed.T
    depth = width // len(piece_refs)
    for target, piece_ref in zip(targets(), piece_refs):
        start = pl.multiple_of(target * depth, 16)
        piece_ref[...] = turned[pl.ds(start, depth), :]
    wide = input_cut_ref.shape[1]
    if cut:
        gain_row[...] = gain
        start = pl.multiple_of(lax.axis_index("tensor") * wide, 128)
        input_cut_ref[...] = input_ref[:, pl.ds(start, wide)]
        gain_cut_ref[...] = gain_row[:, pl.ds(start, wide)]
    else:
        input_cut_ref[...] = jnp.zeros_like(input_cut_ref)
        gain_cut_ref[...] = jnp.zeros_like(gain_cut_ref)


def normalize(layer_input, norm_gain, targets, pieces, block, column_width):
    rows, width = layer_input.shape
    depth = width // pieces
    cut = column_width % 128 == 0
    wide = column_width if cut else 128
    out = pl.pallas_call(
        functools.partial(norm_kernel, targets, cut),
        out_shape=(
            jax.ShapeDtypeStruct((rows, width), jnp.bfloat16),
            jax.ShapeDtypeStruct((rows, 1), jnp.float32),
            jax.ShapeDtypeStruct((rows, wide), jnp.bfloat16),
            jax.ShapeDtypeStruct((1, wide), jnp.float32),
        )
        + (jax.ShapeDtypeStruct((depth, rows), jnp.bfloat16),) * pieces,
        grid=(rows // block,),
        in_specs=[
            pl.BlockSpec((block, width), lambda i: (i, 0)),
            pl.BlockSpec((width,), lambda i: (0,)),
        ],
        out_specs=(
            pl.BlockSpec((block, width), lambda i: (i, 0)),
            pl.BlockSpec((block, 1), lambda i: (i, 0)),
            pl.BlockSpec((block, wide), lambda i: (i, 0)),
            pl.BlockSpec((1, wide), lambda i: (0, 0)),
        )
        + (pl.BlockSpec((depth, block), lambda i: (0, i)),) * pieces,
        scratch_shapes=[
            pltpu.VMEM((width, block), jnp.bfloat16),
            pltpu.VMEM((1, width), jnp.float32),
        ],
        compiler_params=pltpu.CompilerParams(vmem_limit_bytes=VMEM_LIMIT),
        cost_estimate=small_cost(),
        name="norm",
    )(layer_input, norm_gain)
    if cut:
        input_cut, gain_cut = out[2], out[3]
    else:
        start = lax.axis_index("tensor") * column_width
        input_cut = lax.dynamic_slice_in_dim(layer_input, start, column_width, 1)
        gain_cut = lax.dynamic_slice_in_dim(norm_gain, start, column_width, 0)
        gain_cut = gain_cut.reshape(1, column_width)
    return out[0], out[1], input_cut, gain_cut, out[4:]


def ancestor_mask(parent_row):
    rows = parent_row.shape[1]
    row = lax.broadcasted_iota(jnp.int32, (rows, rows), 0)
    column = lax.broadcasted_iota(jnp.int32, (rows, rows), 1)
    reached = jnp.where((parent_row == row) | (row == column), 1.0, 0.0)
    for squaring in range(rows.bit_length() - 1):
        halfway = reached.astype(jnp.bfloat16)
        reached = jnp.minimum(nn_dot(halfway, halfway), 1.0)
    return reached.T


def attention_kernel(
    slots,
    kv_local,
    group,
    packs,
    count_ref,
    parent_ref,
    normed_hbm,
    query_hbm,
    key_hbm,
    value_hbm,
    grad_hbm,
    *rest,
):
    piece_hbm, rest = rest[:packs], rest[packs:]
    pack_hbm, rest = rest[:packs], rest[packs:]
    delta_hbm, rest = rest[: kv_local - 1], rest[kv_local - 1 :]
    turned_hbm, centre_ref, normed_ref, weight_ref, grad_ref = rest[:5]
    sum_ref, delta_ref, turned_ref, load_sem, weight_sem, pack_sem, store_sem = rest[5:]
    head_dim = HEAD_DIM
    rows, width = normed_ref.shape
    block = rows // slots
    span = (group + 2) * head_dim
    mid = group * head_dim

    def fetch(h):
        places = ((query_hbm, 0, mid), (key_hbm, mid, head_dim), (value_hbm, mid + head_dim, head_dim))
        return [
            pltpu.make_async_copy(
                source.at[:, pl.ds(h * wide, wide)],
                weight_ref.at[h, :, pl.ds(start, wide)],
                weight_sem.at[h, which],
            )
            for which, (source, start, wide) in enumerate(places)
        ]

    loads = [
        pltpu.make_async_copy(normed_hbm, normed_ref, load_sem.at[0]),
        pltpu.make_async_copy(grad_hbm, grad_ref, load_sem.at[1]),
    ]
    fetches = [fetch(h) for h in range(kv_local)]
    loads[0].start()
    for copy in sum(fetches, []) + loads[1:]:
        copy.start()
    depth = piece_hbm[0].shape[0]
    stores = [
        pltpu.make_async_copy(piece, pack.at[pl.ds(0, depth), :], pack_sem.at[place])
        for place, (piece, pack) in enumerate(zip(piece_hbm, pack_hbm))
    ]
    for store in stores:
        store.start()

    first_count = lax.axis_index("branch") * slots
    parents = parent_ref[...].reshape(1, rows)
    allowed_slots = [
        ancestor_mask(parents[:, slot * block : (slot + 1) * block]) for slot in range(slots)
    ]
    loads[0].wait()
    for h in range(kv_local):
        for copy in fetches[h]:
            copy.wait()
        sum_ref[h] = nn_dot(normed_ref[...], weight_ref[h])
    loads[1].wait()

    scale = head_dim ** (-0.5)
    pairs = [(h, slot) for h in range(kv_local) for slot in range(slots)]
    queries, keys, values, grads = {}, {}, {}, {}
    for h, slot in pairs:
        lines = slice(slot * block, (slot + 1) * block)
        base = h * mid
        live = (
            lax.broadcasted_iota(jnp.int32, (block, head_dim), 0) < count_ref[first_count + slot]
        )
        queries[h, slot] = jnp.concatenate(
            [sum_ref[h, lines, g * head_dim : (g + 1) * head_dim] for g in range(group)], axis=0
        ).astype(jnp.bfloat16)
        keys[h, slot] = sum_ref[h, lines, mid : mid + head_dim].astype(jnp.bfloat16)
        values[h, slot] = sum_ref[h, lines, mid + head_dim :].astype(jnp.bfloat16)
        grads[h, slot] = jnp.concatenate(
            [
                jnp.where(
                    live,
                    grad_ref[lines, base + g * head_dim : base + (g + 1) * head_dim].astype(
                        jnp.float32
                    ),
                    0.0,
                )
                for g in range(group)
            ],
            axis=0,
        ).astype(jnp.bfloat16)
    scores = jnp.concatenate([nt_dot(queries[p], keys[p]) for p in pairs], axis=0)
    d_probs = jnp.concatenate([nt_dot(grads[p], values[p]) for p in pairs], axis=0)
    allowed = jnp.concatenate([allowed_slots[slot] for h, slot in pairs for g in range(group)], axis=0)
    bounded = jnp.tanh(scores * (scale / softcap_limit))
    weights = allowed * jnp.exp(softcap_limit * bounded)
    probabilities = weights * (1.0 / jnp.sum(weights, axis=-1, keepdims=True))
    d_scores = probabilities * (
        d_probs - jnp.sum(probabilities * d_probs, axis=-1, keepdims=True)
    )
    d_raw_all = (d_scores * (1.0 - bounded * bounded) * scale).astype(jnp.bfloat16)
    prob_half_all = probabilities.astype(jnp.bfloat16)
    centre_parts = [jnp.zeros((block, 1), jnp.float32) for _ in range(slots)]
    for place, (h, slot) in enumerate(pairs):
        lines = slice(slot * block, (slot + 1) * block)
        taken = slice(place * group * block, (place + 1) * group * block)
        d_raw, prob_half = d_raw_all[taken], prob_half_all[taken]
        d_query = nn_dot(d_raw, keys[h, slot]).astype(jnp.bfloat16)
        d_key = tn_dot(d_raw, queries[h, slot]).astype(jnp.bfloat16)
        d_value = tn_dot(prob_half, grads[h, slot]).astype(jnp.bfloat16)
        parts = [d_query[g * block : (g + 1) * block] for g in range(group)] + [d_key, d_value]
        product = None
        for which, part in enumerate(parts):
            columns = slice(which * head_dim, (which + 1) * head_dim)
            delta_ref[h, which * rows + slot * block : which * rows + (slot + 1) * block] = part
            turned_ref[h, columns, lines] = part.T
            term = part.astype(jnp.float32) * sum_ref[h, lines, columns]
            product = term if product is None else product + term
        centre_parts[slot] += jnp.sum(product, axis=-1, keepdims=True)
    lasts = []
    for h in range(kv_local):
        lasts.append(
            pltpu.make_async_copy(
                turned_ref.at[h], turned_hbm.at[pl.ds(h * span, span), :], store_sem.at[h]
            )
        )
    lasts += [
        pltpu.make_async_copy(
            delta_ref.at[0],
            pack.at[pl.ds(depth, (group + 2) * rows), :],
            store_sem.at[kv_local + place],
        )
        for place, pack in enumerate(pack_hbm)
    ]
    lasts += [
        pltpu.make_async_copy(delta_ref.at[h + 1], out, store_sem.at[kv_local + packs + h])
        for h, out in enumerate(delta_hbm)
    ]
    for store in lasts:
        store.start()
    centre = jnp.concatenate(centre_parts, axis=0)
    centre_ref[...] = jnp.broadcast_to(centre, (rows, 128)).T[:CENTRE_ROWS]
    for store in stores + lasts:
        store.wait()


def attention_backward(
    normed, w_query, w_key, w_value, head_grad, parents, counts, pieces, slots
):
    rows, width = normed.shape
    kv_local = w_key.shape[1] // HEAD_DIM
    group = w_query.shape[1] // w_key.shape[1]
    span = (group + 2) * HEAD_DIM
    stack = (group + 2) * rows
    packs = len(pieces)
    depth = pieces[0].shape[0]
    hbm = pl.BlockSpec(memory_space=pl.ANY)
    vmem = pl.BlockSpec(memory_space=pltpu.VMEM)
    out = pl.pallas_call(
        functools.partial(attention_kernel, slots, kv_local, group, packs),
        out_shape=(jax.ShapeDtypeStruct((depth + stack, HEAD_DIM), jnp.bfloat16),) * packs
        + (jax.ShapeDtypeStruct((stack, HEAD_DIM), jnp.bfloat16),) * (kv_local - 1)
        + (
            jax.ShapeDtypeStruct((kv_local * span, rows), jnp.bfloat16),
            jax.ShapeDtypeStruct((CENTRE_ROWS, rows), jnp.float32),
        ),
        in_specs=[pl.BlockSpec(memory_space=pltpu.SMEM), vmem] + [hbm] * (5 + packs),
        out_specs=(hbm,) * (packs + kv_local) + (vmem,),
        scratch_shapes=[
            pltpu.VMEM((rows, width), jnp.bfloat16),
            pltpu.VMEM((kv_local, width, span), jnp.bfloat16),
            pltpu.VMEM(head_grad.shape, jnp.bfloat16),
            pltpu.VMEM((kv_local, rows, span), jnp.float32),
            pltpu.VMEM((kv_local, stack, HEAD_DIM), jnp.bfloat16),
            pltpu.VMEM((kv_local, span, rows), jnp.bfloat16),
            pltpu.SemaphoreType.DMA((2,)),
            pltpu.SemaphoreType.DMA((kv_local, 3)),
            pltpu.SemaphoreType.DMA((packs,)),
            pltpu.SemaphoreType.DMA((packs + 2 * kv_local - 1,)),
        ],
        compiler_params=pltpu.CompilerParams(vmem_limit_bytes=VMEM_LIMIT),
        cost_estimate=small_cost(),
        name="attention",
    )(counts, parents, normed, w_query, w_key, w_value, head_grad, *pieces)
    return out[:packs], out[packs:-2], out[-2], out[-1]


def back_kernel(order, cuts, blocks, *refs):
    turned_ref, centre_ref, query_hbm, key_hbm, value_hbm = refs[:5]
    rest = refs[5:]
    pieces = len(rest) - 4
    out_hbm = rest[:pieces]
    weight_ref, kept, load_sem, store_sem = rest[pieces:]
    head_dim = HEAD_DIM
    kv_local = key_hbm.shape[1] // head_dim
    group = query_hbm.shape[1] // key_hbm.shape[1]
    span = (group + 2) * head_dim
    mid = group * head_dim
    depth = query_hbm.shape[0] // blocks
    lines = depth // cuts
    steps = [(piece, cut) for piece in range(pieces) for cut in range(cuts)]
    picked = order()

    def fetch(step):
        piece, cut = steps[step]
        start = pl.multiple_of(picked[piece] * depth + cut * lines, 16)
        copies = []
        for h in range(kv_local):
            base = h * span
            for source, place, wide in (
                (query_hbm, base, mid),
                (key_hbm, base + mid, head_dim),
                (value_hbm, base + mid + head_dim, head_dim),
            ):
                copies.append(
                    pltpu.make_async_copy(
                        source.at[pl.ds(start, lines), pl.ds(h * wide, wide)],
                        weight_ref.at[step, :, pl.ds(place, wide)],
                        load_sem.at[step, len(copies)],
                    )
                )
        return copies

    fetches = [fetch(step) for step in range(len(steps))]
    for copy in sum(fetches, []):
        copy.start()
    stores = []
    for step, (piece, cut) in enumerate(steps):
        for copy in fetches[step]:
            copy.wait()
        total = nn_dot(weight_ref[step], turned_ref[...])
        kept[piece, cut * lines : (cut + 1) * lines, :] = total.astype(jnp.bfloat16)
        if cut == cuts - 1:
            kept[piece, depth:, :] = centre_ref[...].astype(jnp.bfloat16)
            stores.append(pltpu.make_async_copy(kept.at[piece], out_hbm[piece], store_sem.at[piece]))
            stores[-1].start()
    for store in stores:
        store.wait()


def back_project(order, pieces, turned, centre, w_query, w_key, w_value, blocks):
    total, rows = turned.shape
    depth = w_query.shape[0] // blocks
    cuts = 2
    kv_local = w_key.shape[1] // HEAD_DIM
    hbm = pl.BlockSpec(memory_space=pl.ANY)
    vmem = pl.BlockSpec(memory_space=pltpu.VMEM)
    return pl.pallas_call(
        functools.partial(back_kernel, order, cuts, blocks),
        out_shape=(jax.ShapeDtypeStruct((depth + CENTRE_ROWS, rows), jnp.bfloat16),) * pieces,
        in_specs=[vmem, vmem] + [hbm] * 3,
        out_specs=(hbm,) * pieces,
        scratch_shapes=[
            pltpu.VMEM((pieces * cuts, depth // cuts, total), jnp.bfloat16),
            pltpu.VMEM((pieces, depth + CENTRE_ROWS, rows), jnp.bfloat16),
            pltpu.SemaphoreType.DMA((pieces * cuts, 3 * kv_local)),
            pltpu.SemaphoreType.DMA((pieces,)),
        ],
        compiler_params=pltpu.CompilerParams(vmem_limit_bytes=VMEM_LIMIT),
        cost_estimate=small_cost(),
        name="back",
    )(turned, centre, w_query, w_key, w_value)


def weight_kernel(group, head, sources, skips, cuts, *refs):
    turned_hbm, delta_hbm = refs[:sources], refs[sources : 2 * sources]
    query_hbm, key_hbm, value_hbm, token_ref = refs[-10:-6]
    turned_ref, delta_ref, kept, turned_sem, delta_sem, store_sem = refs[-6:]
    token_ref[...] = jnp.zeros_like(token_ref)
    depth = turned_ref.shape[0]
    rows = turned_ref.shape[1] // sources
    cut = depth // cuts
    mid = group * HEAD_DIM
    loads = []
    for place in range(sources):
        spot = pl.ds(place * rows, rows)
        for block in range(group + 2):
            loads.append(
                pltpu.make_async_copy(
                    delta_hbm[place].at[pl.ds(skips[place] + block * rows, rows), :],
                    delta_ref.at[spot, pl.ds(block * HEAD_DIM, HEAD_DIM)],
                    delta_sem.at[place, block],
                )
            )
        loads.append(
            pltpu.make_async_copy(
                turned_hbm[place].at[pl.ds(0, depth), :],
                turned_ref.at[:, spot],
                turned_sem.at[place],
            )
        )
    for load in loads:
        load.start()
    for load in loads:
        load.wait()
    stores = []
    for step in range(cuts):
        lines = pl.ds(step * cut, cut)
        kept[lines, :] = nn_dot(turned_ref[lines, :], delta_ref[...])
        for which, (out_hbm, start, wide) in enumerate(
            (
                (query_hbm, 0, mid),
                (key_hbm, mid, HEAD_DIM),
                (value_hbm, mid + HEAD_DIM, HEAD_DIM),
            )
        ):
            stores.append(
                pltpu.make_async_copy(
                    kept.at[lines, pl.ds(start, wide)],
                    out_hbm.at[lines, pl.ds(head * wide, wide)],
                    store_sem.at[step, which],
                )
            )
            stores[-1].start()
    for store in stores:
        store.wait()


def weight_gradients(depth, rows, turned, deltas, skips, head, kv_local, group, before):
    span = (group + 2) * HEAD_DIM
    cuts = 4 if depth % 64 == 0 else 2
    sources = len(turned)
    kept = list(before) if before is not None else []
    hbm = pl.BlockSpec(memory_space=pl.ANY)
    return pl.pallas_call(
        functools.partial(weight_kernel, group, head, sources, skips, cuts),
        out_shape=(
            jax.ShapeDtypeStruct((depth, kv_local * group * HEAD_DIM), jnp.float32),
            jax.ShapeDtypeStruct((depth, kv_local * HEAD_DIM), jnp.float32),
            jax.ShapeDtypeStruct((depth, kv_local * HEAD_DIM), jnp.float32),
            jax.ShapeDtypeStruct((8, 128), jnp.float32),
        ),
        in_specs=[hbm] * (2 * sources + len(kept)),
        out_specs=(hbm,) * 3 + (pl.BlockSpec(memory_space=pltpu.VMEM),),
        input_output_aliases={2 * sources + i: i for i in range(len(kept))},
        scratch_shapes=[
            pltpu.VMEM((depth, sources * rows), jnp.bfloat16),
            pltpu.VMEM((sources * rows, span), jnp.bfloat16),
            pltpu.VMEM((depth, span), jnp.float32),
            pltpu.SemaphoreType.DMA((sources,)),
            pltpu.SemaphoreType.DMA((sources, group + 2)),
            pltpu.SemaphoreType.DMA((cuts, 3)),
        ],
        compiler_params=pltpu.CompilerParams(vmem_limit_bytes=VMEM_LIMIT),
        cost_estimate=small_cost(),
        name="weights",
    )(*turned, *deltas, *kept)


def gate_kernel(*refs):
    del refs


def gate(arrays, tokens):
    hbm = pl.BlockSpec(memory_space=pl.ANY)
    return pl.pallas_call(
        gate_kernel,
        out_shape=tuple(jax.ShapeDtypeStruct(x.shape, x.dtype) for x in arrays),
        in_specs=[hbm] * (len(arrays) + len(tokens)),
        out_specs=(hbm,) * len(arrays),
        input_output_aliases={i: i for i in range(len(arrays))},
        compiler_params=pltpu.CompilerParams(vmem_limit_bytes=VMEM_LIMIT),
        cost_estimate=small_cost(),
        name="gate",
    )(*arrays, *tokens)


def join_kernel(inner_ref, other_ref, end_ref, out_ref, token_ref):
    token_ref[...] = jnp.zeros_like(token_ref)
    index = lax.axis_index("tensor")
    inner = (index > 0) & (index < lax.axis_size("tensor") - 1)

    @pl.when(inner)
    def _():
        out_ref[...] = (
            inner_ref[...].astype(jnp.float32) + other_ref[...].astype(jnp.float32)
        ).astype(jnp.bfloat16)

    @pl.when(jnp.logical_not(inner))
    def _():
        out_ref[...] = end_ref[...]


def join(inner_part, other, end_part):
    vmem = pl.BlockSpec(memory_space=pltpu.VMEM)
    return pl.pallas_call(
        join_kernel,
        out_shape=(
            jax.ShapeDtypeStruct(end_part.shape, end_part.dtype),
            jax.ShapeDtypeStruct((8, 128), jnp.float32),
        ),
        in_specs=[vmem] * 3,
        out_specs=(vmem, vmem),
        compiler_params=pltpu.CompilerParams(vmem_limit_bytes=VMEM_LIMIT),
        cost_estimate=small_cost(),
        name="join",
    )(inner_part, other, end_part)


def finish_kernel(width, for_ends, for_inner, input_ref, gain_ref, inverse_ref, *refs):
    part_refs, (out_ref, sum_ref) = refs[:-3], refs[-2:]
    rows, wide = out_ref.shape
    index = lax.axis_index("tensor")
    ends = ((index == 0) | (index == lax.axis_size("tensor") - 1)).astype(jnp.float32)
    total = None
    for place, part_ref in enumerate(part_refs):
        part = part_ref[...].astype(jnp.float32)
        if place < for_ends:
            part = part * ends
        elif place < for_ends + for_inner:
            part = part * (1.0 - ends)
        total = part if total is None else total + part
    total = total.T
    d_normed = total[:, :wide]
    centre = total[:, wide : wide + 1] * (1.0 / width)
    inverse = inverse_ref[...]
    scaled = input_ref[...].astype(jnp.float32) * inverse
    out_ref[...] = (
        inverse * ((1.0 + gain_ref[...]) * d_normed - scaled * centre)
    ).astype(jnp.bfloat16)
    sum_ref[...] = jnp.sum(d_normed * scaled, axis=0, keepdims=True)


def finish(width, for_ends, for_inner, input_columns, gain_columns, inverse, parts, token):
    rows, wide = input_columns.shape
    whole = lambda array: pl.BlockSpec(array.shape, lambda i: (0, 0))
    return pl.pallas_call(
        functools.partial(finish_kernel, width, for_ends, for_inner),
        out_shape=(
            jax.ShapeDtypeStruct((rows, wide), jnp.bfloat16),
            jax.ShapeDtypeStruct((1, wide), jnp.float32),
        ),
        grid=(1,),
        in_specs=[whole(x) for x in (input_columns, gain_columns, inverse, *parts)]
        + [pl.BlockSpec(memory_space=pl.ANY)],
        out_specs=(
            pl.BlockSpec((rows, wide), lambda i: (0, 0)),
            pl.BlockSpec((1, wide), lambda i: (0, 0)),
        ),
        compiler_params=pltpu.CompilerParams(vmem_limit_bytes=VMEM_LIMIT),
        cost_estimate=small_cost(),
        name="finish",
    )(input_columns, gain_columns, inverse, *parts, token)


def branch_send(array, chips, shift, swap):
    pairs = [
        (c * 2 + k, ((c + shift) % chips) * 2 + (k ^ swap)) for c in range(chips) for k in range(2)
    ]
    return lax.ppermute(array, "branch", pairs)


def pick(table, index):
    chosen = table[-1]
    for place in range(len(table) - 2, -1, -1):
        chosen = jnp.where(index == place, table[place], chosen)
    return chosen


def tensor_scatter(project, total):
    index = lambda: lax.axis_index("tensor")
    if total != 4:
        shifts = list(range(1, total)) + [0]
        parts = project(lambda: [lax.rem(index() + shift, total) for shift in shifts], total)
        arrived = [
            lax.ppermute(part, "tensor", [(t, (t + shift) % total) for t in range(total)])
            for shift, part in zip(shifts, parts[:-1])
        ]
        return [parts[-1]] + arrived, 0, 0, (parts[0],), (arrived[-1],)
    table = [[3, 0, 3, 0], [0, 2, 1, 3], [2, 3, 0, 1], [1, 1, 2, 2]]
    order = lambda rows: lambda: [pick(table[row], index()) for row in rows]
    first, second = project(order((0, 1)), 2)
    from_first = lax.ppermute(first, "tensor", [(0, 1), (1, 0), (2, 3), (3, 2)])
    from_inner = lax.ppermute(second, "tensor", [(1, 2), (2, 1)])
    third, fourth = project(order((2, 3)), 2)
    from_ends = lax.ppermute(third, "tensor", [(0, 2), (3, 1)])
    joined, token = join(third, from_first, fourth)
    from_joined = lax.ppermute(joined, "tensor", [(1, 3), (2, 0), (0, 1), (3, 2)])
    parts = [from_first, second, fourth, from_inner, from_ends, from_joined]
    return parts, 2, 1, (token, from_inner, from_ends), (from_joined,)


def local(layer_input, norm_gain, w_query, w_key, w_value, head_grad, parents, row_counts):
    branch_total = lax.axis_size("branch")
    tensor_total = lax.axis_size("tensor")
    slots = row_counts.shape[0] // branch_total
    rows, width = layer_input.shape
    column_width = width // tensor_total
    chips = branch_total // 2
    group = w_query.shape[1] // w_key.shape[1]
    kv_local = w_key.shape[1] // HEAD_DIM
    offsets = [(shift, swap) for shift in range(chips) for swap in range(2)]

    def targets():
        index = lax.axis_index("branch")
        chip, core = index // 2, index % 2
        return [lax.rem(chip + s, chips) * 2 + lax.rem(core + e, 2) for s, e in offsets]

    normed, inverse, input_columns, gain_columns, pieces = normalize(
        layer_input, norm_gain, targets, branch_total, rows // slots, column_width
    )
    direct = [branch_send(pieces[2 * s], chips, s, 0) for s in range(1, chips)]
    packs, deltas, delta_turned, centre = attention_backward(
        normed, w_query, w_key, w_value, head_grad, parents, row_counts, pieces[1::2], slots
    )

    held = gate(packs[1:], direct)

    def project(order, pieces):
        return back_project(
            order, pieces, delta_turned, centre, w_query, w_key, w_value, tensor_total
        )

    parts, for_ends, for_inner, met, arrived = tensor_scatter(project, tensor_total)

    depth = width // branch_total
    sent = [branch_send(pack, chips, s + 1, 0) for s, pack in enumerate(held)]
    *sent, first_pack = gate((*sent, packs[0]), met)
    deltas = gate(deltas, (sent[0],)) if deltas else deltas
    sent = [first_pack] + sent
    handed = [branch_send(pack, chips, 0, 1) for pack in sent]
    turned = [pieces[0]] + direct + handed
    sources = len(turned)
    *weights, token = weight_gradients(
        depth, rows, turned, sent + handed, [depth] * sources, 0, kv_local, group, None
    )
    grad_input, gain_sum = finish(
        width, for_ends, for_inner, input_columns, gain_columns, inverse, parts, token
    )
    for head, delta in enumerate(deltas):
        sent = [delta] + [branch_send(delta, chips, s, 0) for s in range(1, chips)]
        sent = list(gate(sent, (*arrived, token)))
        handed = [branch_send(part, chips, 0, 1) for part in sent]
        *weights, token = weight_gradients(
            depth, rows, turned, sent + handed, [0] * sources, head + 1, kv_local, group, weights
        )
    if chips == 2:
        here = gain_sum + branch_send(gain_sum, chips, 0, 1)
        there = branch_send(gain_sum, chips, 1, 0) + branch_send(gain_sum, chips, 1, 1)
        grad_gain = here + there
    else:
        grad_gain = lax.psum(gain_sum, "branch")
    return (grad_input, *weights, grad_gain.reshape(column_width))


def solution(mesh):
    placed = (
        P(("parts", "branch"), None),
        P(),
        P(None, "tensor"),
        P(None, "tensor"),
        P(None, "tensor"),
        P(("parts", "branch"), "tensor"),
        P(("parts", "branch")),
        P("parts"),
    )
    return jax.shard_map(
        local,
        mesh=mesh,
        in_specs=placed,
        out_specs=(
            P(("parts", "branch"), "tensor"),
            P(("parts", "branch"), "tensor"),
            P(("parts", "branch"), "tensor"),
            P(("parts", "branch"), "tensor"),
            P(("parts", "tensor")),
        ),
        check_vma=False,
    )
```

```python
import functools

import jax
import jax.numpy as jnp
from jax import lax
from jax.experimental import pallas as pl
from jax.experimental.pallas import tpu as pltpu
from jax.sharding import PartitionSpec as P

HEAD_DIM = 256
MIB = 1024 * 1024
CENTRE_ROWS = 16
VMEM_LIMIT = 64 * MIB


epsilon = 1e-06
softcap_limit = 50.0


def nn_dot(left, right):
    return lax.dot_general(
        left, right, (((1,), (0,)), ((), ())), preferred_element_type=jnp.float32
    )


def nt_dot(left, right):
    return lax.dot_general(
        left, right, (((1,), (1,)), ((), ())), preferred_element_type=jnp.float32
    )


def tn_dot(left, right):
    return lax.dot_general(
        left, right, (((0,), (0,)), ((), ())), preferred_element_type=jnp.float32
    )


def small_cost():
    return pl.CostEstimate(flops=1000000, bytes_accessed=100000, transcendentals=0)


def cut_kernel(targets, input_hbm, *rest):
    piece_hbm, sem = rest[:-1], rest[-1]
    depth = piece_hbm[0].shape[1]
    copies = [
        pltpu.make_async_copy(
            input_hbm.at[:, pl.ds(pl.multiple_of(target * depth, 128), depth)],
            piece,
            sem.at[place],
        )
        for place, (target, piece) in enumerate(zip(targets(), piece_hbm))
    ]
    for copy in copies:
        copy.start()
    for copy in copies:
        copy.wait()


def cut_columns(layer_input, targets, pieces):
    rows, width = layer_input.shape
    depth = width // pieces
    if depth % 128:
        return [
            lax.dynamic_slice_in_dim(layer_input, target * depth, depth, 1) for target in targets()
        ]
    hbm = pl.BlockSpec(memory_space=pl.ANY)
    return pl.pallas_call(
        functools.partial(cut_kernel, targets),
        out_shape=(jax.ShapeDtypeStruct((rows, depth), jnp.bfloat16),) * pieces,
        in_specs=[hbm],
        out_specs=(hbm,) * pieces,
        scratch_shapes=[pltpu.SemaphoreType.DMA((pieces,))],
        compiler_params=pltpu.CompilerParams(vmem_limit_bytes=VMEM_LIMIT),
        cost_estimate=small_cost(),
        name="cut",
    )(layer_input)


def turn_kernel(gain_ref, *refs):
    pieces = len(refs) // 2
    gain = 1.0 + gain_ref[...]
    for piece_ref, out_ref in zip(refs[:pieces], refs[pieces:]):
        out_ref[...] = (piece_ref[...].astype(jnp.float32) * gain).astype(jnp.bfloat16).T


def turn(pieces, gain):
    rows, depth = pieces[0].shape
    return pl.pallas_call(
        turn_kernel,
        out_shape=(jax.ShapeDtypeStruct((depth, rows), jnp.bfloat16),) * len(pieces),
        grid=(1,),
        in_specs=[pl.BlockSpec((1, depth), lambda i: (0, 0))]
        + [pl.BlockSpec((rows, depth), lambda i: (0, 0))] * len(pieces),
        out_specs=(pl.BlockSpec((depth, rows), lambda i: (0, 0)),) * len(pieces),
        compiler_params=pltpu.CompilerParams(vmem_limit_bytes=VMEM_LIMIT),
        cost_estimate=small_cost(),
        name="turn",
    )(gain, *pieces)


def ancestor_mask(parent_row):
    rows = parent_row.shape[1]
    row = lax.broadcasted_iota(jnp.int32, (rows, rows), 0)
    column = lax.broadcasted_iota(jnp.int32, (rows, rows), 1)
    reached = jnp.where((parent_row == row) | (row == column), 1.0, 0.0)
    for squaring in range(rows.bit_length() - 1):
        halfway = reached.astype(jnp.bfloat16)
        reached = jnp.minimum(nn_dot(halfway, halfway), 1.0)
    return reached.T


def attention_kernel(
    slots,
    count_ref,
    parent_ref,
    gain_ref,
    input_ref,
    query_ref,
    key_ref,
    value_ref,
    grad_ref,
    delta_ref,
    centre_ref,
    inverse_ref,
    *rest,
):
    scaled_refs, (normed_ref, allowed_ref) = rest[:-2], rest[-2:]
    head_dim = HEAD_DIM
    rows, width = input_ref.shape
    block = rows // slots
    group = query_ref.shape[1] // head_dim
    step = pl.program_id(0)

    @pl.when(step == 0)
    def _():
        values = input_ref[...].astype(jnp.float32)
        inverse = lax.rsqrt(jnp.mean(values * values, axis=-1, keepdims=True) + epsilon)
        inverse_ref[...] = inverse
        gain = gain_ref[...].reshape(1, width)
        normed_ref[...] = (values * inverse * (1.0 + gain)).astype(jnp.bfloat16)
        centre_ref[...] = jnp.zeros_like(centre_ref)
        parents = parent_ref[...].reshape(1, rows)
        for slot in range(slots):
            allowed_ref[slot] = ancestor_mask(parents[:, slot * block : (slot + 1) * block])

    first_count = lax.axis_index("branch") * slots
    normed = normed_ref[...]
    query_sum = nn_dot(normed, query_ref[...])
    key_sum = nn_dot(normed, key_ref[...])
    value_sum = nn_dot(normed, value_ref[...])
    scale = head_dim ** (-0.5)
    for slot in range(slots):
        lines = slice(slot * block, (slot + 1) * block)
        query_parts = [
            query_sum[lines, g * head_dim : (g + 1) * head_dim] for g in range(group)
        ]
        queries = jnp.concatenate(query_parts, axis=0).astype(jnp.bfloat16)
        keys = key_sum[lines].astype(jnp.bfloat16)
        values = value_sum[lines].astype(jnp.bfloat16)
        live = (
            lax.broadcasted_iota(jnp.int32, (block, head_dim), 0) < count_ref[first_count + slot]
        )
        grads = jnp.concatenate(
            [
                jnp.where(
                    live,
                    grad_ref[lines, g * head_dim : (g + 1) * head_dim].astype(jnp.float32),
                    0.0,
                )
                for g in range(group)
            ],
            axis=0,
        ).astype(jnp.bfloat16)
        allowed = jnp.concatenate([allowed_ref[slot]] * group, axis=0)
        bounded = jnp.tanh(nt_dot(queries, keys) * (scale / softcap_limit))
        weights = allowed * jnp.exp(softcap_limit * bounded)
        probabilities = weights * (1.0 / jnp.sum(weights, axis=-1, keepdims=True))
        d_probs = nt_dot(grads, values)
        d_scores = probabilities * (
            d_probs - jnp.sum(probabilities * d_probs, axis=-1, keepdims=True)
        )
        d_raw = (d_scores * (1.0 - bounded * bounded) * scale).astype(jnp.bfloat16)
        prob_half = probabilities.astype(jnp.bfloat16)
        d_query = nn_dot(d_raw, keys)
        parts = [d_query[g * block : (g + 1) * block] for g in range(group)]
        parts += [tn_dot(d_raw, queries), tn_dot(prob_half, grads)]
        whole = query_parts + [key_sum[lines], value_sum[lines]]
        inverse = inverse_ref[lines, :]
        product = None
        for which, (part, sums) in enumerate(zip(parts, whole)):
            columns = slice(which * head_dim, (which + 1) * head_dim)
            half = part.astype(jnp.bfloat16)
            delta_ref[lines, columns] = half
            term = half.astype(jnp.float32) * sums
            product = term if product is None else product + term
            scaled = (part * inverse).astype(jnp.bfloat16)
            for place, scaled_ref in enumerate(scaled_refs):

                @pl.when(step == place)
                def _():
                    scaled_ref[lines, columns] = scaled

        centre_ref[lines, :] += jnp.sum(product, axis=-1, keepdims=True)


def attention_backward(
    layer_input, norm_gain, w_query, w_key, w_value, head_grad, parents, counts, slots
):
    rows, width = layer_input.shape
    kv_local = w_key.shape[1] // HEAD_DIM
    group = w_query.shape[1] // w_key.shape[1]
    span = (group + 2) * HEAD_DIM
    block = rows // slots
    whole = lambda h: (0, 0)
    by_head = lambda h: (0, h)
    out = pl.pallas_call(
        functools.partial(attention_kernel, slots),
        out_shape=(
            jax.ShapeDtypeStruct((rows, kv_local * span), jnp.bfloat16),
            jax.ShapeDtypeStruct((rows, 1), jnp.float32),
            jax.ShapeDtypeStruct((rows, 1), jnp.float32),
        )
        + (jax.ShapeDtypeStruct((rows, span), jnp.bfloat16),) * kv_local,
        grid=(kv_local,),
        in_specs=[
            pl.BlockSpec(memory_space=pltpu.SMEM),
            pl.BlockSpec((rows,), lambda h: (0,)),
            pl.BlockSpec((width,), lambda h: (0,)),
            pl.BlockSpec((rows, width), whole),
            pl.BlockSpec((width, group * HEAD_DIM), by_head),
            pl.BlockSpec((width, HEAD_DIM), by_head),
            pl.BlockSpec((width, HEAD_DIM), by_head),
            pl.BlockSpec((rows, group * HEAD_DIM), by_head),
        ],
        out_specs=(
            pl.BlockSpec((rows, span), by_head),
            pl.BlockSpec((rows, 1), whole),
            pl.BlockSpec((rows, 1), whole),
        )
        + (pl.BlockSpec((rows, span), whole),) * kv_local,
        scratch_shapes=[
            pltpu.VMEM((rows, width), jnp.bfloat16),
            pltpu.VMEM((slots, block, block), jnp.float32),
        ],
        compiler_params=pltpu.CompilerParams(vmem_limit_bytes=VMEM_LIMIT),
        cost_estimate=small_cost(),
        name="attention",
    )(counts, parents, norm_gain, layer_input, w_query, w_key, w_value, head_grad)
    return out[0], out[1], out[2], out[3:]


def back_kernel(delta_ref, centre_ref, query_ref, key_ref, value_ref, *out_refs):
    step = pl.program_id(0)
    head_dim = HEAD_DIM
    kv_local = key_ref.shape[1] // head_dim
    group = query_ref.shape[1] // key_ref.shape[1]
    span = (group + 2) * head_dim
    rows = delta_ref.shape[0]
    total = None
    for h in range(kv_local):
        base = h * span
        mid = base + group * head_dim
        term = nt_dot(
            delta_ref[:, base:mid],
            query_ref[:, h * group * head_dim : (h + 1) * group * head_dim],
        )
        term += nt_dot(
            delta_ref[:, mid : mid + head_dim], key_ref[:, h * head_dim : (h + 1) * head_dim]
        )
        term += nt_dot(
            delta_ref[:, mid + head_dim : mid + 2 * head_dim],
            value_ref[:, h * head_dim : (h + 1) * head_dim],
        )
        total = term if total is None else total + term
    total = total.astype(jnp.bfloat16)
    centre = jnp.broadcast_to(centre_ref[...], (rows, 128)).T[:CENTRE_ROWS].astype(jnp.bfloat16)
    for place, out_ref in enumerate(out_refs):

        @pl.when(step == place)
        def _():
            out_ref[:rows, :] = total
            out_ref[rows:, :] = jnp.zeros((CENTRE_ROWS, out_ref.shape[1]), jnp.bfloat16)
            out_ref[rows:, :rows] = centre


def back_project(order, pieces, delta, centre, w_query, w_key, w_value, blocks):
    rows = delta.shape[0]
    depth = w_query.shape[0] // blocks
    picked = lambda i: (order(i), 0)
    whole = lambda i: (0, 0)
    return pl.pallas_call(
        back_kernel,
        out_shape=(jax.ShapeDtypeStruct((rows + CENTRE_ROWS, depth), jnp.bfloat16),) * pieces,
        grid=(pieces,),
        in_specs=[
            pl.BlockSpec(delta.shape, whole),
            pl.BlockSpec(centre.shape, whole),
            pl.BlockSpec((depth, w_query.shape[1]), picked),
            pl.BlockSpec((depth, w_key.shape[1]), picked),
            pl.BlockSpec((depth, w_value.shape[1]), picked),
        ],
        out_specs=(pl.BlockSpec((rows + CENTRE_ROWS, depth), whole),) * pieces,
        compiler_params=pltpu.CompilerParams(vmem_limit_bytes=VMEM_LIMIT),
        cost_estimate=small_cost(),
        name="back",
    )(delta, centre, w_query, w_key, w_value)


def weight_kernel(group, sources, *refs):
    turned_refs, delta_refs = refs[:sources], refs[sources : 2 * sources]
    query_ref, key_ref, value_ref, token_ref = refs[-4:]
    token_ref[...] = jnp.zeros_like(token_ref)
    total = None
    for turned_ref, delta_ref in zip(turned_refs, delta_refs):
        term = nn_dot(turned_ref[...], delta_ref[...])
        total = term if total is None else total + term
    mid = group * HEAD_DIM
    query_ref[...] = total[:, :mid]
    key_ref[...] = total[:, mid : mid + HEAD_DIM]
    value_ref[...] = total[:, mid + HEAD_DIM :]


def weight_gradients(turned, deltas, head, kv_local, group, before):
    depth, rows = turned[0].shape
    span = (group + 2) * HEAD_DIM
    cuts = 4 if depth % 64 == 0 else 2
    cut = depth // cuts
    sources = len(turned)
    out_block = lambda i: (i, head)
    kept = list(before) if before is not None else []
    estimate = small_cost()
    if kept:
        estimate = pl.CostEstimate(
            flops=2 * sources * rows * depth * span,
            bytes_accessed=4 * depth * span + 2 * sources * rows * (depth + span),
            transcendentals=0,
        )
    return pl.pallas_call(
        functools.partial(weight_kernel, group, sources),
        out_shape=(
            jax.ShapeDtypeStruct((depth, kv_local * group * HEAD_DIM), jnp.float32),
            jax.ShapeDtypeStruct((depth, kv_local * HEAD_DIM), jnp.float32),
            jax.ShapeDtypeStruct((depth, kv_local * HEAD_DIM), jnp.float32),
            jax.ShapeDtypeStruct((8, 128), jnp.float32),
        ),
        grid=(cuts,),
        in_specs=[pl.BlockSpec((cut, rows), lambda i: (i, 0))] * sources
        + [pl.BlockSpec((rows, span), lambda i: (0, 0))] * sources
        + [pl.BlockSpec(memory_space=pl.ANY)] * len(kept),
        out_specs=(
            pl.BlockSpec((cut, group * HEAD_DIM), out_block),
            pl.BlockSpec((cut, HEAD_DIM), out_block),
            pl.BlockSpec((cut, HEAD_DIM), out_block),
            pl.BlockSpec((8, 128), lambda i: (0, 0)),
        ),
        input_output_aliases={2 * sources + i: i for i in range(len(kept))},
        compiler_params=pltpu.CompilerParams(vmem_limit_bytes=VMEM_LIMIT),
        cost_estimate=estimate,
        name="weights",
    )(*turned, *deltas, *kept)


def gate_kernel(*refs):
    del refs


def gate(arrays, tokens):
    hbm = pl.BlockSpec(memory_space=pl.ANY)
    return pl.pallas_call(
        gate_kernel,
        out_shape=tuple(jax.ShapeDtypeStruct(x.shape, x.dtype) for x in arrays),
        in_specs=[hbm] * (len(arrays) + len(tokens)),
        out_specs=(hbm,) * len(arrays),
        input_output_aliases={i: i for i in range(len(arrays))},
        compiler_params=pltpu.CompilerParams(vmem_limit_bytes=VMEM_LIMIT),
        cost_estimate=small_cost(),
        name="gate",
    )(*arrays, *tokens)


def join_kernel(inner_ref, other_ref, end_ref, *rest):
    out_ref, token_ref = rest[-2:]
    token_ref[...] = jnp.zeros_like(token_ref)
    index = lax.axis_index("tensor")
    inner = (index > 0) & (index < lax.axis_size("tensor") - 1)

    @pl.when(inner)
    def _():
        out_ref[...] = (
            inner_ref[...].astype(jnp.float32) + other_ref[...].astype(jnp.float32)
        ).astype(jnp.bfloat16)

    @pl.when(jnp.logical_not(inner))
    def _():
        out_ref[...] = end_ref[...]


def join(inner_part, other, end_part, tokens):
    vmem = pl.BlockSpec(memory_space=pltpu.VMEM)
    return pl.pallas_call(
        join_kernel,
        out_shape=(
            jax.ShapeDtypeStruct(end_part.shape, end_part.dtype),
            jax.ShapeDtypeStruct((8, 128), jnp.float32),
        ),
        in_specs=[vmem] * 3 + [pl.BlockSpec(memory_space=pl.ANY)] * len(tokens),
        out_specs=(vmem, vmem),
        compiler_params=pltpu.CompilerParams(vmem_limit_bytes=VMEM_LIMIT),
        cost_estimate=small_cost(),
        name="join",
    )(inner_part, other, end_part, *tokens)


def finish_kernel(width, for_ends, for_inner, input_ref, gain_ref, inverse_ref, *refs):
    part_refs, (out_ref, sum_ref) = refs[:-3], refs[-2:]
    rows, wide = out_ref.shape
    index = lax.axis_index("tensor")
    ends = ((index == 0) | (index == lax.axis_size("tensor") - 1)).astype(jnp.float32)
    total = None
    for place, part_ref in enumerate(part_refs):
        part = part_ref[...].astype(jnp.float32)
        if place < for_ends:
            part = part * ends
        elif place < for_ends + for_inner:
            part = part * (1.0 - ends)
        total = part if total is None else total + part
    d_normed = total[:rows]
    centre = total[rows:, :rows].T[:, :1] * (1.0 / width)
    inverse = inverse_ref[...]
    scaled = input_ref[...].astype(jnp.float32) * inverse
    out_ref[...] = (
        inverse * ((1.0 + gain_ref[...]) * d_normed - scaled * centre)
    ).astype(jnp.bfloat16)
    sum_ref[...] = jnp.sum(d_normed * scaled, axis=0, keepdims=True)


def finish(width, for_ends, for_inner, input_columns, gain_columns, inverse, parts, token):
    rows, wide = input_columns.shape
    whole = lambda array: pl.BlockSpec(array.shape, lambda i: (0, 0))
    return pl.pallas_call(
        functools.partial(finish_kernel, width, for_ends, for_inner),
        out_shape=(
            jax.ShapeDtypeStruct((rows, wide), jnp.bfloat16),
            jax.ShapeDtypeStruct((1, wide), jnp.float32),
        ),
        grid=(1,),
        in_specs=[whole(x) for x in (input_columns, gain_columns, inverse, *parts)]
        + [pl.BlockSpec(memory_space=pl.ANY)],
        out_specs=(
            pl.BlockSpec((rows, wide), lambda i: (0, 0)),
            pl.BlockSpec((1, wide), lambda i: (0, 0)),
        ),
        compiler_params=pltpu.CompilerParams(vmem_limit_bytes=VMEM_LIMIT),
        cost_estimate=small_cost(),
        name="finish",
    )(input_columns, gain_columns, inverse, *parts, token)


def total_kernel(*refs):
    refs[-1][...] = (refs[0][...] + refs[1][...]) + (refs[2][...] + refs[3][...])


def total_of_four(arrays, token):
    whole = pl.BlockSpec(arrays[0].shape, lambda i: (0, 0))
    return pl.pallas_call(
        total_kernel,
        out_shape=jax.ShapeDtypeStruct(arrays[0].shape, arrays[0].dtype),
        grid=(1,),
        in_specs=[whole] * 4 + [pl.BlockSpec(memory_space=pl.ANY)],
        out_specs=whole,
        compiler_params=pltpu.CompilerParams(vmem_limit_bytes=VMEM_LIMIT),
        cost_estimate=small_cost(),
        name="total",
    )(*arrays, token)


def branch_send(array, chips, shift, swap):
    pairs = [
        (c * 2 + k, ((c + shift) % chips) * 2 + (k ^ swap)) for c in range(chips) for k in range(2)
    ]
    return lax.ppermute(array, "branch", pairs)


def pick(table, index):
    chosen = table[-1]
    for place in range(len(table) - 2, -1, -1):
        chosen = jnp.where(index == place, table[place], chosen)
    return chosen


def scatter_begin(project, total):
    index = lambda: lax.axis_index("tensor")
    if total != 4:
        parts = project(lambda i: lax.rem(index() + i + 1, total), total)
        arrived = [
            lax.ppermute(part, "tensor", [(t, (t + shift) % total) for t in range(total)])
            for shift, part in zip(range(1, total), parts[:-1])
        ]
        return parts, arrived
    table = [[3, 0, 3, 0], [0, 2, 1, 3], [2, 3, 0, 1], [1, 1, 2, 2]]
    order = lambda base: lambda i: pick([pick(row, index()) for row in table[base : base + 2]], i)
    first, second = project(order(0), 2)
    from_first = lax.ppermute(first, "tensor", [(0, 1), (1, 0), (2, 3), (3, 2)])
    from_inner = lax.ppermute(second, "tensor", [(1, 2), (2, 1)])
    third, fourth = project(order(2), 2)
    return (first, second, third, fourth), (from_first, from_inner)


def scatter_end(parts, arrived, total, tokens):
    if total != 4:
        return [parts[-1], *arrived], 0, 0, arrived[0], arrived
    _, second, third, fourth = parts
    from_first, from_inner = arrived
    joined, token = join(third, from_first, fourth, (from_inner, *tokens))
    (held,) = gate((third,), (token,))
    from_ends = lax.ppermute(held, "tensor", [(0, 2), (3, 1)])
    from_joined = lax.ppermute(joined, "tensor", [(1, 3), (2, 0), (0, 1), (3, 2)])
    return [from_first, second, fourth, from_inner, from_ends, from_joined], 2, 1, token, (from_ends, from_joined)


def local(layer_input, norm_gain, w_query, w_key, w_value, head_grad, parents, row_counts):
    branch_total = lax.axis_size("branch")
    tensor_total = lax.axis_size("tensor")
    slots = row_counts.shape[0] // branch_total
    rows, width = layer_input.shape
    column_width = width // tensor_total
    depth = width // branch_total
    chips = branch_total // 2
    group = w_query.shape[1] // w_key.shape[1]
    kv_local = w_key.shape[1] // HEAD_DIM
    offsets = [(shift, swap) for shift in range(chips) for swap in range(2)]

    def targets():
        index = lax.axis_index("branch")
        chip, core = index // 2, index % 2
        return [lax.rem(chip + s, chips) * 2 + lax.rem(core + e, 2) for s, e in offsets]

    pieces = cut_columns(layer_input, targets, branch_total)
    shared = [branch_send(piece, chips, s, e) for piece, (s, e) in zip(pieces[1:], offsets[1:])]
    delta, centre, inverse, scaled = attention_backward(
        layer_input, norm_gain, w_query, w_key, w_value, head_grad, parents, row_counts, slots
    )

    def project(order, pieces):
        return back_project(
            order, pieces, delta, centre, w_query, w_key, w_value, tensor_total
        )

    parts, arrived = scatter_begin(project, tensor_total)

    (first,) = gate(scaled[:1], (*shared, parts[1]))
    sent = [branch_send(first, chips, s, 0) for s in range(1, chips)]
    gain_own = lax.dynamic_slice_in_dim(norm_gain, lax.axis_index("branch") * depth, depth)
    turned = turn([pieces[0]] + shared, gain_own.reshape(1, depth))
    parts, for_ends, for_inner, met, late = scatter_end(parts, arrived, tensor_total, turned[:1])
    *sent, first = gate((*sent, first), (met,))
    others = gate(scaled[1:], (sent[0],)) if kv_local > 1 else ()
    weights, tokens = None, []
    for head, scaled_delta in enumerate((first, *others)):
        if head > 0:
            sent = [branch_send(scaled_delta, chips, s, 0) for s in range(1, chips)]
            scaled_delta, *sent = gate((scaled_delta, *sent), (*late, tokens[0]))
        gathered = []
        for part in [scaled_delta] + sent:
            gathered += [part, branch_send(part, chips, 0, 1)]
        *weights, token = weight_gradients(turned, gathered, head, kv_local, group, weights)
        tokens.append(token)

    column_start = lax.axis_index("tensor") * column_width
    input_columns = lax.dynamic_slice_in_dim(layer_input, column_start, column_width, 1)
    gain_columns = lax.dynamic_slice_in_dim(norm_gain, column_start, column_width, 0)
    grad_input, gain_sum = finish(
        width,
        for_ends,
        for_inner,
        input_columns,
        gain_columns.reshape(1, column_width),
        inverse,
        parts,
        tokens[0],
    )
    if chips == 2:
        sums = [gain_sum] + [branch_send(gain_sum, chips, s, e) for s, e in offsets[1:]]
        grad_gain = total_of_four(sums, tokens[-1])
    else:
        grad_gain = lax.psum(gain_sum, "branch")
    return (grad_input, *weights, grad_gain.reshape(column_width))


def solution(mesh):
    placed = (
        P(("parts", "branch"), None),
        P(),
        P(None, "tensor"),
        P(None, "tensor"),
        P(None, "tensor"),
        P(("parts", "branch"), "tensor"),
        P(("parts", "branch")),
        P("parts"),
    )
    return jax.shard_map(
        local,
        mesh=mesh,
        in_specs=placed,
        out_specs=(
            P(("parts", "branch"), "tensor"),
            P(("parts", "branch"), "tensor"),
            P(("parts", "branch"), "tensor"),
            P(("parts", "branch"), "tensor"),
            P(("parts", "tensor")),
        ),
        check_vma=False,
    )
```

```python
import functools

import jax
import jax.numpy as jnp
from jax import lax
from jax.experimental import pallas as pl
from jax.experimental.pallas import tpu as pltpu
from jax.sharding import PartitionSpec as P

HEAD_DIM = 256
MIB = 1024 * 1024
CENTRE_ROWS = 16
VMEM_LIMIT = 64 * MIB


epsilon = 1e-06
softcap_limit = 50.0


def nn_dot(left, right):
    return lax.dot_general(
        left, right, (((1,), (0,)), ((), ())), preferred_element_type=jnp.float32
    )


def nt_dot(left, right):
    return lax.dot_general(
        left, right, (((1,), (1,)), ((), ())), preferred_element_type=jnp.float32
    )


def tn_dot(left, right):
    return lax.dot_general(
        left, right, (((0,), (0,)), ((), ())), preferred_element_type=jnp.float32
    )


def small_cost():
    return pl.CostEstimate(flops=1000000, bytes_accessed=100000, transcendentals=0)


def norm_kernel(targets, input_ref, gain_ref, inverse_ref, *rest):
    piece_refs, turned = rest[:-1], rest[-1]
    rows, width = input_ref.shape
    values = input_ref[...].astype(jnp.float32)
    inverse = lax.rsqrt(jnp.mean(values * values, axis=-1, keepdims=True) + epsilon)
    inverse_ref[...] = inverse
    gain = gain_ref[...].reshape(1, width)
    turned[...] = (values * inverse * (1.0 + gain)).astype(jnp.bfloat16).T
    depth = width // len(piece_refs)
    for target, piece_ref in zip(targets(), piece_refs):
        start = pl.multiple_of(target * depth, 16)
        piece_ref[...] = turned[pl.ds(start, depth), :]


def normalize(layer_input, norm_gain, targets, pieces, block):
    rows, width = layer_input.shape
    depth = width // pieces
    out = pl.pallas_call(
        functools.partial(norm_kernel, targets),
        out_shape=(jax.ShapeDtypeStruct((rows, 1), jnp.float32),)
        + (jax.ShapeDtypeStruct((depth, rows), jnp.bfloat16),) * pieces,
        grid=(rows // block,),
        in_specs=[
            pl.BlockSpec((block, width), lambda i: (i, 0)),
            pl.BlockSpec((width,), lambda i: (0,)),
        ],
        out_specs=(pl.BlockSpec((block, 1), lambda i: (i, 0)),)
        + (pl.BlockSpec((depth, block), lambda i: (0, i)),) * pieces,
        scratch_shapes=[pltpu.VMEM((width, block), jnp.bfloat16)],
        compiler_params=pltpu.CompilerParams(vmem_limit_bytes=VMEM_LIMIT),
        cost_estimate=small_cost(),
        name="norm",
    )(layer_input, norm_gain)
    return out[0], out[1:]


def ancestor_mask(parent_row):
    rows = parent_row.shape[1]
    row = lax.broadcasted_iota(jnp.int32, (rows, rows), 0)
    column = lax.broadcasted_iota(jnp.int32, (rows, rows), 1)
    reached = jnp.where((parent_row == row) | (row == column), 1.0, 0.0)
    for squaring in range(rows.bit_length() - 1):
        halfway = reached.astype(jnp.bfloat16)
        reached = jnp.minimum(nn_dot(halfway, halfway), 1.0)
    return reached.T


def attention_kernel(
    slots,
    group,
    kv_local,
    order,
    blocks,
    columns,
    shares,
    count_ref,
    parent_ref,
    inverse_ref,
    gain_ref,
    input_hbm,
    query_hbm,
    key_hbm,
    value_hbm,
    grad_hbm,
    *rest,
):
    delta_hbm, rest = rest[: len(shares)], rest[len(shares) :]
    part_hbm, rest = rest[:blocks], rest[blocks:]
    column_hbm, column_gain_ref, rest = rest[0], rest[1], rest[2:]
    (
        input_ref,
        gain_row,
        query_ref,
        key_ref,
        value_ref,
        grad_ref,
        sum_ref,
        delta_ref,
        query_turned,
        key_turned,
        value_turned,
        allowed_ref,
        centre_ref,
        kept,
        load_sem,
        weight_sem,
        store_sem,
        part_sem,
    ) = rest
    head_dim = HEAD_DIM
    rows, width = input_ref.shape
    block = rows // slots
    mid = group * head_dim
    steps = weight_sem.shape[0]
    chunk = width // steps
    weights = ((query_hbm, query_ref, mid, 0), (key_hbm, key_ref, head_dim, mid))
    weights += ((value_hbm, value_ref, head_dim, mid + head_dim),)

    def fetch(step, which):
        lines = pl.ds(pl.multiple_of(step * chunk, chunk), chunk)
        source, kept_ref = weights[which][:2]
        return pltpu.make_async_copy(
            source.at[lines, :], kept_ref.at[lines, :], weight_sem.at[step, which]
        )

    input_load = pltpu.make_async_copy(input_hbm, input_ref, load_sem.at[0])
    grad_load = pltpu.make_async_copy(grad_hbm, grad_ref, load_sem.at[1])
    input_load.start()
    for step in range(steps):
        for which in range(3):
            fetch(step, which).start()
    grad_load.start()
    gain_row[...] = gain_ref[...].reshape(1, width)

    first_count = lax.axis_index("branch") * slots
    parents = parent_ref[...].reshape(1, rows)
    for slot in range(slots):
        allowed_ref[slot] = ancestor_mask(parents[:, slot * block : (slot + 1) * block])
    sum_ref[...] = jnp.zeros_like(sum_ref)
    inverse = inverse_ref[...]
    input_load.wait()
    stores = []
    if columns:
        start = pl.multiple_of(lax.axis_index("tensor") * columns, 128)
        stores.append(
            pltpu.make_async_copy(
                input_ref.at[:, pl.ds(start, columns)], column_hbm, store_sem.at[0]
            )
        )
        stores[0].start()
        column_gain_ref[...] = gain_row[:, pl.ds(start, columns)]
    else:
        column_gain_ref[...] = jnp.zeros_like(column_gain_ref)

    def project(step, carry):
        lines = pl.ds(pl.multiple_of(step * chunk, chunk), chunk)
        gain = 1.0 + gain_row[:, lines]
        normed = (input_ref[:, lines].astype(jnp.float32) * inverse * gain).astype(jnp.bfloat16)
        for which, (_, kept_ref, wide, place) in enumerate(weights):
            fetch(step, which).wait()
            term = nn_dot(normed, kept_ref[lines, :])
            for h in range(kv_local):
                sum_ref[h, :, place : place + wide] += term[:, h * wide : (h + 1) * wide]
        return carry

    lax.fori_loop(0, steps, project, 0)
    grad_load.wait()
    scale = head_dim ** (-0.5)
    centre_ref[...] = jnp.zeros_like(centre_ref)

    def attend(h, carry):
        for slot in range(slots):
            lines = slice(slot * block, (slot + 1) * block)
            live = (
                lax.broadcasted_iota(jnp.int32, (block, mid), 0) < count_ref[first_count + slot]
            )
            columns = pl.ds(pl.multiple_of(h * mid, mid), mid)
            grad_rows = jnp.where(live, grad_ref[lines, columns].astype(jnp.float32), 0.0)
            pair = [slice(g * head_dim, (g + 1) * head_dim) for g in range(group)]
            grads = jnp.concatenate([grad_rows[:, p] for p in pair], axis=0).astype(jnp.bfloat16)
            queries = jnp.concatenate([sum_ref[h, lines, p] for p in pair], axis=0)
            queries = queries.astype(jnp.bfloat16)
            keys = sum_ref[h, lines, mid : mid + head_dim].astype(jnp.bfloat16)
            values = sum_ref[h, lines, mid + head_dim :].astype(jnp.bfloat16)
            allowed = jnp.concatenate([allowed_ref[slot]] * group, axis=0)
            bounded = jnp.tanh(nt_dot(queries, keys) * (scale / softcap_limit))
            weighted = allowed * jnp.exp(softcap_limit * bounded)
            probabilities = weighted * (1.0 / jnp.sum(weighted, axis=-1, keepdims=True))
            d_probs = nt_dot(grads, values)
            d_scores = probabilities * (
                d_probs - jnp.sum(probabilities * d_probs, axis=-1, keepdims=True)
            )
            d_raw = (d_scores * (1.0 - bounded * bounded) * scale).astype(jnp.bfloat16)
            prob_half = probabilities.astype(jnp.bfloat16)
            d_query = nn_dot(d_raw, keys)
            d_key = tn_dot(d_raw, queries)
            d_value = tn_dot(prob_half, grads)
            places = [
                (d_query[g * block : (g + 1) * block], query_turned, h * mid + g * head_dim)
                for g in range(group)
            ]
            places += [(d_key, key_turned, h * head_dim), (d_value, value_turned, h * head_dim)]
            product = None
            for which, (part, turned_ref, start) in enumerate(places):
                half = part.astype(jnp.bfloat16)
                line = which * rows + slot * block
                delta_ref[h, line : line + block, :] = half
                spot = pl.ds(pl.multiple_of(start, head_dim), head_dim)
                turned_ref[spot, lines] = half.T
                term = half.astype(jnp.float32) * sum_ref[
                    h, lines, which * head_dim : (which + 1) * head_dim
                ]
                product = term if product is None else product + term
            centre_ref[lines, :] += jnp.sum(product, axis=-1, keepdims=True)
        return carry

    lax.fori_loop(0, kv_local, attend, 0)
    lasts = []
    for share, out in zip(shares, delta_hbm):
        for place, block_index in enumerate(share):
            h, which = divmod(block_index, group + 2)
            lasts.append(
                pltpu.make_async_copy(
                    delta_ref.at[h, pl.ds(which * rows, rows), :],
                    out.at[pl.ds(place * rows, rows), :],
                    store_sem.at[1 + len(lasts)],
                )
            )
    for store in lasts:
        store.start()

    centre = jnp.broadcast_to(centre_ref[...], (rows, 128)).T[:CENTRE_ROWS].astype(jnp.bfloat16)
    span = width // blocks
    cuts = 2
    cut_lines = span // cuts
    parts = [
        pltpu.make_async_copy(kept.at[place], part_hbm[place], part_sem.at[place])
        for place in range(blocks)
    ]

    def project_back(step, carry):
        place, cut = step // cuts, lax.rem(step, cuts)
        lines = pl.ds(pl.multiple_of(order(place) * span + cut * cut_lines, 16), cut_lines)
        total = nn_dot(query_ref[lines, :], query_turned[...])
        total += nn_dot(key_ref[lines, :], key_turned[...])
        total += nn_dot(value_ref[lines, :], value_turned[...])
        spot = pl.ds(pl.multiple_of(cut * cut_lines, 16), cut_lines)
        kept[place, spot, :] = total.astype(jnp.bfloat16)
        for which, part in enumerate(parts):

            @pl.when((place == which) & (cut == cuts - 1))
            def _():
                kept[which, span:, :] = centre
                part.start()

        return carry

    lax.fori_loop(0, blocks * cuts, project_back, 0)
    for store in stores + lasts + parts:
        store.wait()


def attention_backward(
    layer_input,
    inverse,
    norm_gain,
    w_query,
    w_key,
    w_value,
    head_grad,
    parents,
    counts,
    slots,
    order,
    blocks,
    shares,
):
    rows, width = layer_input.shape
    kv_local = w_key.shape[1] // HEAD_DIM
    group = w_query.shape[1] // w_key.shape[1]
    span = (group + 2) * HEAD_DIM
    stack = (group + 2) * rows
    column_width = width // blocks
    cut = column_width % 128 == 0
    wide = column_width if cut else 128
    steps = width // 512 if width % 512 == 0 else 1
    part_shape = (column_width + CENTRE_ROWS, rows)
    hbm = pl.BlockSpec(memory_space=pl.ANY)
    vmem = pl.BlockSpec(memory_space=pltpu.VMEM)
    half = lambda *shape: jax.ShapeDtypeStruct(shape, jnp.bfloat16)
    out = pl.pallas_call(
        functools.partial(
            attention_kernel, slots, group, kv_local, order, blocks, wide if cut else 0, shares
        ),
        out_shape=tuple(half(len(share) * rows, HEAD_DIM) for share in shares)
        + (half(*part_shape),) * blocks
        + (half(rows, wide), jax.ShapeDtypeStruct((1, wide), jnp.float32)),
        in_specs=[pl.BlockSpec(memory_space=pltpu.SMEM), vmem, vmem, vmem] + [hbm] * 5,
        out_specs=(hbm,) * (1 + len(shares) + blocks) + (vmem,),
        scratch_shapes=[
            pltpu.VMEM((rows, width), jnp.bfloat16),
            pltpu.VMEM((1, width), jnp.float32),
            pltpu.VMEM(w_query.shape, jnp.bfloat16),
            pltpu.VMEM(w_key.shape, jnp.bfloat16),
            pltpu.VMEM(w_value.shape, jnp.bfloat16),
            pltpu.VMEM(head_grad.shape, jnp.bfloat16),
            pltpu.VMEM((kv_local, rows, span), jnp.float32),
            pltpu.VMEM((kv_local, stack, HEAD_DIM), jnp.bfloat16),
            pltpu.VMEM((w_query.shape[1], rows), jnp.bfloat16),
            pltpu.VMEM((w_key.shape[1], rows), jnp.bfloat16),
            pltpu.VMEM((w_value.shape[1], rows), jnp.bfloat16),
            pltpu.VMEM((slots, rows // slots, rows // slots), jnp.float32),
            pltpu.VMEM((rows, 1), jnp.float32),
            pltpu.VMEM((blocks, *part_shape), jnp.bfloat16),
            pltpu.SemaphoreType.DMA((2,)),
            pltpu.SemaphoreType.DMA((steps, 3)),
            pltpu.SemaphoreType.DMA((1 + kv_local * (group + 2),)),
            pltpu.SemaphoreType.DMA((blocks,)),
        ],
        compiler_params=pltpu.CompilerParams(vmem_limit_bytes=VMEM_LIMIT),
        cost_estimate=small_cost(),
        name="attention",
    )(counts, parents, inverse, norm_gain, layer_input, w_query, w_key, w_value, head_grad)
    deltas, parts = out[: len(shares)], out[len(shares) : len(shares) + blocks]
    if cut:
        input_cut, gain_cut = out[-2], out[-1]
    else:
        start = lax.axis_index("tensor") * column_width
        input_cut = lax.dynamic_slice_in_dim(layer_input, start, column_width, 1)
        gain_cut = lax.dynamic_slice_in_dim(norm_gain, start, column_width, 0)
        gain_cut = gain_cut.reshape(1, column_width)
    return deltas, parts, input_cut, gain_cut


def weight_kernel(outs, sources, *refs):
    turned_hbm, delta_hbm = refs[:sources], refs[sources : 2 * sources]
    out_hbm, token_ref = refs[-10:-7], refs[-7]
    turned_ref, delta_ref, kept, turned_sem, delta_sem, store_sem = refs[-6:]
    token_ref[...] = jnp.zeros_like(token_ref)
    rows = turned_ref.shape[2]
    loads = []
    for place in range(sources):
        loads.append(
            pltpu.make_async_copy(
                turned_hbm[place], turned_ref.at[place], turned_sem.at[place]
            )
        )
        loads.append(
            pltpu.make_async_copy(delta_hbm[place], delta_ref.at[place], delta_sem.at[place])
        )
    for load in loads:
        load.start()
    for load in loads:
        load.wait()
    stores = [
        pltpu.make_async_copy(
            kept.at[block],
            out_hbm[which].at[:, pl.ds(column * HEAD_DIM, HEAD_DIM)],
            store_sem.at[block],
        )
        for block, (which, column) in enumerate(outs)
    ]

    def fill(block, carry):
        lines = pl.ds(pl.multiple_of(block * rows, rows), rows)
        total = None
        for place in range(sources):
            term = nn_dot(turned_ref[place], delta_ref[place, lines, :])
            total = term if total is None else total + term
        kept[block] = total
        for which, store in enumerate(stores):

            @pl.when(block == which)
            def _():
                store.start()

        return carry

    lax.fori_loop(0, len(outs), fill, 0)
    for store in stores:
        store.wait()


def weight_gradients(turned, deltas, share, kv_local, group, before):
    depth, rows = turned[0].shape
    sources = len(turned)
    outs = []
    for block in share:
        h, which = divmod(block, group + 2)
        outs.append((0, h * group + which) if which < group else (which - group + 1, h))
    kept = list(before) if before is not None else []
    hbm = pl.BlockSpec(memory_space=pl.ANY)
    return pl.pallas_call(
        functools.partial(weight_kernel, outs, sources),
        out_shape=(
            jax.ShapeDtypeStruct((depth, kv_local * group * HEAD_DIM), jnp.float32),
            jax.ShapeDtypeStruct((depth, kv_local * HEAD_DIM), jnp.float32),
            jax.ShapeDtypeStruct((depth, kv_local * HEAD_DIM), jnp.float32),
            jax.ShapeDtypeStruct((8, 128), jnp.float32),
        ),
        in_specs=[hbm] * (2 * sources + len(kept)),
        out_specs=(hbm,) * 3 + (pl.BlockSpec(memory_space=pltpu.VMEM),),
        input_output_aliases={2 * sources + i: i for i in range(len(kept))},
        scratch_shapes=[
            pltpu.VMEM((sources, depth, rows), jnp.bfloat16),
            pltpu.VMEM((sources, len(share) * rows, HEAD_DIM), jnp.bfloat16),
            pltpu.VMEM((len(share), depth, HEAD_DIM), jnp.float32),
            pltpu.SemaphoreType.DMA((sources,)),
            pltpu.SemaphoreType.DMA((sources,)),
            pltpu.SemaphoreType.DMA((len(share),)),
        ],
        compiler_params=pltpu.CompilerParams(vmem_limit_bytes=VMEM_LIMIT),
        cost_estimate=small_cost(),
        name="weights",
    )(*turned, *deltas, *kept)


def gate_kernel(*refs):
    del refs


def gate(arrays, tokens):
    hbm = pl.BlockSpec(memory_space=pl.ANY)
    return pl.pallas_call(
        gate_kernel,
        out_shape=tuple(jax.ShapeDtypeStruct(x.shape, x.dtype) for x in arrays),
        in_specs=[hbm] * (len(arrays) + len(tokens)),
        out_specs=(hbm,) * len(arrays),
        input_output_aliases={i: i for i in range(len(arrays))},
        compiler_params=pltpu.CompilerParams(vmem_limit_bytes=VMEM_LIMIT),
        cost_estimate=small_cost(),
        name="gate",
    )(*arrays, *tokens)


def join_kernel(inner_ref, other_ref, end_ref, *rest):
    out_ref, token_ref = rest[-2:]
    token_ref[...] = jnp.zeros_like(token_ref)
    index = lax.axis_index("tensor")
    inner = (index > 0) & (index < lax.axis_size("tensor") - 1)

    @pl.when(inner)
    def _():
        out_ref[...] = (
            inner_ref[...].astype(jnp.float32) + other_ref[...].astype(jnp.float32)
        ).astype(jnp.bfloat16)

    @pl.when(jnp.logical_not(inner))
    def _():
        out_ref[...] = end_ref[...]


def join(inner_part, other, end_part, tokens):
    vmem = pl.BlockSpec(memory_space=pltpu.VMEM)
    return pl.pallas_call(
        join_kernel,
        out_shape=(
            jax.ShapeDtypeStruct(end_part.shape, end_part.dtype),
            jax.ShapeDtypeStruct((8, 128), jnp.float32),
        ),
        in_specs=[vmem] * 3 + [pl.BlockSpec(memory_space=pl.ANY)] * len(tokens),
        out_specs=(vmem, vmem),
        compiler_params=pltpu.CompilerParams(vmem_limit_bytes=VMEM_LIMIT),
        cost_estimate=small_cost(),
        name="join",
    )(inner_part, other, end_part, *tokens)


def finish_kernel(width, for_ends, for_inner, count, input_ref, gain_ref, inverse_ref, *refs):
    part_refs, centre_refs, (out_ref, sum_ref) = refs[:count], refs[count : 2 * count], refs[-2:]
    step = pl.program_id(0)
    index = lax.axis_index("tensor")
    ends = ((index == 0) | (index == lax.axis_size("tensor") - 1)).astype(jnp.float32)

    def total_of(part_refs):
        total = None
        for place, part_ref in enumerate(part_refs):
            part = part_ref[...].astype(jnp.float32)
            if place < for_ends:
                part = part * ends
            elif place < for_ends + for_inner:
                part = part * (1.0 - ends)
            total = part if total is None else total + part
        return total

    d_normed = total_of(part_refs).T
    centre = total_of(centre_refs).T[:, :1] * (1.0 / width)
    inverse = inverse_ref[...]
    scaled = input_ref[...].astype(jnp.float32) * inverse
    out_ref[...] = (
        inverse * ((1.0 + gain_ref[...]) * d_normed - scaled * centre)
    ).astype(jnp.bfloat16)

    @pl.when(step == 0)
    def _():
        sum_ref[...] = jnp.zeros_like(sum_ref)

    sum_ref[...] += jnp.sum(d_normed * scaled, axis=0, keepdims=True)


def finish(width, for_ends, for_inner, input_columns, gain_columns, inverse, parts, token):
    rows, wide = input_columns.shape
    some = 128
    whole = pl.BlockSpec((1, wide), lambda i: (0, 0))
    return pl.pallas_call(
        functools.partial(finish_kernel, width, for_ends, for_inner, len(parts)),
        out_shape=(
            jax.ShapeDtypeStruct((rows, wide), jnp.bfloat16),
            jax.ShapeDtypeStruct((1, wide), jnp.float32),
        ),
        grid=(rows // some,),
        in_specs=[
            pl.BlockSpec((some, wide), lambda i: (i, 0)),
            whole,
            pl.BlockSpec((some, 1), lambda i: (i, 0)),
        ]
        + [pl.BlockSpec((wide, some), lambda i: (0, i))] * len(parts)
        + [pl.BlockSpec((CENTRE_ROWS, some), lambda i: (wide // CENTRE_ROWS, i))] * len(parts)
        + [pl.BlockSpec(memory_space=pl.ANY)],
        out_specs=(pl.BlockSpec((some, wide), lambda i: (i, 0)), whole),
        compiler_params=pltpu.CompilerParams(vmem_limit_bytes=VMEM_LIMIT),
        cost_estimate=small_cost(),
        name="finish",
    )(input_columns, gain_columns, inverse, *parts, *parts, token)


def total_kernel(*refs):
    total = (refs[0][...] + refs[1][...]) + (refs[2][...] + refs[3][...])
    refs[-1][...] = total.reshape(refs[-1].shape)


def total_of_four(arrays):
    whole = pl.BlockSpec(arrays[0].shape, lambda i: (0, 0))
    wide = arrays[0].shape[1]
    return pl.pallas_call(
        total_kernel,
        out_shape=jax.ShapeDtypeStruct((wide,), arrays[0].dtype),
        grid=(1,),
        in_specs=[whole] * 4,
        out_specs=pl.BlockSpec((wide,), lambda i: (0,)),
        compiler_params=pltpu.CompilerParams(vmem_limit_bytes=VMEM_LIMIT),
        cost_estimate=small_cost(),
        name="total",
    )(*arrays)


def branch_send(array, chips, shift, swap):
    pairs = [
        (c * 2 + k, ((c + shift) % chips) * 2 + (k ^ swap)) for c in range(chips) for k in range(2)
    ]
    return lax.ppermute(array, "branch", pairs)


def pick(table, index):
    chosen = table[-1]
    for place in range(len(table) - 2, -1, -1):
        chosen = jnp.where(index == place, table[place], chosen)
    return chosen


def scatter_order(total):
    index = lax.axis_index("tensor")
    if total != 4:
        return lambda place: lax.rem(index + place + 1, total)
    table = [[3, 0, 3, 0], [0, 2, 1, 3], [2, 3, 0, 1], [1, 1, 2, 2]]
    here = [pick(row, index) for row in table]
    return lambda place: pick(here, place)


def scatter_begin(parts, total):
    if total != 4:
        return [
            lax.ppermute(part, "tensor", [(t, (t + shift) % total) for t in range(total)])
            for shift, part in zip(range(1, total), parts[:-1])
        ]
    from_first = lax.ppermute(parts[0], "tensor", [(0, 1), (1, 0), (2, 3), (3, 2)])
    from_inner = lax.ppermute(parts[1], "tensor", [(1, 2), (2, 1)])
    return from_first, from_inner


def scatter_end(parts, arrived, total, tokens):
    if total != 4:
        return [parts[-1], *arrived], 0, 0, arrived[0], arrived
    _, second, third, fourth = parts
    from_first, from_inner = arrived
    joined, token = join(third, from_first, fourth, (from_inner, *tokens))
    (held,) = gate((third,), (token,))
    from_ends = lax.ppermute(held, "tensor", [(0, 2), (3, 1)])
    from_joined = lax.ppermute(joined, "tensor", [(1, 3), (2, 0), (0, 1), (3, 2)])
    return [from_first, second, fourth, from_inner, from_ends, from_joined], 2, 1, token, (from_ends, from_joined)


def local(layer_input, norm_gain, w_query, w_key, w_value, head_grad, parents, row_counts):
    branch_total = lax.axis_size("branch")
    tensor_total = lax.axis_size("tensor")
    slots = row_counts.shape[0] // branch_total
    rows, width = layer_input.shape
    column_width = width // tensor_total
    chips = branch_total // 2
    group = w_query.shape[1] // w_key.shape[1]
    kv_local = w_key.shape[1] // HEAD_DIM
    offsets = [(shift, swap) for shift in range(chips) for swap in range(2)]
    blocks = list(range(kv_local * (group + 2)))
    early = blocks[: group + 2] + [h * (group + 2) + group for h in range(1, kv_local)]
    shares = [early, [block for block in blocks if block not in early]]
    shares = [share for share in shares if share]

    def targets():
        index = lax.axis_index("branch")
        chip, core = index // 2, index % 2
        return [lax.rem(chip + s, chips) * 2 + lax.rem(core + e, 2) for s, e in offsets]

    inverse, pieces = normalize(layer_input, norm_gain, targets, branch_total, rows // slots)
    shared = [branch_send(piece, chips, s, e) for piece, (s, e) in zip(pieces[1:], offsets[1:])]
    deltas, parts, input_columns, gain_columns = attention_backward(
        layer_input,
        inverse,
        norm_gain,
        w_query,
        w_key,
        w_value,
        head_grad,
        parents,
        row_counts,
        slots,
        lambda place: scatter_order(tensor_total)(place),
        tensor_total,
        shares,
    )
    arrived = scatter_begin(parts, tensor_total)

    (first,) = gate(deltas[:1], shared)
    sent = [branch_send(first, chips, s, 0) for s in range(1, chips)]
    parts, for_ends, for_inner, met, _ = scatter_end(parts, arrived, tensor_total, ())
    *sent, first = gate((*sent, first), (met,))
    others = gate(deltas[1:], (sent[0],)) if deltas[1:] else ()
    turned = [pieces[0]] + shared
    weights, token = None, None
    for share, delta in zip(shares, (first, *others)):
        if token is not None:
            sent = [branch_send(delta, chips, s, 0) for s in range(1, chips)]
            delta, *sent = gate((delta, *sent), (token,))
        gathered = []
        for part in [delta] + sent:
            gathered += [part, branch_send(part, chips, 0, 1)]
        *weights, token = weight_gradients(turned, gathered, share, kv_local, group, weights)

    grad_input, gain_sum = finish(
        width, for_ends, for_inner, input_columns, gain_columns, inverse, parts, token
    )
    if chips == 2:
        sums = [gain_sum] + [branch_send(gain_sum, chips, s, e) for s, e in offsets[1:]]
        grad_gain = total_of_four(sums)
    else:
        grad_gain = lax.psum(gain_sum, "branch").reshape(column_width)
    return (grad_input, *weights, grad_gain)


def solution(mesh):
    placed = (
        P(("parts", "branch"), None),
        P(),
        P(None, "tensor"),
        P(None, "tensor"),
        P(None, "tensor"),
        P(("parts", "branch"), "tensor"),
        P(("parts", "branch")),
        P("parts"),
    )
    return jax.shard_map(
        local,
        mesh=mesh,
        in_specs=placed,
        out_specs=(
            P(("parts", "branch"), "tensor"),
            P(("parts", "branch"), "tensor"),
            P(("parts", "branch"), "tensor"),
            P(("parts", "branch"), "tensor"),
            P(("parts", "tensor")),
        ),
        check_vma=False,
    )
```

```python
import functools

import jax
import jax.numpy as jnp
from jax import lax
from jax.experimental import pallas as pl
from jax.experimental.pallas import tpu as pltpu
from jax.sharding import PartitionSpec as P

HEAD_DIM = 256
MIB = 1024 * 1024
CENTRE_ROWS = 16
VMEM_LIMIT = 64 * MIB


epsilon = 1e-06
softcap_limit = 50.0


def nn_dot(left, right):
    return lax.dot_general(
        left, right, (((1,), (0,)), ((), ())), preferred_element_type=jnp.float32
    )


def nt_dot(left, right):
    return lax.dot_general(
        left, right, (((1,), (1,)), ((), ())), preferred_element_type=jnp.float32
    )


def tn_dot(left, right):
    return lax.dot_general(
        left, right, (((0,), (0,)), ((), ())), preferred_element_type=jnp.float32
    )


def small_cost():
    return pl.CostEstimate(flops=1000000, bytes_accessed=100000, transcendentals=0)


def norm_kernel(targets, input_ref, gain_ref, inverse_ref, *rest):
    piece_refs, turned = rest[:-1], rest[-1]
    rows, width = input_ref.shape
    values = input_ref[...].astype(jnp.float32)
    inverse = lax.rsqrt(jnp.mean(values * values, axis=-1, keepdims=True) + epsilon)
    inverse_ref[...] = inverse
    gain = gain_ref[...].reshape(1, width)
    turned[...] = (values * inverse * (1.0 + gain)).astype(jnp.bfloat16).T
    depth = width // len(piece_refs)
    for target, piece_ref in zip(targets(), piece_refs):
        start = pl.multiple_of(target * depth, 16)
        piece_ref[...] = turned[pl.ds(start, depth), :]


def normalize(layer_input, norm_gain, targets, pieces, block):
    rows, width = layer_input.shape
    depth = width // pieces
    out = pl.pallas_call(
        functools.partial(norm_kernel, targets),
        out_shape=(jax.ShapeDtypeStruct((rows, 1), jnp.float32),)
        + (jax.ShapeDtypeStruct((depth, rows), jnp.bfloat16),) * pieces,
        grid=(rows // block,),
        in_specs=[
            pl.BlockSpec((block, width), lambda i: (i, 0)),
            pl.BlockSpec((width,), lambda i: (0,)),
        ],
        out_specs=(pl.BlockSpec((block, 1), lambda i: (i, 0)),)
        + (pl.BlockSpec((depth, block), lambda i: (0, i)),) * pieces,
        scratch_shapes=[pltpu.VMEM((width, block), jnp.bfloat16)],
        compiler_params=pltpu.CompilerParams(vmem_limit_bytes=VMEM_LIMIT),
        cost_estimate=small_cost(),
        name="norm",
    )(layer_input, norm_gain)
    return out[0], out[1:]


def ancestor_mask(parent_row):
    rows = parent_row.shape[1]
    row = lax.broadcasted_iota(jnp.int32, (rows, rows), 0)
    column = lax.broadcasted_iota(jnp.int32, (rows, rows), 1)
    reached = jnp.where((parent_row == row) | (row == column), 1.0, 0.0)
    for squaring in range(rows.bit_length() - 1):
        halfway = reached.astype(jnp.bfloat16)
        reached = jnp.minimum(nn_dot(halfway, halfway), 1.0)
    return reached.T


def attention_kernel(
    slots,
    group,
    kv_local,
    order,
    blocks,
    ready,
    columns,
    shares,
    count_ref,
    parent_ref,
    inverse_ref,
    gain_ref,
    input_hbm,
    query_hbm,
    key_hbm,
    value_hbm,
    grad_hbm,
    *rest,
):
    delta_hbm, rest = rest[: len(shares)], rest[len(shares) :]
    part_hbm, rest = rest[:ready], rest[ready:]
    turned_hbm, centre_out, rest = rest[:3], rest[3], rest[4:]
    column_hbm, column_gain_ref, rest = rest[0], rest[1], rest[2:]
    (
        input_ref,
        gain_row,
        query_ref,
        key_ref,
        value_ref,
        grad_ref,
        sum_ref,
        delta_ref,
        query_turned,
        key_turned,
        value_turned,
        allowed_ref,
        centre_ref,
        kept,
        load_sem,
        weight_sem,
        store_sem,
        part_sem,
    ) = rest
    head_dim = HEAD_DIM
    rows, width = input_ref.shape
    block = rows // slots
    mid = group * head_dim
    steps = weight_sem.shape[0]
    chunk = width // steps
    weights = ((query_hbm, query_ref, mid, 0), (key_hbm, key_ref, head_dim, mid))
    weights += ((value_hbm, value_ref, head_dim, mid + head_dim),)

    def fetch(step, which):
        lines = pl.ds(pl.multiple_of(step * chunk, chunk), chunk)
        source, kept_ref = weights[which][:2]
        return pltpu.make_async_copy(
            source.at[lines, :], kept_ref.at[lines, :], weight_sem.at[step, which]
        )

    input_load = pltpu.make_async_copy(input_hbm, input_ref, load_sem.at[0])
    grad_load = pltpu.make_async_copy(grad_hbm, grad_ref, load_sem.at[1])
    input_load.start()
    for step in range(steps):
        for which in range(3):
            fetch(step, which).start()
    grad_load.start()
    gain_row[...] = gain_ref[...].reshape(1, width)

    first_count = lax.axis_index("branch") * slots
    parents = parent_ref[...].reshape(1, rows)
    for slot in range(slots):
        allowed_ref[slot] = ancestor_mask(parents[:, slot * block : (slot + 1) * block])
    sum_ref[...] = jnp.zeros_like(sum_ref)
    inverse = inverse_ref[...]
    input_load.wait()
    stores = []
    if columns:
        start = pl.multiple_of(lax.axis_index("tensor") * columns, 128)
        stores.append(
            pltpu.make_async_copy(
                input_ref.at[:, pl.ds(start, columns)], column_hbm, store_sem.at[0]
            )
        )
        stores[0].start()
        column_gain_ref[...] = gain_row[:, pl.ds(start, columns)]
    else:
        column_gain_ref[...] = jnp.zeros_like(column_gain_ref)

    def project(step, carry):
        lines = pl.ds(pl.multiple_of(step * chunk, chunk), chunk)
        gain = 1.0 + gain_row[:, lines]
        normed = (input_ref[:, lines].astype(jnp.float32) * inverse * gain).astype(jnp.bfloat16)
        for which, (_, kept_ref, wide, place) in enumerate(weights):
            fetch(step, which).wait()
            term = nn_dot(normed, kept_ref[lines, :])
            for h in range(kv_local):
                sum_ref[h, :, place : place + wide] += term[:, h * wide : (h + 1) * wide]
        return carry

    lax.fori_loop(0, steps, project, 0)
    grad_load.wait()
    scale = head_dim ** (-0.5)
    centre_ref[...] = jnp.zeros_like(centre_ref)

    def attend(h, carry):
        for slot in range(slots):
            lines = slice(slot * block, (slot + 1) * block)
            live = (
                lax.broadcasted_iota(jnp.int32, (block, mid), 0) < count_ref[first_count + slot]
            )
            columns = pl.ds(pl.multiple_of(h * mid, mid), mid)
            grad_rows = jnp.where(live, grad_ref[lines, columns].astype(jnp.float32), 0.0)
            pair = [slice(g * head_dim, (g + 1) * head_dim) for g in range(group)]
            grads = jnp.concatenate([grad_rows[:, p] for p in pair], axis=0).astype(jnp.bfloat16)
            queries = jnp.concatenate([sum_ref[h, lines, p] for p in pair], axis=0)
            queries = queries.astype(jnp.bfloat16)
            keys = sum_ref[h, lines, mid : mid + head_dim].astype(jnp.bfloat16)
            values = sum_ref[h, lines, mid + head_dim :].astype(jnp.bfloat16)
            allowed = jnp.concatenate([allowed_ref[slot]] * group, axis=0)
            bounded = jnp.tanh(nt_dot(queries, keys) * (scale / softcap_limit))
            weighted = allowed * jnp.exp(softcap_limit * bounded)
            probabilities = weighted * (1.0 / jnp.sum(weighted, axis=-1, keepdims=True))
            d_probs = nt_dot(grads, values)
            d_scores = probabilities * (
                d_probs - jnp.sum(probabilities * d_probs, axis=-1, keepdims=True)
            )
            d_raw = (d_scores * (1.0 - bounded * bounded) * scale).astype(jnp.bfloat16)
            prob_half = probabilities.astype(jnp.bfloat16)
            d_query = nn_dot(d_raw, keys)
            d_key = tn_dot(d_raw, queries)
            d_value = tn_dot(prob_half, grads)
            places = [
                (d_query[g * block : (g + 1) * block], query_turned, h * mid + g * head_dim)
                for g in range(group)
            ]
            places += [(d_key, key_turned, h * head_dim), (d_value, value_turned, h * head_dim)]
            product = None
            for which, (part, turned_ref, start) in enumerate(places):
                half = part.astype(jnp.bfloat16)
                line = which * rows + slot * block
                delta_ref[h, line : line + block, :] = half
                spot = pl.ds(pl.multiple_of(start, head_dim), head_dim)
                turned_ref[spot, lines] = half.T
                term = half.astype(jnp.float32) * sum_ref[
                    h, lines, which * head_dim : (which + 1) * head_dim
                ]
                product = term if product is None else product + term
            centre_ref[lines, :] += jnp.sum(product, axis=-1, keepdims=True)
        return carry

    lax.fori_loop(0, kv_local, attend, 0)
    lasts = []
    for share, out in zip(shares, delta_hbm):
        for place, block_index in enumerate(share):
            h, which = divmod(block_index, group + 2)
            lasts.append(
                pltpu.make_async_copy(
                    delta_ref.at[h, pl.ds(which * rows, rows), :],
                    out.at[pl.ds(place * rows, rows), :],
                    store_sem.at[1 + len(lasts)],
                )
            )
    for which, turned_ref in enumerate((query_turned, key_turned, value_turned)):
        lasts.append(
            pltpu.make_async_copy(turned_ref, turned_hbm[which], store_sem.at[1 + len(lasts)])
        )
    for store in lasts:
        store.start()

    centre = jnp.broadcast_to(centre_ref[...], (rows, 128)).T[:CENTRE_ROWS].astype(jnp.bfloat16)
    centre_out[...] = centre
    span = width // blocks
    cuts = 2
    cut_lines = span // cuts
    parts = [
        pltpu.make_async_copy(kept.at[place], part_hbm[place], part_sem.at[place])
        for place in range(ready)
    ]

    def project_back(step, carry):
        place, cut = step // cuts, lax.rem(step, cuts)
        lines = pl.ds(pl.multiple_of(order(place) * span + cut * cut_lines, 16), cut_lines)
        total = nn_dot(query_ref[lines, :], query_turned[...])
        total += nn_dot(key_ref[lines, :], key_turned[...])
        total += nn_dot(value_ref[lines, :], value_turned[...])
        spot = pl.ds(pl.multiple_of(cut * cut_lines, 16), cut_lines)
        kept[place, spot, :] = total.astype(jnp.bfloat16)
        for which, part in enumerate(parts):

            @pl.when((place == which) & (cut == cuts - 1))
            def _():
                kept[which, span:, :] = centre
                part.start()

        return carry

    lax.fori_loop(0, ready * cuts, project_back, 0)
    for store in stores + lasts + parts:
        store.wait()


def attention_backward(
    layer_input,
    inverse,
    norm_gain,
    w_query,
    w_key,
    w_value,
    head_grad,
    parents,
    counts,
    slots,
    order,
    blocks,
    ready,
    shares,
):
    rows, width = layer_input.shape
    kv_local = w_key.shape[1] // HEAD_DIM
    group = w_query.shape[1] // w_key.shape[1]
    span = (group + 2) * HEAD_DIM
    stack = (group + 2) * rows
    column_width = width // blocks
    cut = column_width % 128 == 0
    wide = column_width if cut else 128
    steps = 2 if width % 512 == 0 else 1
    part_shape = (column_width + CENTRE_ROWS, rows)
    hbm = pl.BlockSpec(memory_space=pl.ANY)
    vmem = pl.BlockSpec(memory_space=pltpu.VMEM)
    half = lambda *shape: jax.ShapeDtypeStruct(shape, jnp.bfloat16)
    out = pl.pallas_call(
        functools.partial(
            attention_kernel,
            slots,
            group,
            kv_local,
            order,
            blocks,
            ready,
            wide if cut else 0,
            shares,
        ),
        out_shape=tuple(half(len(share) * rows, HEAD_DIM) for share in shares)
        + (half(*part_shape),) * ready
        + tuple(half(w.shape[1], rows) for w in (w_query, w_key, w_value))
        + (half(CENTRE_ROWS, rows),)
        + (half(rows, wide), jax.ShapeDtypeStruct((1, wide), jnp.float32)),
        in_specs=[pl.BlockSpec(memory_space=pltpu.SMEM), vmem, vmem, vmem] + [hbm] * 5,
        out_specs=(hbm,) * (len(shares) + ready + 3) + (vmem, hbm, vmem),
        scratch_shapes=[
            pltpu.VMEM((rows, width), jnp.bfloat16),
            pltpu.VMEM((1, width), jnp.float32),
            pltpu.VMEM(w_query.shape, jnp.bfloat16),
            pltpu.VMEM(w_key.shape, jnp.bfloat16),
            pltpu.VMEM(w_value.shape, jnp.bfloat16),
            pltpu.VMEM(head_grad.shape, jnp.bfloat16),
            pltpu.VMEM((kv_local, rows, span), jnp.float32),
            pltpu.VMEM((kv_local, stack, HEAD_DIM), jnp.bfloat16),
            pltpu.VMEM((w_query.shape[1], rows), jnp.bfloat16),
            pltpu.VMEM((w_key.shape[1], rows), jnp.bfloat16),
            pltpu.VMEM((w_value.shape[1], rows), jnp.bfloat16),
            pltpu.VMEM((slots, rows // slots, rows // slots), jnp.float32),
            pltpu.VMEM((rows, 1), jnp.float32),
            pltpu.VMEM((ready, *part_shape), jnp.bfloat16),
            pltpu.SemaphoreType.DMA((2,)),
            pltpu.SemaphoreType.DMA((steps, 3)),
            pltpu.SemaphoreType.DMA((4 + kv_local * (group + 2),)),
            pltpu.SemaphoreType.DMA((ready,)),
        ],
        compiler_params=pltpu.CompilerParams(vmem_limit_bytes=VMEM_LIMIT),
        cost_estimate=small_cost(),
        name="attention",
    )(counts, parents, inverse, norm_gain, layer_input, w_query, w_key, w_value, head_grad)
    deltas, out = out[: len(shares)], out[len(shares) :]
    parts, turned, centre = out[:ready], out[ready : ready + 3], out[ready + 3]
    if cut:
        input_cut, gain_cut = out[-2], out[-1]
    else:
        start = lax.axis_index("tensor") * column_width
        input_cut = lax.dynamic_slice_in_dim(layer_input, start, column_width, 1)
        gain_cut = lax.dynamic_slice_in_dim(norm_gain, start, column_width, 0)
        gain_cut = gain_cut.reshape(1, column_width)
    return deltas, parts, turned, centre, input_cut, gain_cut


def back_kernel(centre_ref, *refs):
    turned_refs, weight_refs, out_refs = refs[:3], refs[3:6], refs[6:]
    piece, cut = pl.program_id(0), pl.program_id(1)
    lines = weight_refs[0].shape[0]
    total = None
    for weight_ref, turned_ref in zip(weight_refs, turned_refs):
        term = nn_dot(weight_ref[...], turned_ref[...])
        total = term if total is None else total + term
    total = total.astype(jnp.bfloat16)
    start = pl.multiple_of(cut * lines, 16)
    depth = out_refs[0].shape[0] - CENTRE_ROWS
    for place, out_ref in enumerate(out_refs):

        @pl.when(piece == place)
        def _():
            out_ref[pl.ds(start, lines), :] = total
            out_ref[depth:, :] = centre_ref[...]


def back_project(order, first, pieces, turned, centre, weights, blocks):
    rows = centre.shape[1]
    depth = weights[0].shape[0] // blocks
    cuts = 2
    whole = lambda i, j: (0, 0)
    return pl.pallas_call(
        back_kernel,
        out_shape=(jax.ShapeDtypeStruct((depth + CENTRE_ROWS, rows), jnp.bfloat16),) * pieces,
        grid=(pieces, cuts),
        in_specs=[pl.BlockSpec(x.shape, whole) for x in (centre, *turned)]
        + [
            pl.BlockSpec((depth // cuts, w.shape[1]), lambda i, j: (order(first + i) * cuts + j, 0))
            for w in weights
        ],
        out_specs=(pl.BlockSpec((depth + CENTRE_ROWS, rows), whole),) * pieces,
        compiler_params=pltpu.CompilerParams(vmem_limit_bytes=VMEM_LIMIT),
        cost_estimate=small_cost(),
        name="back",
    )(centre, *turned, *weights)


def weight_kernel(outs, sources, *refs):
    turned_hbm, delta_hbm = refs[:sources], refs[sources : 2 * sources]
    out_hbm, token_ref = refs[-10:-7], refs[-7]
    turned_ref, delta_ref, kept, turned_sem, delta_sem, store_sem = refs[-6:]
    token_ref[...] = jnp.zeros_like(token_ref)
    rows = turned_ref.shape[2]
    loads = []
    for place in range(sources):
        loads.append(
            pltpu.make_async_copy(
                turned_hbm[place], turned_ref.at[place], turned_sem.at[place]
            )
        )
        loads.append(
            pltpu.make_async_copy(delta_hbm[place], delta_ref.at[place], delta_sem.at[place])
        )
    for load in loads:
        load.start()
    for load in loads:
        load.wait()
    stores = [
        pltpu.make_async_copy(
            kept.at[block],
            out_hbm[which].at[:, pl.ds(column * HEAD_DIM, HEAD_DIM)],
            store_sem.at[block],
        )
        for block, (which, column) in enumerate(outs)
    ]

    def fill(block, carry):
        lines = pl.ds(pl.multiple_of(block * rows, rows), rows)
        total = None
        for place in range(sources):
            term = nn_dot(turned_ref[place], delta_ref[place, lines, :])
            total = term if total is None else total + term
        kept[block] = total
        for which, store in enumerate(stores):

            @pl.when(block == which)
            def _():
                store.start()

        return carry

    lax.fori_loop(0, len(outs), fill, 0)
    for store in stores:
        store.wait()


def weight_gradients(turned, deltas, share, kv_local, group, before):
    depth, rows = turned[0].shape
    sources = len(turned)
    outs = []
    for block in share:
        h, which = divmod(block, group + 2)
        outs.append((0, h * group + which) if which < group else (which - group + 1, h))
    kept = list(before) if before is not None else []
    hbm = pl.BlockSpec(memory_space=pl.ANY)
    return pl.pallas_call(
        functools.partial(weight_kernel, outs, sources),
        out_shape=(
            jax.ShapeDtypeStruct((depth, kv_local * group * HEAD_DIM), jnp.float32),
            jax.ShapeDtypeStruct((depth, kv_local * HEAD_DIM), jnp.float32),
            jax.ShapeDtypeStruct((depth, kv_local * HEAD_DIM), jnp.float32),
            jax.ShapeDtypeStruct((8, 128), jnp.float32),
        ),
        in_specs=[hbm] * (2 * sources + len(kept)),
        out_specs=(hbm,) * 3 + (pl.BlockSpec(memory_space=pltpu.VMEM),),
        input_output_aliases={2 * sources + i: i for i in range(len(kept))},
        scratch_shapes=[
            pltpu.VMEM((sources, depth, rows), jnp.bfloat16),
            pltpu.VMEM((sources, len(share) * rows, HEAD_DIM), jnp.bfloat16),
            pltpu.VMEM((len(share), depth, HEAD_DIM), jnp.float32),
            pltpu.SemaphoreType.DMA((sources,)),
            pltpu.SemaphoreType.DMA((sources,)),
            pltpu.SemaphoreType.DMA((len(share),)),
        ],
        compiler_params=pltpu.CompilerParams(vmem_limit_bytes=VMEM_LIMIT),
        cost_estimate=small_cost(),
        name="weights",
    )(*turned, *deltas, *kept)


def gate_kernel(*refs):
    del refs


def gate(arrays, tokens):
    hbm = pl.BlockSpec(memory_space=pl.ANY)
    return pl.pallas_call(
        gate_kernel,
        out_shape=tuple(jax.ShapeDtypeStruct(x.shape, x.dtype) for x in arrays),
        in_specs=[hbm] * (len(arrays) + len(tokens)),
        out_specs=(hbm,) * len(arrays),
        input_output_aliases={i: i for i in range(len(arrays))},
        compiler_params=pltpu.CompilerParams(vmem_limit_bytes=VMEM_LIMIT),
        cost_estimate=small_cost(),
        name="gate",
    )(*arrays, *tokens)


def join_kernel(inner_ref, other_ref, end_ref, *rest):
    out_ref, token_ref = rest[-2:]
    token_ref[...] = jnp.zeros_like(token_ref)
    index = lax.axis_index("tensor")
    inner = (index > 0) & (index < lax.axis_size("tensor") - 1)

    @pl.when(inner)
    def _():
        out_ref[...] = (
            inner_ref[...].astype(jnp.float32) + other_ref[...].astype(jnp.float32)
        ).astype(jnp.bfloat16)

    @pl.when(jnp.logical_not(inner))
    def _():
        out_ref[...] = end_ref[...]


def join(inner_part, other, end_part, tokens):
    vmem = pl.BlockSpec(memory_space=pltpu.VMEM)
    return pl.pallas_call(
        join_kernel,
        out_shape=(
            jax.ShapeDtypeStruct(end_part.shape, end_part.dtype),
            jax.ShapeDtypeStruct((8, 128), jnp.float32),
        ),
        in_specs=[vmem] * 3 + [pl.BlockSpec(memory_space=pl.ANY)] * len(tokens),
        out_specs=(vmem, vmem),
        compiler_params=pltpu.CompilerParams(vmem_limit_bytes=VMEM_LIMIT),
        cost_estimate=small_cost(),
        name="join",
    )(inner_part, other, end_part, *tokens)


def add_parts(for_ends, for_inner, part_refs):
    index = lax.axis_index("tensor")
    ends = ((index == 0) | (index == lax.axis_size("tensor") - 1)).astype(jnp.float32)
    total = None
    for place, part_ref in enumerate(part_refs):
        part = part_ref[...].astype(jnp.float32)
        if place < for_ends:
            part = part * ends
        elif place < for_ends + for_inner:
            part = part * (1.0 - ends)
        total = part if total is None else total + part
    return total


def gain_kernel(add, count, input_ref, inverse_ref, *refs):
    part_refs, (sum_ref, total_ref) = refs[:count], refs[-2:]

    @pl.when(pl.program_id(0) == 0)
    def _():
        sum_ref[...] = jnp.zeros_like(sum_ref)

    d_normed = add(part_refs).T
    total_ref[...] = d_normed
    scaled = input_ref[...].astype(jnp.float32) * inverse_ref[...]
    sum_ref[...] += jnp.sum(d_normed * scaled, axis=0, keepdims=True)


def gain_sums(add, input_columns, inverse, parts, token):
    rows, wide = input_columns.shape
    some = 128
    return pl.pallas_call(
        functools.partial(gain_kernel, add, len(parts)),
        out_shape=(
            jax.ShapeDtypeStruct((1, wide), jnp.float32),
            jax.ShapeDtypeStruct((rows, wide), jnp.float32),
        ),
        grid=(rows // some,),
        in_specs=[
            pl.BlockSpec((some, wide), lambda i: (i, 0)),
            pl.BlockSpec((some, 1), lambda i: (i, 0)),
        ]
        + [pl.BlockSpec((wide, some), lambda i: (0, i))] * len(parts)
        + [pl.BlockSpec(memory_space=pl.ANY)],
        out_specs=(
            pl.BlockSpec((1, wide), lambda i: (0, 0)),
            pl.BlockSpec((some, wide), lambda i: (i, 0)),
        ),
        compiler_params=pltpu.CompilerParams(vmem_limit_bytes=VMEM_LIMIT),
        cost_estimate=small_cost(),
        name="gains",
    )(input_columns, inverse, *parts, token)


def finish_kernel(width, add, total_ref, input_ref, gain_ref, inverse_ref, *refs):
    centre_refs, out_ref = refs[:-1], refs[-1]
    centre = add(centre_refs).T[:, :1] * (1.0 / width)
    inverse = inverse_ref[...]
    scaled = input_ref[...].astype(jnp.float32) * inverse
    out_ref[...] = (
        inverse * ((1.0 + gain_ref[...]) * total_ref[...] - scaled * centre)
    ).astype(jnp.bfloat16)


def finish(width, add, total, input_columns, gain_columns, inverse, parts):
    rows, wide = input_columns.shape
    some = 128
    row_block = pl.BlockSpec((some, wide), lambda i: (i, 0))
    return pl.pallas_call(
        functools.partial(finish_kernel, width, add),
        out_shape=jax.ShapeDtypeStruct((rows, wide), jnp.bfloat16),
        grid=(rows // some,),
        in_specs=[
            row_block,
            row_block,
            pl.BlockSpec((1, wide), lambda i: (0, 0)),
            pl.BlockSpec((some, 1), lambda i: (i, 0)),
        ]
        + [pl.BlockSpec((CENTRE_ROWS, some), lambda i: (wide // CENTRE_ROWS, i))] * len(parts),
        out_specs=row_block,
        compiler_params=pltpu.CompilerParams(vmem_limit_bytes=VMEM_LIMIT),
        cost_estimate=small_cost(),
        name="finish",
    )(total, input_columns, gain_columns, inverse, *parts)


def total_kernel(*refs):
    total = (refs[0][...] + refs[1][...]) + (refs[2][...] + refs[3][...])
    refs[-1][...] = total.reshape(refs[-1].shape)


def total_of_four(arrays, token):
    whole = pl.BlockSpec(arrays[0].shape, lambda i: (0, 0))
    wide = arrays[0].shape[1]
    return pl.pallas_call(
        total_kernel,
        out_shape=jax.ShapeDtypeStruct((wide,), arrays[0].dtype),
        grid=(1,),
        in_specs=[whole] * 4 + [pl.BlockSpec(memory_space=pl.ANY)],
        out_specs=pl.BlockSpec((wide,), lambda i: (0,)),
        compiler_params=pltpu.CompilerParams(vmem_limit_bytes=VMEM_LIMIT),
        cost_estimate=small_cost(),
        name="total",
    )(*arrays, token)


def branch_send(array, chips, shift, swap):
    pairs = [
        (c * 2 + k, ((c + shift) % chips) * 2 + (k ^ swap)) for c in range(chips) for k in range(2)
    ]
    return lax.ppermute(array, "branch", pairs)


def pick(table, index):
    chosen = table[-1]
    for place in range(len(table) - 2, -1, -1):
        chosen = jnp.where(index == place, table[place], chosen)
    return chosen


def scatter_order(total):
    index = lax.axis_index("tensor")
    if total != 4:
        return lambda place: lax.rem(index + place + 1, total)
    table = [[3, 0, 3, 0], [0, 2, 1, 3], [2, 3, 0, 1], [1, 1, 2, 2]]
    here = [pick(row, index) for row in table]
    return lambda place: pick(here, place)


def scatter_begin(parts, total):
    if total != 4:
        return [
            lax.ppermute(part, "tensor", [(t, (t + shift) % total) for t in range(total)])
            for shift, part in zip(range(1, total), parts[:-1])
        ]
    from_first = lax.ppermute(parts[0], "tensor", [(0, 1), (1, 0), (2, 3), (3, 2)])
    from_inner = lax.ppermute(parts[1], "tensor", [(1, 2), (2, 1)])
    return from_first, from_inner


def scatter_middle(parts, arrived, total):
    if total != 4:
        return arrived, None, arrived[0]
    (held,) = gate((parts[2],), (arrived[0],))
    from_ends = lax.ppermute(held, "tensor", [(0, 2), (3, 1)])
    joined, token = join(held, arrived[0], parts[3], (arrived[1],))
    return (*arrived, from_ends), joined, token


def scatter_end(parts, arrived, joined, total, token):
    if total != 4:
        return [parts[-1], *arrived], 0, 0
    from_first, from_inner, from_ends = arrived
    (joined,) = gate((joined,), (from_ends, token))
    from_joined = lax.ppermute(joined, "tensor", [(1, 3), (2, 0), (0, 1), (3, 2)])
    return [from_first, parts[1], parts[3], from_inner, from_ends, from_joined], 2, 1


def local(layer_input, norm_gain, w_query, w_key, w_value, head_grad, parents, row_counts):
    branch_total = lax.axis_size("branch")
    tensor_total = lax.axis_size("tensor")
    slots = row_counts.shape[0] // branch_total
    rows, width = layer_input.shape
    column_width = width // tensor_total
    chips = branch_total // 2
    group = w_query.shape[1] // w_key.shape[1]
    kv_local = w_key.shape[1] // HEAD_DIM
    offsets = [(shift, swap) for shift in range(chips) for swap in range(2)]
    blocks = list(range(kv_local * (group + 2)))
    early = blocks[: group + 2] + [h * (group + 2) + group for h in range(1, kv_local)]
    shares = [early, [block for block in blocks if block not in early]]
    shares = [share for share in shares if share]

    def targets():
        index = lax.axis_index("branch")
        chip, core = index // 2, index % 2
        return [lax.rem(chip + s, chips) * 2 + lax.rem(core + e, 2) for s, e in offsets]

    inverse, pieces = normalize(layer_input, norm_gain, targets, branch_total, rows // slots)
    shared = [branch_send(piece, chips, s, e) for piece, (s, e) in zip(pieces[1:], offsets[1:])]
    order = lambda place: scatter_order(tensor_total)(place)
    ready = min(2, tensor_total)
    deltas, parts, delta_turned, centre, input_columns, gain_columns = attention_backward(
        layer_input,
        inverse,
        norm_gain,
        w_query,
        w_key,
        w_value,
        head_grad,
        parents,
        row_counts,
        slots,
        order,
        tensor_total,
        ready,
        shares,
    )
    if ready < tensor_total:
        weights = (w_query, w_key, w_value)
        parts += back_project(
            order, ready, tensor_total - ready, delta_turned, centre, weights, tensor_total
        )
    arrived = scatter_begin(parts, tensor_total)

    (first,) = gate(deltas[:1], shared)
    sent = [branch_send(first, chips, s, 0) for s in range(1, chips)]
    arrived, joined, met = scatter_middle(parts, arrived, tensor_total)
    *sent, first = gate((*sent, first), (met,))
    others = gate(deltas[1:], (sent[0],)) if deltas[1:] else ()
    turned = [pieces[0]] + shared
    weights, token = None, None
    for share, delta in zip(shares, (first, *others)):
        if token is not None:
            sent = [branch_send(delta, chips, s, 0) for s in range(1, chips)]
            delta, *sent = gate((delta, *sent), (token,))
        gathered = []
        for part in [delta] + sent:
            gathered += [part, branch_send(part, chips, 0, 1)]
        first_share = weights is None
        *weights, token = weight_gradients(turned, gathered, share, kv_local, group, weights)
        if first_share:
            parts, for_ends, for_inner = scatter_end(parts, arrived, joined, tensor_total, token)

    add = functools.partial(add_parts, for_ends, for_inner)
    gain_sum, total = gain_sums(add, input_columns, inverse, parts, token)
    grad_input = finish(width, add, total, input_columns, gain_columns, inverse, parts)
    if chips == 2:
        sums = [gain_sum] + [branch_send(gain_sum, chips, s, e) for s, e in offsets[1:]]
        grad_gain = total_of_four(sums, grad_input)
    else:
        grad_gain = lax.psum(gain_sum, "branch").reshape(column_width)
    return (grad_input, *weights, grad_gain)


def solution(mesh):
    placed = (
        P(("parts", "branch"), None),
        P(),
        P(None, "tensor"),
        P(None, "tensor"),
        P(None, "tensor"),
        P(("parts", "branch"), "tensor"),
        P(("parts", "branch")),
        P("parts"),
    )
    return jax.shard_map(
        local,
        mesh=mesh,
        in_specs=placed,
        out_specs=(
            P(("parts", "branch"), "tensor"),
            P(("parts", "branch"), "tensor"),
            P(("parts", "branch"), "tensor"),
            P(("parts", "branch"), "tensor"),
            P(("parts", "tensor")),
        ),
        check_vma=False,
    )
```

```python
import functools

import jax
import jax.numpy as jnp
from jax import lax
from jax.experimental import pallas as pl
from jax.experimental.pallas import tpu as pltpu
from jax.sharding import PartitionSpec as P

HEAD_DIM = 256
MIB = 1024 * 1024
CENTRE_ROWS = 16
VMEM_LIMIT = 64 * MIB


epsilon = 1e-06
softcap_limit = 50.0


def nn_dot(left, right):
    return lax.dot_general(
        left, right, (((1,), (0,)), ((), ())), preferred_element_type=jnp.float32
    )


def nt_dot(left, right):
    return lax.dot_general(
        left, right, (((1,), (1,)), ((), ())), preferred_element_type=jnp.float32
    )


def tn_dot(left, right):
    return lax.dot_general(
        left, right, (((0,), (0,)), ((), ())), preferred_element_type=jnp.float32
    )


def small_cost():
    return pl.CostEstimate(flops=1000000, bytes_accessed=100000, transcendentals=0)


def norm_kernel(targets, input_ref, gain_ref, inverse_ref, *rest):
    piece_refs, turned = rest[:-1], rest[-1]
    rows, width = input_ref.shape
    values = input_ref[...].astype(jnp.float32)
    inverse = lax.rsqrt(jnp.mean(values * values, axis=-1, keepdims=True) + epsilon)
    inverse_ref[...] = inverse
    gain = gain_ref[...].reshape(1, width)
    turned[...] = (values * inverse * (1.0 + gain)).astype(jnp.bfloat16).T
    depth = width // len(piece_refs)
    for target, piece_ref in zip(targets(), piece_refs):
        start = pl.multiple_of(target * depth, 16)
        piece_ref[...] = turned[pl.ds(start, depth), :]


def normalize(layer_input, norm_gain, targets, pieces, block):
    rows, width = layer_input.shape
    depth = width // pieces
    out = pl.pallas_call(
        functools.partial(norm_kernel, targets),
        out_shape=(jax.ShapeDtypeStruct((rows, 1), jnp.float32),)
        + (jax.ShapeDtypeStruct((depth, rows), jnp.bfloat16),) * pieces,
        grid=(rows // block,),
        in_specs=[
            pl.BlockSpec((block, width), lambda i: (i, 0)),
            pl.BlockSpec((width,), lambda i: (0,)),
        ],
        out_specs=(pl.BlockSpec((block, 1), lambda i: (i, 0)),)
        + (pl.BlockSpec((depth, block), lambda i: (0, i)),) * pieces,
        scratch_shapes=[pltpu.VMEM((width, block), jnp.bfloat16)],
        compiler_params=pltpu.CompilerParams(vmem_limit_bytes=VMEM_LIMIT),
        cost_estimate=small_cost(),
        name="norm",
    )(layer_input, norm_gain)
    return out[0], out[1:]


def ancestor_mask(parent_row):
    rows = parent_row.shape[1]
    row = lax.broadcasted_iota(jnp.int32, (rows, rows), 0)
    column = lax.broadcasted_iota(jnp.int32, (rows, rows), 1)
    reached = jnp.where((parent_row == row) | (row == column), 1.0, 0.0)
    for squaring in range(rows.bit_length() - 1):
        halfway = reached.astype(jnp.bfloat16)
        reached = jnp.minimum(nn_dot(halfway, halfway), 1.0)
    return reached.T


def attention_kernel(
    slots,
    group,
    kv_local,
    order,
    blocks,
    ready,
    columns,
    shares,
    count_ref,
    parent_ref,
    inverse_ref,
    gain_ref,
    input_hbm,
    query_hbm,
    key_hbm,
    value_hbm,
    grad_hbm,
    *rest,
):
    delta_hbm, rest = rest[: len(shares)], rest[len(shares) :]
    part_hbm, rest = rest[:ready], rest[ready:]
    turned_hbm, centre_out, rest = rest[:3], rest[3], rest[4:]
    column_hbm, column_gain_ref, rest = rest[0], rest[1], rest[2:]
    (
        input_ref,
        gain_row,
        query_ref,
        key_ref,
        value_ref,
        grad_ref,
        sum_ref,
        delta_ref,
        query_turned,
        key_turned,
        value_turned,
        allowed_ref,
        centre_ref,
        kept,
        load_sem,
        weight_sem,
        store_sem,
        part_sem,
    ) = rest
    head_dim = HEAD_DIM
    rows, width = input_ref.shape
    block = rows // slots
    mid = group * head_dim
    steps = weight_sem.shape[0]
    chunk = width // steps
    weights = ((query_hbm, query_ref, mid, 0), (key_hbm, key_ref, head_dim, mid))
    weights += ((value_hbm, value_ref, head_dim, mid + head_dim),)

    def fetch(step, which):
        lines = pl.ds(pl.multiple_of(step * chunk, chunk), chunk)
        source, kept_ref = weights[which][:2]
        return pltpu.make_async_copy(
            source.at[lines, :], kept_ref.at[lines, :], weight_sem.at[step, which]
        )

    input_load = pltpu.make_async_copy(input_hbm, input_ref, load_sem.at[0])
    grad_load = pltpu.make_async_copy(grad_hbm, grad_ref, load_sem.at[1])
    input_load.start()
    for step in range(steps):
        for which in range(3):
            fetch(step, which).start()
    grad_load.start()
    gain_row[...] = gain_ref[...].reshape(1, width)

    first_count = lax.axis_index("branch") * slots
    parents = parent_ref[...].reshape(1, rows)
    for slot in range(slots):
        allowed_ref[slot] = ancestor_mask(parents[:, slot * block : (slot + 1) * block])
    sum_ref[...] = jnp.zeros_like(sum_ref)
    inverse = inverse_ref[...]
    input_load.wait()
    stores = []
    if columns:
        start = pl.multiple_of(lax.axis_index("tensor") * columns, 128)
        stores.append(
            pltpu.make_async_copy(
                input_ref.at[:, pl.ds(start, columns)], column_hbm, store_sem.at[0]
            )
        )
        stores[0].start()
        column_gain_ref[...] = gain_row[:, pl.ds(start, columns)]
    else:
        column_gain_ref[...] = jnp.zeros_like(column_gain_ref)

    def project(step, carry):
        lines = pl.ds(pl.multiple_of(step * chunk, chunk), chunk)
        gain = 1.0 + gain_row[:, lines]
        normed = (input_ref[:, lines].astype(jnp.float32) * inverse * gain).astype(jnp.bfloat16)
        for which, (_, kept_ref, wide, place) in enumerate(weights):
            fetch(step, which).wait()
            term = nn_dot(normed, kept_ref[lines, :])
            for h in range(kv_local):
                sum_ref[h, :, place : place + wide] += term[:, h * wide : (h + 1) * wide]
        return carry

    lax.fori_loop(0, steps, project, 0)
    grad_load.wait()
    scale = head_dim ** (-0.5)
    centre_ref[...] = jnp.zeros_like(centre_ref)

    def attend(h, carry):
        for slot in range(slots):
            lines = slice(slot * block, (slot + 1) * block)
            live = (
                lax.broadcasted_iota(jnp.int32, (block, mid), 0) < count_ref[first_count + slot]
            )
            columns = pl.ds(pl.multiple_of(h * mid, mid), mid)
            grad_rows = jnp.where(live, grad_ref[lines, columns].astype(jnp.float32), 0.0)
            pair = [slice(g * head_dim, (g + 1) * head_dim) for g in range(group)]
            grads = jnp.concatenate([grad_rows[:, p] for p in pair], axis=0).astype(jnp.bfloat16)
            queries = jnp.concatenate([sum_ref[h, lines, p] for p in pair], axis=0)
            queries = queries.astype(jnp.bfloat16)
            keys = sum_ref[h, lines, mid : mid + head_dim].astype(jnp.bfloat16)
            values = sum_ref[h, lines, mid + head_dim :].astype(jnp.bfloat16)
            allowed = jnp.concatenate([allowed_ref[slot]] * group, axis=0)
            bounded = jnp.tanh(nt_dot(queries, keys) * (scale / softcap_limit))
            weighted = allowed * jnp.exp(softcap_limit * bounded)
            probabilities = weighted * (1.0 / jnp.sum(weighted, axis=-1, keepdims=True))
            d_probs = nt_dot(grads, values)
            d_scores = probabilities * (
                d_probs - jnp.sum(probabilities * d_probs, axis=-1, keepdims=True)
            )
            d_raw = (d_scores * (1.0 - bounded * bounded) * scale).astype(jnp.bfloat16)
            prob_half = probabilities.astype(jnp.bfloat16)
            d_query = nn_dot(d_raw, keys)
            d_key = tn_dot(d_raw, queries)
            d_value = tn_dot(prob_half, grads)
            places = [
                (d_query[g * block : (g + 1) * block], query_turned, h * mid + g * head_dim)
                for g in range(group)
            ]
            places += [(d_key, key_turned, h * head_dim), (d_value, value_turned, h * head_dim)]
            product = None
            for which, (part, turned_ref, start) in enumerate(places):
                half = part.astype(jnp.bfloat16)
                line = which * rows + slot * block
                delta_ref[h, line : line + block, :] = half
                spot = pl.ds(pl.multiple_of(start, head_dim), head_dim)
                turned_ref[spot, lines] = half.T
                term = half.astype(jnp.float32) * sum_ref[
                    h, lines, which * head_dim : (which + 1) * head_dim
                ]
                product = term if product is None else product + term
            centre_ref[lines, :] += jnp.sum(product, axis=-1, keepdims=True)
        return carry

    lax.fori_loop(0, kv_local, attend, 0)
    lasts = []
    for share, out in zip(shares, delta_hbm):
        for place, block_index in enumerate(share):
            h, which = divmod(block_index, group + 2)
            lasts.append(
                pltpu.make_async_copy(
                    delta_ref.at[h, pl.ds(which * rows, rows), :],
                    out.at[pl.ds(place * rows, rows), :],
                    store_sem.at[1 + len(lasts)],
                )
            )
    for which, turned_ref in enumerate((query_turned, key_turned, value_turned)):
        lasts.append(
            pltpu.make_async_copy(turned_ref, turned_hbm[which], store_sem.at[1 + len(lasts)])
        )
    for store in lasts:
        store.start()

    centre = jnp.broadcast_to(centre_ref[...], (rows, 128)).T[:CENTRE_ROWS].astype(jnp.bfloat16)
    centre_out[...] = centre
    span = width // blocks
    cuts = 2
    cut_lines = span // cuts
    parts = [
        pltpu.make_async_copy(kept.at[place], part_hbm[place], part_sem.at[place])
        for place in range(ready)
    ]

    def project_back(step, carry):
        place, cut = step // cuts, lax.rem(step, cuts)
        lines = pl.ds(pl.multiple_of(order(place) * span + cut * cut_lines, 16), cut_lines)
        total = nn_dot(query_ref[lines, :], query_turned[...])
        total += nn_dot(key_ref[lines, :], key_turned[...])
        total += nn_dot(value_ref[lines, :], value_turned[...])
        spot = pl.ds(pl.multiple_of(cut * cut_lines, 16), cut_lines)
        kept[place, spot, :] = total.astype(jnp.bfloat16)
        for which, part in enumerate(parts):

            @pl.when((place == which) & (cut == cuts - 1))
            def _():
                kept[which, span:, :] = centre
                part.start()

        return carry

    lax.fori_loop(0, ready * cuts, project_back, 0)
    for store in stores + lasts + parts:
        store.wait()


def attention_backward(
    layer_input,
    inverse,
    norm_gain,
    w_query,
    w_key,
    w_value,
    head_grad,
    parents,
    counts,
    slots,
    order,
    blocks,
    ready,
    shares,
):
    rows, width = layer_input.shape
    kv_local = w_key.shape[1] // HEAD_DIM
    group = w_query.shape[1] // w_key.shape[1]
    span = (group + 2) * HEAD_DIM
    stack = (group + 2) * rows
    column_width = width // blocks
    cut = column_width % 128 == 0
    wide = column_width if cut else 128
    steps = 2 if width % 512 == 0 else 1
    part_shape = (column_width + CENTRE_ROWS, rows)
    hbm = pl.BlockSpec(memory_space=pl.ANY)
    vmem = pl.BlockSpec(memory_space=pltpu.VMEM)
    half = lambda *shape: jax.ShapeDtypeStruct(shape, jnp.bfloat16)
    out = pl.pallas_call(
        functools.partial(
            attention_kernel,
            slots,
            group,
            kv_local,
            order,
            blocks,
            ready,
            wide if cut else 0,
            shares,
        ),
        out_shape=tuple(half(len(share) * rows, HEAD_DIM) for share in shares)
        + (half(*part_shape),) * ready
        + tuple(half(w.shape[1], rows) for w in (w_query, w_key, w_value))
        + (half(CENTRE_ROWS, rows),)
        + (half(rows, wide), jax.ShapeDtypeStruct((1, wide), jnp.float32)),
        in_specs=[pl.BlockSpec(memory_space=pltpu.SMEM), vmem, vmem, vmem] + [hbm] * 5,
        out_specs=(hbm,) * (len(shares) + ready + 3) + (vmem, hbm, vmem),
        scratch_shapes=[
            pltpu.VMEM((rows, width), jnp.bfloat16),
            pltpu.VMEM((1, width), jnp.float32),
            pltpu.VMEM(w_query.shape, jnp.bfloat16),
            pltpu.VMEM(w_key.shape, jnp.bfloat16),
            pltpu.VMEM(w_value.shape, jnp.bfloat16),
            pltpu.VMEM(head_grad.shape, jnp.bfloat16),
            pltpu.VMEM((kv_local, rows, span), jnp.float32),
            pltpu.VMEM((kv_local, stack, HEAD_DIM), jnp.bfloat16),
            pltpu.VMEM((w_query.shape[1], rows), jnp.bfloat16),
            pltpu.VMEM((w_key.shape[1], rows), jnp.bfloat16),
            pltpu.VMEM((w_value.shape[1], rows), jnp.bfloat16),
            pltpu.VMEM((slots, rows // slots, rows // slots), jnp.float32),
            pltpu.VMEM((rows, 1), jnp.float32),
            pltpu.VMEM((ready, *part_shape), jnp.bfloat16),
            pltpu.SemaphoreType.DMA((2,)),
            pltpu.SemaphoreType.DMA((steps, 3)),
            pltpu.SemaphoreType.DMA((4 + kv_local * (group + 2),)),
            pltpu.SemaphoreType.DMA((ready,)),
        ],
        compiler_params=pltpu.CompilerParams(vmem_limit_bytes=VMEM_LIMIT),
        cost_estimate=small_cost(),
        name="attention",
    )(counts, parents, inverse, norm_gain, layer_input, w_query, w_key, w_value, head_grad)
    deltas, out = out[: len(shares)], out[len(shares) :]
    parts, turned, centre = out[:ready], out[ready : ready + 3], out[ready + 3]
    if cut:
        input_cut, gain_cut = out[-2], out[-1]
    else:
        start = lax.axis_index("tensor") * column_width
        input_cut = lax.dynamic_slice_in_dim(layer_input, start, column_width, 1)
        gain_cut = lax.dynamic_slice_in_dim(norm_gain, start, column_width, 0)
        gain_cut = gain_cut.reshape(1, column_width)
    return deltas, parts, turned, centre, input_cut, gain_cut


def back_kernel(centre_ref, *refs):
    turned_refs, weight_refs, out_refs = refs[:3], refs[3:6], refs[6:]
    piece, cut = pl.program_id(0), pl.program_id(1)
    lines = weight_refs[0].shape[0]
    total = None
    for weight_ref, turned_ref in zip(weight_refs, turned_refs):
        term = nn_dot(weight_ref[...], turned_ref[...])
        total = term if total is None else total + term
    total = total.astype(jnp.bfloat16)
    start = pl.multiple_of(cut * lines, 16)
    depth = out_refs[0].shape[0] - CENTRE_ROWS
    for place, out_ref in enumerate(out_refs):

        @pl.when(piece == place)
        def _():
            out_ref[pl.ds(start, lines), :] = total
            out_ref[depth:, :] = centre_ref[...]


def back_project(order, first, pieces, turned, centre, weights, blocks):
    rows = centre.shape[1]
    depth = weights[0].shape[0] // blocks
    cuts = 2
    whole = lambda i, j: (0, 0)
    return pl.pallas_call(
        back_kernel,
        out_shape=(jax.ShapeDtypeStruct((depth + CENTRE_ROWS, rows), jnp.bfloat16),) * pieces,
        grid=(pieces, cuts),
        in_specs=[pl.BlockSpec(x.shape, whole) for x in (centre, *turned)]
        + [
            pl.BlockSpec((depth // cuts, w.shape[1]), lambda i, j: (order(first + i) * cuts + j, 0))
            for w in weights
        ],
        out_specs=(pl.BlockSpec((depth + CENTRE_ROWS, rows), whole),) * pieces,
        compiler_params=pltpu.CompilerParams(vmem_limit_bytes=VMEM_LIMIT),
        cost_estimate=small_cost(),
        name="back",
    )(centre, *turned, *weights)


def weight_kernel(outs, owners, sources, *refs):
    turned_hbm, delta_hbm = refs[:sources], refs[sources]
    out_hbm, token_ref = refs[-10:-7], refs[-7]
    token_ref[...] = jnp.zeros_like(token_ref)
    turned_ref, delta_ref, kept, turned_sem, delta_sem, store_sem = refs[-6:]
    rows = turned_ref.shape[2]
    loads = []
    for place, owner in enumerate(owners()):
        loads.append(
            pltpu.make_async_copy(
                turned_hbm[place], turned_ref.at[place], turned_sem.at[place]
            )
        )
        loads.append(
            pltpu.make_async_copy(delta_hbm.at[owner], delta_ref.at[place], delta_sem.at[place])
        )
    for load in loads:
        load.start()
    for load in loads:
        load.wait()
    stores = [
        pltpu.make_async_copy(
            kept.at[block],
            out_hbm[which].at[:, pl.ds(column * HEAD_DIM, HEAD_DIM)],
            store_sem.at[block],
        )
        for block, (which, column) in enumerate(outs)
    ]

    def fill(block, carry):
        lines = pl.ds(pl.multiple_of(block * rows, rows), rows)
        total = None
        for place in range(sources):
            term = nn_dot(turned_ref[place], delta_ref[place, lines, :])
            total = term if total is None else total + term
        kept[block] = total
        for which, store in enumerate(stores):

            @pl.when(block == which)
            def _():
                store.start()

        return carry

    lax.fori_loop(0, len(outs), fill, 0)
    for store in stores:
        store.wait()


def weight_gradients(turned, gathered, owners, kv_local, group, tokens):
    depth, rows = turned[0].shape
    sources = len(turned)
    stack = gathered.shape[1]
    outs = []
    for block in range(kv_local * (group + 2)):
        h, which = divmod(block, group + 2)
        outs.append((0, h * group + which) if which < group else (which - group + 1, h))
    hbm = pl.BlockSpec(memory_space=pl.ANY)
    return pl.pallas_call(
        functools.partial(weight_kernel, outs, owners, sources),
        out_shape=(
            jax.ShapeDtypeStruct((depth, kv_local * group * HEAD_DIM), jnp.float32),
            jax.ShapeDtypeStruct((depth, kv_local * HEAD_DIM), jnp.float32),
            jax.ShapeDtypeStruct((depth, kv_local * HEAD_DIM), jnp.float32),
            jax.ShapeDtypeStruct((8, 128), jnp.float32),
        ),
        in_specs=[hbm] * (sources + 1 + len(tokens)),
        out_specs=(hbm,) * 3 + (pl.BlockSpec(memory_space=pltpu.VMEM),),
        scratch_shapes=[
            pltpu.VMEM((sources, depth, rows), jnp.bfloat16),
            pltpu.VMEM((sources, stack, HEAD_DIM), jnp.bfloat16),
            pltpu.VMEM((len(outs), depth, HEAD_DIM), jnp.float32),
            pltpu.SemaphoreType.DMA((sources,)),
            pltpu.SemaphoreType.DMA((sources,)),
            pltpu.SemaphoreType.DMA((len(outs),)),
        ],
        compiler_params=pltpu.CompilerParams(vmem_limit_bytes=VMEM_LIMIT),
        cost_estimate=pl.CostEstimate(
            flops=2 * sources * rows * depth * stack,
            bytes_accessed=4 * depth * stack + 2 * sources * rows * (depth + stack),
            transcendentals=0,
        ),
        name="weights",
    )(*turned, gathered, *tokens)


def gate_kernel(*refs):
    del refs


def gate(arrays, tokens):
    hbm = pl.BlockSpec(memory_space=pl.ANY)
    return pl.pallas_call(
        gate_kernel,
        out_shape=tuple(jax.ShapeDtypeStruct(x.shape, x.dtype) for x in arrays),
        in_specs=[hbm] * (len(arrays) + len(tokens)),
        out_specs=(hbm,) * len(arrays),
        input_output_aliases={i: i for i in range(len(arrays))},
        compiler_params=pltpu.CompilerParams(vmem_limit_bytes=VMEM_LIMIT),
        cost_estimate=small_cost(),
        name="gate",
    )(*arrays, *tokens)


def add_parts(part_refs):
    total = part_refs[0][...].astype(jnp.float32)
    for part_ref in part_refs[1:]:
        total += part_ref[...].astype(jnp.float32)
    return total


def gain_kernel(count, input_ref, inverse_ref, *refs):
    part_refs, (sum_ref, total_ref) = refs[:count], refs[-2:]

    @pl.when(pl.program_id(0) == 0)
    def _():
        sum_ref[...] = jnp.zeros_like(sum_ref)

    d_normed = add_parts(part_refs).T
    total_ref[...] = d_normed
    scaled = input_ref[...].astype(jnp.float32) * inverse_ref[...]
    sum_ref[...] += jnp.sum(d_normed * scaled, axis=0, keepdims=True)


def gain_sums(input_columns, inverse, parts, token):
    rows, wide = input_columns.shape
    some = 128
    return pl.pallas_call(
        functools.partial(gain_kernel, len(parts)),
        out_shape=(
            jax.ShapeDtypeStruct((1, wide), jnp.float32),
            jax.ShapeDtypeStruct((rows, wide), jnp.float32),
        ),
        grid=(rows // some,),
        in_specs=[
            pl.BlockSpec((some, wide), lambda i: (i, 0)),
            pl.BlockSpec((some, 1), lambda i: (i, 0)),
        ]
        + [pl.BlockSpec((wide, some), lambda i: (0, i))] * len(parts)
        + [pl.BlockSpec(memory_space=pl.ANY)],
        out_specs=(
            pl.BlockSpec((1, wide), lambda i: (0, 0)),
            pl.BlockSpec((some, wide), lambda i: (i, 0)),
        ),
        compiler_params=pltpu.CompilerParams(vmem_limit_bytes=VMEM_LIMIT),
        cost_estimate=small_cost(),
        name="gains",
    )(input_columns, inverse, *parts, token)


def finish_kernel(width, total_ref, input_ref, gain_ref, inverse_ref, *refs):
    centre_refs, out_ref = refs[:-1], refs[-1]
    centre = add_parts(centre_refs).T[:, :1] * (1.0 / width)
    inverse = inverse_ref[...]
    scaled = input_ref[...].astype(jnp.float32) * inverse
    out_ref[...] = (
        inverse * ((1.0 + gain_ref[...]) * total_ref[...] - scaled * centre)
    ).astype(jnp.bfloat16)


def finish(width, total, input_columns, gain_columns, inverse, parts):
    rows, wide = input_columns.shape
    some = 128
    row_block = pl.BlockSpec((some, wide), lambda i: (i, 0))
    return pl.pallas_call(
        functools.partial(finish_kernel, width),
        out_shape=jax.ShapeDtypeStruct((rows, wide), jnp.bfloat16),
        grid=(rows // some,),
        in_specs=[
            row_block,
            row_block,
            pl.BlockSpec((1, wide), lambda i: (0, 0)),
            pl.BlockSpec((some, 1), lambda i: (i, 0)),
        ]
        + [pl.BlockSpec((CENTRE_ROWS, some), lambda i: (wide // CENTRE_ROWS, i))] * len(parts),
        out_specs=row_block,
        compiler_params=pltpu.CompilerParams(vmem_limit_bytes=VMEM_LIMIT),
        cost_estimate=small_cost(),
        name="finish",
    )(total, input_columns, gain_columns, inverse, *parts)


def total_kernel(*refs):
    total = (refs[0][...] + refs[1][...]) + (refs[2][...] + refs[3][...])
    refs[-1][...] = total.reshape(refs[-1].shape)


def total_of_four(arrays, token):
    whole = pl.BlockSpec(arrays[0].shape, lambda i: (0, 0))
    wide = arrays[0].shape[1]
    return pl.pallas_call(
        total_kernel,
        out_shape=jax.ShapeDtypeStruct((wide,), arrays[0].dtype),
        grid=(1,),
        in_specs=[whole] * 4 + [pl.BlockSpec(memory_space=pl.ANY)],
        out_specs=pl.BlockSpec((wide,), lambda i: (0,)),
        compiler_params=pltpu.CompilerParams(vmem_limit_bytes=VMEM_LIMIT),
        cost_estimate=small_cost(),
        name="total",
    )(*arrays, token)


def branch_send(array, chips, shift, swap):
    pairs = [
        (c * 2 + k, ((c + shift) % chips) * 2 + (k ^ swap)) for c in range(chips) for k in range(2)
    ]
    return lax.ppermute(array, "branch", pairs)


def local(layer_input, norm_gain, w_query, w_key, w_value, head_grad, parents, row_counts):
    branch_total = lax.axis_size("branch")
    tensor_total = lax.axis_size("tensor")
    slots = row_counts.shape[0] // branch_total
    rows, width = layer_input.shape
    column_width = width // tensor_total
    chips = branch_total // 2
    group = w_query.shape[1] // w_key.shape[1]
    kv_local = w_key.shape[1] // HEAD_DIM
    offsets = [(shift, swap) for shift in range(chips) for swap in range(2)]
    shares = [list(range(kv_local * (group + 2)))]

    def targets():
        index = lax.axis_index("branch")
        chip, core = index // 2, index % 2
        return [lax.rem(chip + s, chips) * 2 + lax.rem(core + e, 2) for s, e in offsets]

    def owners():
        index = lax.axis_index("branch")
        chip, core = index // 2, index % 2
        return [lax.rem(chip + chips - s, chips) * 2 + lax.rem(core + e, 2) for s, e in offsets]

    inverse, pieces = normalize(layer_input, norm_gain, targets, branch_total, rows // slots)
    near = branch_send(pieces[1], chips, 0, 1)
    direct = [branch_send(pieces[2 * s], chips, s, 0) for s in range(1, chips)]
    held = gate(pieces[3::2], direct) if chips > 1 else ()
    across = [branch_send(piece, chips, s + 1, 1) for s, piece in enumerate(held)]
    turned = [pieces[0], near]
    for pair in zip(direct, across):
        turned += pair
    shifts = list(range(1, tensor_total)) + [0]
    if tensor_total > 2:
        shifts = [2, 1] + shifts[2:]

    def order(place):
        shift = sum(jnp.where(place == i, s, 0) for i, s in enumerate(shifts))
        return lax.rem(lax.axis_index("tensor") + shift, tensor_total)

    ready = min(2, tensor_total)
    deltas, parts, delta_turned, centre, input_columns, gain_columns = attention_backward(
        layer_input,
        inverse,
        norm_gain,
        w_query,
        w_key,
        w_value,
        head_grad,
        parents,
        row_counts,
        slots,
        order,
        tensor_total,
        ready,
        shares,
    )
    if ready < tensor_total:
        weights = (w_query, w_key, w_value)
        parts += back_project(
            order, ready, tensor_total - ready, delta_turned, centre, weights, tensor_total
        )
    (delta,) = gate(deltas[:1], (near, *direct))
    gathered = lax.all_gather(delta, "branch")
    arrived = [
        lax.ppermute(part, "tensor", [(t, (t + shift) % tensor_total) for t in range(tensor_total)])
        for part, shift in zip(parts, shifts[:-1])
    ]
    parts = [parts[-1]] + arrived
    *weights, token = weight_gradients(
        turned, gathered, owners, kv_local, group, arrived[:ready]
    )
    gain_sum, total = gain_sums(input_columns, inverse, parts, token)
    grad_input = finish(width, total, input_columns, gain_columns, inverse, parts)
    if chips == 2:
        sums = [gain_sum] + [branch_send(gain_sum, chips, s, e) for s, e in offsets[1:]]
        grad_gain = total_of_four(sums, grad_input)
    else:
        grad_gain = lax.psum(gain_sum, "branch").reshape(column_width)
    return (grad_input, *weights, grad_gain)


def solution(mesh):
    placed = (
        P(("parts", "branch"), None),
        P(),
        P(None, "tensor"),
        P(None, "tensor"),
        P(None, "tensor"),
        P(("parts", "branch"), "tensor"),
        P(("parts", "branch")),
        P("parts"),
    )
    return jax.shard_map(
        local,
        mesh=mesh,
        in_specs=placed,
        out_specs=(
            P(("parts", "branch"), "tensor"),
            P(("parts", "branch"), "tensor"),
            P(("parts", "branch"), "tensor"),
            P(("parts", "branch"), "tensor"),
            P(("parts", "tensor")),
        ),
        check_vma=False,
    )
```

```python
import functools

import jax
import jax.numpy as jnp
from jax import lax
from jax.experimental import pallas as pl
from jax.experimental.pallas import tpu as pltpu
from jax.sharding import PartitionSpec as P

HEAD_DIM = 256
MIB = 1024 * 1024
CENTRE_ROWS = 16
VMEM_LIMIT = 64 * MIB


epsilon = 1e-06
softcap_limit = 50.0


def nn_dot(left, right):
    return lax.dot_general(
        left, right, (((1,), (0,)), ((), ())), preferred_element_type=jnp.float32
    )


def nt_dot(left, right):
    return lax.dot_general(
        left, right, (((1,), (1,)), ((), ())), preferred_element_type=jnp.float32
    )


def tn_dot(left, right):
    return lax.dot_general(
        left, right, (((0,), (0,)), ((), ())), preferred_element_type=jnp.float32
    )


def small_cost():
    return pl.CostEstimate(flops=1000000, bytes_accessed=100000, transcendentals=0)


def norm_kernel(targets, input_ref, gain_ref, inverse_ref, *rest):
    piece_refs, turned = rest[:-1], rest[-1]
    rows, width = input_ref.shape
    values = input_ref[...].astype(jnp.float32)
    inverse = lax.rsqrt(jnp.mean(values * values, axis=-1, keepdims=True) + epsilon)
    inverse_ref[...] = inverse
    gain = gain_ref[...].reshape(1, width)
    turned[...] = (values * inverse * (1.0 + gain)).astype(jnp.bfloat16).T
    depth = width // len(piece_refs)
    for target, piece_ref in zip(targets(), piece_refs):
        start = pl.multiple_of(target * depth, 16)
        piece_ref[...] = turned[pl.ds(start, depth), :]


def normalize(layer_input, norm_gain, targets, pieces, block):
    rows, width = layer_input.shape
    depth = width // pieces
    out = pl.pallas_call(
        functools.partial(norm_kernel, targets),
        out_shape=(jax.ShapeDtypeStruct((rows, 1), jnp.float32),)
        + (jax.ShapeDtypeStruct((depth, rows), jnp.bfloat16),) * pieces,
        grid=(rows // block,),
        in_specs=[
            pl.BlockSpec((block, width), lambda i: (i, 0)),
            pl.BlockSpec((width,), lambda i: (0,)),
        ],
        out_specs=(pl.BlockSpec((block, 1), lambda i: (i, 0)),)
        + (pl.BlockSpec((depth, block), lambda i: (0, i)),) * pieces,
        scratch_shapes=[pltpu.VMEM((width, block), jnp.bfloat16)],
        compiler_params=pltpu.CompilerParams(vmem_limit_bytes=VMEM_LIMIT),
        cost_estimate=small_cost(),
        name="norm",
    )(layer_input, norm_gain)
    return out[0], out[1:]


def ancestor_mask(parent_row):
    rows = parent_row.shape[1]
    row = lax.broadcasted_iota(jnp.int32, (rows, rows), 0)
    column = lax.broadcasted_iota(jnp.int32, (rows, rows), 1)
    reached = jnp.where((parent_row == row) | (row == column), 1.0, 0.0)
    for squaring in range(rows.bit_length() - 1):
        halfway = reached.astype(jnp.bfloat16)
        reached = jnp.minimum(nn_dot(halfway, halfway), 1.0)
    return reached.T


def attention_kernel(
    slots,
    group,
    kv_local,
    order,
    blocks,
    ready,
    columns,
    shares,
    count_ref,
    parent_ref,
    inverse_ref,
    gain_ref,
    input_hbm,
    query_hbm,
    key_hbm,
    value_hbm,
    grad_hbm,
    *rest,
):
    delta_hbm, rest = rest[: len(shares)], rest[len(shares) :]
    part_hbm, rest = rest[:ready], rest[ready:]
    turned_hbm, centre_out, rest = rest[:3], rest[3], rest[4:]
    column_hbm, column_gain_ref, rest = rest[0], rest[1], rest[2:]
    (
        input_ref,
        gain_row,
        query_ref,
        key_ref,
        value_ref,
        grad_ref,
        sum_ref,
        delta_ref,
        query_turned,
        key_turned,
        value_turned,
        allowed_ref,
        centre_ref,
        kept,
        load_sem,
        weight_sem,
        store_sem,
        part_sem,
    ) = rest
    head_dim = HEAD_DIM
    rows, width = input_ref.shape
    block = rows // slots
    mid = group * head_dim
    steps = weight_sem.shape[0]
    chunk = width // steps
    weights = ((query_hbm, query_ref, mid, 0), (key_hbm, key_ref, head_dim, mid))
    weights += ((value_hbm, value_ref, head_dim, mid + head_dim),)

    def fetch(step, which):
        lines = pl.ds(pl.multiple_of(step * chunk, chunk), chunk)
        source, kept_ref = weights[which][:2]
        return pltpu.make_async_copy(
            source.at[lines, :], kept_ref.at[lines, :], weight_sem.at[step, which]
        )

    input_load = pltpu.make_async_copy(input_hbm, input_ref, load_sem.at[0])
    grad_load = pltpu.make_async_copy(grad_hbm, grad_ref, load_sem.at[1])
    input_load.start()
    for step in range(steps):
        for which in range(3):
            fetch(step, which).start()
    grad_load.start()
    gain_row[...] = gain_ref[...].reshape(1, width)

    first_count = lax.axis_index("branch") * slots
    parents = parent_ref[...].reshape(1, rows)
    for slot in range(slots):
        allowed_ref[slot] = ancestor_mask(parents[:, slot * block : (slot + 1) * block])
    sum_ref[...] = jnp.zeros_like(sum_ref)
    inverse = inverse_ref[...]
    input_load.wait()
    stores = []
    if columns:
        start = pl.multiple_of(lax.axis_index("tensor") * columns, 128)
        stores.append(
            pltpu.make_async_copy(
                input_ref.at[:, pl.ds(start, columns)], column_hbm, store_sem.at[0]
            )
        )
        stores[0].start()
        column_gain_ref[...] = gain_row[:, pl.ds(start, columns)]
    else:
        column_gain_ref[...] = jnp.zeros_like(column_gain_ref)

    def project(step, carry):
        lines = pl.ds(pl.multiple_of(step * chunk, chunk), chunk)
        gain = 1.0 + gain_row[:, lines]
        normed = (input_ref[:, lines].astype(jnp.float32) * inverse * gain).astype(jnp.bfloat16)
        for which, (_, kept_ref, wide, place) in enumerate(weights):
            fetch(step, which).wait()
            term = nn_dot(normed, kept_ref[lines, :])
            for h in range(kv_local):
                sum_ref[h, :, place : place + wide] += term[:, h * wide : (h + 1) * wide]
        return carry

    lax.fori_loop(0, steps, project, 0)
    grad_load.wait()
    scale = head_dim ** (-0.5)
    centre_ref[...] = jnp.zeros_like(centre_ref)

    def attend(h, carry):
        for slot in range(slots):
            lines = slice(slot * block, (slot + 1) * block)
            live = (
                lax.broadcasted_iota(jnp.int32, (block, mid), 0) < count_ref[first_count + slot]
            )
            columns = pl.ds(pl.multiple_of(h * mid, mid), mid)
            grad_rows = jnp.where(live, grad_ref[lines, columns].astype(jnp.float32), 0.0)
            pair = [slice(g * head_dim, (g + 1) * head_dim) for g in range(group)]
            grads = jnp.concatenate([grad_rows[:, p] for p in pair], axis=0).astype(jnp.bfloat16)
            queries = jnp.concatenate([sum_ref[h, lines, p] for p in pair], axis=0)
            queries = queries.astype(jnp.bfloat16)
            keys = sum_ref[h, lines, mid : mid + head_dim].astype(jnp.bfloat16)
            values = sum_ref[h, lines, mid + head_dim :].astype(jnp.bfloat16)
            allowed = jnp.concatenate([allowed_ref[slot]] * group, axis=0)
            bounded = jnp.tanh(nt_dot(queries, keys) * (scale / softcap_limit))
            weighted = allowed * jnp.exp(softcap_limit * bounded)
            probabilities = weighted * (1.0 / jnp.sum(weighted, axis=-1, keepdims=True))
            d_probs = nt_dot(grads, values)
            d_scores = probabilities * (
                d_probs - jnp.sum(probabilities * d_probs, axis=-1, keepdims=True)
            )
            d_raw = (d_scores * (1.0 - bounded * bounded) * scale).astype(jnp.bfloat16)
            prob_half = probabilities.astype(jnp.bfloat16)
            d_query = nn_dot(d_raw, keys)
            d_key = tn_dot(d_raw, queries)
            d_value = tn_dot(prob_half, grads)
            places = [
                (d_query[g * block : (g + 1) * block], query_turned, h * mid + g * head_dim)
                for g in range(group)
            ]
            places += [(d_key, key_turned, h * head_dim), (d_value, value_turned, h * head_dim)]
            product = None
            for which, (part, turned_ref, start) in enumerate(places):
                half = part.astype(jnp.bfloat16)
                line = which * rows + slot * block
                delta_ref[h, line : line + block, :] = half
                spot = pl.ds(pl.multiple_of(start, head_dim), head_dim)
                turned_ref[spot, lines] = half.T
                term = half.astype(jnp.float32) * sum_ref[
                    h, lines, which * head_dim : (which + 1) * head_dim
                ]
                product = term if product is None else product + term
            centre_ref[lines, :] += jnp.sum(product, axis=-1, keepdims=True)
        return carry

    lax.fori_loop(0, kv_local, attend, 0)
    lasts = []
    for share, out in zip(shares, delta_hbm):
        for place, block_index in enumerate(share):
            h, which = divmod(block_index, group + 2)
            lasts.append(
                pltpu.make_async_copy(
                    delta_ref.at[h, pl.ds(which * rows, rows), :],
                    out.at[pl.ds(place * rows, rows), :],
                    store_sem.at[1 + len(lasts)],
                )
            )
    for which, turned_ref in enumerate((query_turned, key_turned, value_turned)):
        lasts.append(
            pltpu.make_async_copy(turned_ref, turned_hbm[which], store_sem.at[1 + len(lasts)])
        )
    for store in lasts:
        store.start()

    centre = jnp.broadcast_to(centre_ref[...], (rows, 128)).T[:CENTRE_ROWS].astype(jnp.bfloat16)
    centre_out[...] = centre
    span = width // blocks
    cuts = 2
    cut_lines = span // cuts
    parts = [
        pltpu.make_async_copy(kept.at[place], part_hbm[place], part_sem.at[place])
        for place in range(ready)
    ]

    def project_back(step, carry):
        place, cut = step // cuts, lax.rem(step, cuts)
        lines = pl.ds(pl.multiple_of(order(place) * span + cut * cut_lines, 16), cut_lines)
        total = nn_dot(query_ref[lines, :], query_turned[...])
        total += nn_dot(key_ref[lines, :], key_turned[...])
        total += nn_dot(value_ref[lines, :], value_turned[...])
        spot = pl.ds(pl.multiple_of(cut * cut_lines, 16), cut_lines)
        kept[place, spot, :] = total.astype(jnp.bfloat16)
        for which, part in enumerate(parts):

            @pl.when((place == which) & (cut == cuts - 1))
            def _():
                kept[which, span:, :] = centre
                part.start()

        return carry

    lax.fori_loop(0, ready * cuts, project_back, 0)
    for store in stores + lasts + parts:
        store.wait()


def attention_backward(
    layer_input,
    inverse,
    norm_gain,
    w_query,
    w_key,
    w_value,
    head_grad,
    parents,
    counts,
    slots,
    order,
    blocks,
    ready,
    shares,
):
    rows, width = layer_input.shape
    kv_local = w_key.shape[1] // HEAD_DIM
    group = w_query.shape[1] // w_key.shape[1]
    span = (group + 2) * HEAD_DIM
    stack = (group + 2) * rows
    column_width = width // blocks
    cut = column_width % 128 == 0
    wide = column_width if cut else 128
    steps = 2 if width % 512 == 0 else 1
    part_shape = (column_width + CENTRE_ROWS, rows)
    hbm = pl.BlockSpec(memory_space=pl.ANY)
    vmem = pl.BlockSpec(memory_space=pltpu.VMEM)
    half = lambda *shape: jax.ShapeDtypeStruct(shape, jnp.bfloat16)
    out = pl.pallas_call(
        functools.partial(
            attention_kernel,
            slots,
            group,
            kv_local,
            order,
            blocks,
            ready,
            wide if cut else 0,
            shares,
        ),
        out_shape=tuple(half(len(share) * rows, HEAD_DIM) for share in shares)
        + (half(*part_shape),) * ready
        + tuple(half(w.shape[1], rows) for w in (w_query, w_key, w_value))
        + (half(CENTRE_ROWS, rows),)
        + (half(rows, wide), jax.ShapeDtypeStruct((1, wide), jnp.float32)),
        in_specs=[pl.BlockSpec(memory_space=pltpu.SMEM), vmem, vmem, vmem] + [hbm] * 5,
        out_specs=(hbm,) * (len(shares) + ready + 3) + (vmem, hbm, vmem),
        scratch_shapes=[
            pltpu.VMEM((rows, width), jnp.bfloat16),
            pltpu.VMEM((1, width), jnp.float32),
            pltpu.VMEM(w_query.shape, jnp.bfloat16),
            pltpu.VMEM(w_key.shape, jnp.bfloat16),
            pltpu.VMEM(w_value.shape, jnp.bfloat16),
            pltpu.VMEM(head_grad.shape, jnp.bfloat16),
            pltpu.VMEM((kv_local, rows, span), jnp.float32),
            pltpu.VMEM((kv_local, stack, HEAD_DIM), jnp.bfloat16),
            pltpu.VMEM((w_query.shape[1], rows), jnp.bfloat16),
            pltpu.VMEM((w_key.shape[1], rows), jnp.bfloat16),
            pltpu.VMEM((w_value.shape[1], rows), jnp.bfloat16),
            pltpu.VMEM((slots, rows // slots, rows // slots), jnp.float32),
            pltpu.VMEM((rows, 1), jnp.float32),
            pltpu.VMEM((ready, *part_shape), jnp.bfloat16),
            pltpu.SemaphoreType.DMA((2,)),
            pltpu.SemaphoreType.DMA((steps, 3)),
            pltpu.SemaphoreType.DMA((4 + kv_local * (group + 2),)),
            pltpu.SemaphoreType.DMA((ready,)),
        ],
        compiler_params=pltpu.CompilerParams(vmem_limit_bytes=VMEM_LIMIT),
        cost_estimate=small_cost(),
        name="attention",
    )(counts, parents, inverse, norm_gain, layer_input, w_query, w_key, w_value, head_grad)
    deltas, out = out[: len(shares)], out[len(shares) :]
    parts, turned, centre = out[:ready], out[ready : ready + 3], out[ready + 3]
    if cut:
        input_cut, gain_cut = out[-2], out[-1]
    else:
        start = lax.axis_index("tensor") * column_width
        input_cut = lax.dynamic_slice_in_dim(layer_input, start, column_width, 1)
        gain_cut = lax.dynamic_slice_in_dim(norm_gain, start, column_width, 0)
        gain_cut = gain_cut.reshape(1, column_width)
    return deltas, parts, turned, centre, input_cut, gain_cut


def back_kernel(centre_ref, *refs):
    turned_refs, weight_refs, out_refs = refs[:3], refs[3:6], refs[6:]
    piece, cut = pl.program_id(0), pl.program_id(1)
    lines = weight_refs[0].shape[0]
    total = None
    for weight_ref, turned_ref in zip(weight_refs, turned_refs):
        term = nn_dot(weight_ref[...], turned_ref[...])
        total = term if total is None else total + term
    total = total.astype(jnp.bfloat16)
    start = pl.multiple_of(cut * lines, 16)
    depth = out_refs[0].shape[0] - CENTRE_ROWS
    for place, out_ref in enumerate(out_refs):

        @pl.when(piece == place)
        def _():
            out_ref[pl.ds(start, lines), :] = total
            out_ref[depth:, :] = centre_ref[...]


def back_project(order, first, pieces, turned, centre, weights, blocks):
    rows = centre.shape[1]
    depth = weights[0].shape[0] // blocks
    cuts = 2
    whole = lambda i, j: (0, 0)
    return pl.pallas_call(
        back_kernel,
        out_shape=(jax.ShapeDtypeStruct((depth + CENTRE_ROWS, rows), jnp.bfloat16),) * pieces,
        grid=(pieces, cuts),
        in_specs=[pl.BlockSpec(x.shape, whole) for x in (centre, *turned)]
        + [
            pl.BlockSpec((depth // cuts, w.shape[1]), lambda i, j: (order(first + i) * cuts + j, 0))
            for w in weights
        ],
        out_specs=(pl.BlockSpec((depth + CENTRE_ROWS, rows), whole),) * pieces,
        compiler_params=pltpu.CompilerParams(vmem_limit_bytes=VMEM_LIMIT),
        cost_estimate=small_cost(),
        name="back",
    )(centre, *turned, *weights)


def weight_kernel(outs, sources, *refs):
    turned_hbm, delta_hbm = refs[:sources], refs[sources : 2 * sources]
    out_hbm, token_ref = refs[-10:-7], refs[-7]
    turned_ref, delta_ref, kept, turned_sem, delta_sem, store_sem = refs[-6:]
    token_ref[...] = jnp.zeros_like(token_ref)
    rows = turned_ref.shape[2]
    loads = []
    for place in range(sources):
        loads.append(
            pltpu.make_async_copy(
                turned_hbm[place], turned_ref.at[place], turned_sem.at[place]
            )
        )
        loads.append(
            pltpu.make_async_copy(delta_hbm[place], delta_ref.at[place], delta_sem.at[place])
        )
    for load in loads:
        load.start()
    for load in loads:
        load.wait()
    stores = [
        pltpu.make_async_copy(
            kept.at[block],
            out_hbm[which].at[:, pl.ds(column * HEAD_DIM, HEAD_DIM)],
            store_sem.at[block],
        )
        for block, (which, column) in enumerate(outs)
    ]

    def fill(block, carry):
        lines = pl.ds(pl.multiple_of(block * rows, rows), rows)
        total = None
        for place in range(sources):
            term = nn_dot(turned_ref[place], delta_ref[place, lines, :])
            total = term if total is None else total + term
        kept[block] = total
        for which, store in enumerate(stores):

            @pl.when(block == which)
            def _():
                store.start()

        return carry

    lax.fori_loop(0, len(outs), fill, 0)
    for store in stores:
        store.wait()


def weight_gradients(turned, deltas, share, kv_local, group, before):
    depth, rows = turned[0].shape
    sources = len(turned)
    outs = []
    for block in share:
        h, which = divmod(block, group + 2)
        outs.append((0, h * group + which) if which < group else (which - group + 1, h))
    kept = list(before) if before is not None else []
    hbm = pl.BlockSpec(memory_space=pl.ANY)
    return pl.pallas_call(
        functools.partial(weight_kernel, outs, sources),
        out_shape=(
            jax.ShapeDtypeStruct((depth, kv_local * group * HEAD_DIM), jnp.float32),
            jax.ShapeDtypeStruct((depth, kv_local * HEAD_DIM), jnp.float32),
            jax.ShapeDtypeStruct((depth, kv_local * HEAD_DIM), jnp.float32),
            jax.ShapeDtypeStruct((8, 128), jnp.float32),
        ),
        in_specs=[hbm] * (2 * sources + len(kept)),
        out_specs=(hbm,) * 3 + (pl.BlockSpec(memory_space=pltpu.VMEM),),
        input_output_aliases={2 * sources + i: i for i in range(len(kept))},
        scratch_shapes=[
            pltpu.VMEM((sources, depth, rows), jnp.bfloat16),
            pltpu.VMEM((sources, len(share) * rows, HEAD_DIM), jnp.bfloat16),
            pltpu.VMEM((len(share), depth, HEAD_DIM), jnp.float32),
            pltpu.SemaphoreType.DMA((sources,)),
            pltpu.SemaphoreType.DMA((sources,)),
            pltpu.SemaphoreType.DMA((len(share),)),
        ],
        compiler_params=pltpu.CompilerParams(vmem_limit_bytes=VMEM_LIMIT),
        cost_estimate=small_cost(),
        name="weights",
    )(*turned, *deltas, *kept)


def gate_kernel(*refs):
    del refs


def gate(arrays, tokens):
    hbm = pl.BlockSpec(memory_space=pl.ANY)
    return pl.pallas_call(
        gate_kernel,
        out_shape=tuple(jax.ShapeDtypeStruct(x.shape, x.dtype) for x in arrays),
        in_specs=[hbm] * (len(arrays) + len(tokens)),
        out_specs=(hbm,) * len(arrays),
        input_output_aliases={i: i for i in range(len(arrays))},
        compiler_params=pltpu.CompilerParams(vmem_limit_bytes=VMEM_LIMIT),
        cost_estimate=small_cost(),
        name="gate",
    )(*arrays, *tokens)


def join_kernel(inner_ref, other_ref, end_ref, *rest):
    out_ref, token_ref = rest[-2:]
    token_ref[...] = jnp.zeros_like(token_ref)
    index = lax.axis_index("tensor")
    inner = (index > 0) & (index < lax.axis_size("tensor") - 1)

    @pl.when(inner)
    def _():
        out_ref[...] = (
            inner_ref[...].astype(jnp.float32) + other_ref[...].astype(jnp.float32)
        ).astype(jnp.bfloat16)

    @pl.when(jnp.logical_not(inner))
    def _():
        out_ref[...] = end_ref[...]


def join(inner_part, other, end_part, tokens):
    vmem = pl.BlockSpec(memory_space=pltpu.VMEM)
    return pl.pallas_call(
        join_kernel,
        out_shape=(
            jax.ShapeDtypeStruct(end_part.shape, end_part.dtype),
            jax.ShapeDtypeStruct((8, 128), jnp.float32),
        ),
        in_specs=[vmem] * 3 + [pl.BlockSpec(memory_space=pl.ANY)] * len(tokens),
        out_specs=(vmem, vmem),
        compiler_params=pltpu.CompilerParams(vmem_limit_bytes=VMEM_LIMIT),
        cost_estimate=small_cost(),
        name="join",
    )(inner_part, other, end_part, *tokens)


def add_parts(for_ends, for_inner, part_refs):
    index = lax.axis_index("tensor")
    ends = ((index == 0) | (index == lax.axis_size("tensor") - 1)).astype(jnp.float32)
    total = None
    for place, part_ref in enumerate(part_refs):
        part = part_ref[...].astype(jnp.float32)
        if place < for_ends:
            part = part * ends
        elif place < for_ends + for_inner:
            part = part * (1.0 - ends)
        total = part if total is None else total + part
    return total


def gain_kernel(add, count, input_ref, inverse_ref, *refs):
    part_refs, (sum_ref, total_ref) = refs[:count], refs[-2:]

    @pl.when(pl.program_id(0) == 0)
    def _():
        sum_ref[...] = jnp.zeros_like(sum_ref)

    d_normed = add(part_refs).T
    total_ref[...] = d_normed
    scaled = input_ref[...].astype(jnp.float32) * inverse_ref[...]
    sum_ref[...] += jnp.sum(d_normed * scaled, axis=0, keepdims=True)


def gain_sums(add, input_columns, inverse, parts, token):
    rows, wide = input_columns.shape
    some = 128
    return pl.pallas_call(
        functools.partial(gain_kernel, add, len(parts)),
        out_shape=(
            jax.ShapeDtypeStruct((1, wide), jnp.float32),
            jax.ShapeDtypeStruct((rows, wide), jnp.float32),
        ),
        grid=(rows // some,),
        in_specs=[
            pl.BlockSpec((some, wide), lambda i: (i, 0)),
            pl.BlockSpec((some, 1), lambda i: (i, 0)),
        ]
        + [pl.BlockSpec((wide, some), lambda i: (0, i))] * len(parts)
        + [pl.BlockSpec(memory_space=pl.ANY)],
        out_specs=(
            pl.BlockSpec((1, wide), lambda i: (0, 0)),
            pl.BlockSpec((some, wide), lambda i: (i, 0)),
        ),
        compiler_params=pltpu.CompilerParams(vmem_limit_bytes=VMEM_LIMIT),
        cost_estimate=small_cost(),
        name="gains",
    )(input_columns, inverse, *parts, token)


def finish_kernel(width, add, total_ref, input_ref, gain_ref, inverse_ref, *refs):
    centre_refs, out_ref = refs[:-1], refs[-1]
    centre = add(centre_refs).T[:, :1] * (1.0 / width)
    inverse = inverse_ref[...]
    scaled = input_ref[...].astype(jnp.float32) * inverse
    out_ref[...] = (
        inverse * ((1.0 + gain_ref[...]) * total_ref[...] - scaled * centre)
    ).astype(jnp.bfloat16)


def finish(width, add, total, input_columns, gain_columns, inverse, parts):
    rows, wide = input_columns.shape
    some = 128
    row_block = pl.BlockSpec((some, wide), lambda i: (i, 0))
    return pl.pallas_call(
        functools.partial(finish_kernel, width, add),
        out_shape=jax.ShapeDtypeStruct((rows, wide), jnp.bfloat16),
        grid=(rows // some,),
        in_specs=[
            row_block,
            row_block,
            pl.BlockSpec((1, wide), lambda i: (0, 0)),
            pl.BlockSpec((some, 1), lambda i: (i, 0)),
        ]
        + [pl.BlockSpec((CENTRE_ROWS, some), lambda i: (wide // CENTRE_ROWS, i))] * len(parts),
        out_specs=row_block,
        compiler_params=pltpu.CompilerParams(vmem_limit_bytes=VMEM_LIMIT),
        cost_estimate=small_cost(),
        name="finish",
    )(total, input_columns, gain_columns, inverse, *parts)


def total_kernel(*refs):
    total = (refs[0][...] + refs[1][...]) + (refs[2][...] + refs[3][...])
    refs[-1][...] = total.reshape(refs[-1].shape)


def total_of_four(arrays, token):
    whole = pl.BlockSpec(arrays[0].shape, lambda i: (0, 0))
    wide = arrays[0].shape[1]
    return pl.pallas_call(
        total_kernel,
        out_shape=jax.ShapeDtypeStruct((wide,), arrays[0].dtype),
        grid=(1,),
        in_specs=[whole] * 4 + [pl.BlockSpec(memory_space=pl.ANY)],
        out_specs=pl.BlockSpec((wide,), lambda i: (0,)),
        compiler_params=pltpu.CompilerParams(vmem_limit_bytes=VMEM_LIMIT),
        cost_estimate=small_cost(),
        name="total",
    )(*arrays, token)


def branch_send(array, chips, shift, swap):
    pairs = [
        (c * 2 + k, ((c + shift) % chips) * 2 + (k ^ swap)) for c in range(chips) for k in range(2)
    ]
    return lax.ppermute(array, "branch", pairs)


def pick(table, index):
    chosen = table[-1]
    for place in range(len(table) - 2, -1, -1):
        chosen = jnp.where(index == place, table[place], chosen)
    return chosen


def scatter_order(total):
    index = lax.axis_index("tensor")
    if total != 4:
        return lambda place: lax.rem(index + place + 1, total)
    table = [[3, 0, 3, 0], [0, 2, 1, 3], [2, 3, 0, 1], [1, 1, 2, 2]]
    here = [pick(row, index) for row in table]
    return lambda place: pick(here, place)


def scatter_begin(parts, total):
    if total != 4:
        return [
            lax.ppermute(part, "tensor", [(t, (t + shift) % total) for t in range(total)])
            for shift, part in zip(range(1, total), parts[:-1])
        ]
    from_first = lax.ppermute(parts[0], "tensor", [(0, 1), (1, 0), (2, 3), (3, 2)])
    from_inner = lax.ppermute(parts[1], "tensor", [(1, 2), (2, 1)])
    from_ends = lax.ppermute(parts[2], "tensor", [(0, 2), (3, 1)])
    return from_first, from_inner, from_ends


def scatter_end(parts, arrived, total):
    if total != 4:
        return [parts[-1], *arrived], 0, 0, arrived[0]
    from_first, from_inner, from_ends = arrived
    joined, token = join(parts[2], from_first, parts[3], (from_inner, from_ends))
    from_joined = lax.ppermute(joined, "tensor", [(1, 3), (2, 0), (0, 1), (3, 2)])
    return [from_first, parts[1], parts[3], from_inner, from_ends, from_joined], 2, 1, token


def local(layer_input, norm_gain, w_query, w_key, w_value, head_grad, parents, row_counts):
    branch_total = lax.axis_size("branch")
    tensor_total = lax.axis_size("tensor")
    slots = row_counts.shape[0] // branch_total
    rows, width = layer_input.shape
    column_width = width // tensor_total
    chips = branch_total // 2
    group = w_query.shape[1] // w_key.shape[1]
    kv_local = w_key.shape[1] // HEAD_DIM
    offsets = [(shift, swap) for shift in range(chips) for swap in range(2)]
    blocks = list(range(kv_local * (group + 2)))
    early = blocks[: group + 2] + [h * (group + 2) + group for h in range(1, kv_local)]
    shares = [early, [block for block in blocks if block not in early]]
    shares = [share for share in shares if share]

    def targets():
        index = lax.axis_index("branch")
        chip, core = index // 2, index % 2
        return [lax.rem(chip + s, chips) * 2 + lax.rem(core + e, 2) for s, e in offsets]

    inverse, pieces = normalize(layer_input, norm_gain, targets, branch_total, rows // slots)
    near = branch_send(pieces[1], chips, 0, 1)
    direct = [branch_send(pieces[2 * s], chips, s, 0) for s in range(1, chips)]
    held = gate(pieces[3::2], direct) if chips > 1 else ()
    across = [branch_send(piece, chips, s + 1, 1) for s, piece in enumerate(held)]
    turned = [pieces[0]] + direct + [near] + across
    order = lambda place: scatter_order(tensor_total)(place)
    ready = min(3, tensor_total)
    deltas, parts, delta_turned, centre, input_columns, gain_columns = attention_backward(
        layer_input,
        inverse,
        norm_gain,
        w_query,
        w_key,
        w_value,
        head_grad,
        parents,
        row_counts,
        slots,
        order,
        tensor_total,
        ready,
        shares,
    )
    if ready < tensor_total:
        weights = (w_query, w_key, w_value)
        parts += back_project(
            order, ready, tensor_total - ready, delta_turned, centre, weights, tensor_total
        )
    arrived = scatter_begin(parts, tensor_total)

    (first,) = gate(deltas[:1], (near, *direct))
    sent = [branch_send(first, chips, s, 0) for s in range(1, chips)]
    parts, for_ends, for_inner, met = scatter_end(parts, arrived, tensor_total)
    *sent, first = gate((*sent, first), parts[2:3])
    others = gate(deltas[1:], (sent[0],)) if deltas[1:] else ()
    weights, tokens = None, []
    for share, delta in zip(shares, (first, *others)):
        if tokens:
            sent = [branch_send(delta, chips, s, 0) for s in range(1, chips)]
            delta, *sent = gate((delta, *sent), ())
        gathered = [delta] + sent
        gathered += [branch_send(part, chips, 0, 1) for part in gathered]
        *weights, token = weight_gradients(turned, gathered, share, kv_local, group, weights)
        tokens.append(token)

    add = functools.partial(add_parts, for_ends, for_inner)
    gain_sum, total = gain_sums(add, input_columns, inverse, parts, tokens[0])
    grad_input = finish(width, add, total, input_columns, gain_columns, inverse, parts)
    if chips == 2:
        sums = [gain_sum] + [branch_send(gain_sum, chips, s, e) for s, e in offsets[1:]]
        grad_gain = total_of_four(sums, tokens[-1])
    else:
        grad_gain = lax.psum(gain_sum, "branch").reshape(column_width)
    return (grad_input, *weights, grad_gain)


def solution(mesh):
    placed = (
        P(("parts", "branch"), None),
        P(),
        P(None, "tensor"),
        P(None, "tensor"),
        P(None, "tensor"),
        P(("parts", "branch"), "tensor"),
        P(("parts", "branch")),
        P("parts"),
    )
    return jax.shard_map(
        local,
        mesh=mesh,
        in_specs=placed,
        out_specs=(
            P(("parts", "branch"), "tensor"),
            P(("parts", "branch"), "tensor"),
            P(("parts", "branch"), "tensor"),
            P(("parts", "branch"), "tensor"),
            P(("parts", "tensor")),
        ),
        check_vma=False,
    )
```

```python
import functools

import jax
import jax.numpy as jnp
from jax import lax
from jax.experimental import pallas as pl
from jax.experimental.pallas import tpu as pltpu
from jax.sharding import PartitionSpec as P

HEAD_DIM = 256
MIB = 1024 * 1024
CENTRE_ROWS = 16
VMEM_LIMIT = 64 * MIB


epsilon = 1e-06
softcap_limit = 50.0


def nn_dot(left, right):
    return lax.dot_general(
        left, right, (((1,), (0,)), ((), ())), preferred_element_type=jnp.float32
    )


def nt_dot(left, right):
    return lax.dot_general(
        left, right, (((1,), (1,)), ((), ())), preferred_element_type=jnp.float32
    )


def tn_dot(left, right):
    return lax.dot_general(
        left, right, (((0,), (0,)), ((), ())), preferred_element_type=jnp.float32
    )


def small_cost():
    return pl.CostEstimate(flops=1000000, bytes_accessed=100000, transcendentals=0)


def norm_kernel(targets, input_ref, gain_ref, inverse_ref, *rest):
    piece_refs, turned = rest[:-1], rest[-1]
    rows, width = input_ref.shape
    values = input_ref[...].astype(jnp.float32)
    inverse = lax.rsqrt(jnp.mean(values * values, axis=-1, keepdims=True) + epsilon)
    inverse_ref[...] = inverse
    gain = gain_ref[...].reshape(1, width)
    turned[...] = (values * inverse * (1.0 + gain)).astype(jnp.bfloat16).T
    depth = width // len(piece_refs)
    for target, piece_ref in zip(targets(), piece_refs):
        start = pl.multiple_of(target * depth, 16)
        piece_ref[...] = turned[pl.ds(start, depth), :]


def normalize(layer_input, norm_gain, targets, pieces, block):
    rows, width = layer_input.shape
    depth = width // pieces
    out = pl.pallas_call(
        functools.partial(norm_kernel, targets),
        out_shape=(jax.ShapeDtypeStruct((rows, 1), jnp.float32),)
        + (jax.ShapeDtypeStruct((depth, rows), jnp.bfloat16),) * pieces,
        grid=(rows // block,),
        in_specs=[
            pl.BlockSpec((block, width), lambda i: (i, 0)),
            pl.BlockSpec((width,), lambda i: (0,)),
        ],
        out_specs=(pl.BlockSpec((block, 1), lambda i: (i, 0)),)
        + (pl.BlockSpec((depth, block), lambda i: (0, i)),) * pieces,
        scratch_shapes=[pltpu.VMEM((width, block), jnp.bfloat16)],
        compiler_params=pltpu.CompilerParams(vmem_limit_bytes=VMEM_LIMIT),
        cost_estimate=small_cost(),
        name="norm",
    )(layer_input, norm_gain)
    return out[0], out[1:]


def ancestor_mask(parent_row):
    rows = parent_row.shape[1]
    row = lax.broadcasted_iota(jnp.int32, (rows, rows), 0)
    column = lax.broadcasted_iota(jnp.int32, (rows, rows), 1)
    reached = jnp.where((parent_row == row) | (row == column), 1.0, 0.0)
    for squaring in range(rows.bit_length() - 1):
        halfway = reached.astype(jnp.bfloat16)
        reached = jnp.minimum(nn_dot(halfway, halfway), 1.0)
    return reached.T


def attention_kernel(
    slots,
    group,
    kv_local,
    order,
    blocks,
    ready,
    columns,
    shares,
    count_ref,
    parent_ref,
    inverse_ref,
    gain_ref,
    input_hbm,
    query_hbm,
    key_hbm,
    value_hbm,
    grad_hbm,
    *rest,
):
    delta_hbm, rest = rest[: len(shares)], rest[len(shares) :]
    part_hbm, rest = rest[:ready], rest[ready:]
    turned_hbm, centre_out, rest = rest[:3], rest[3], rest[4:]
    column_hbm, column_gain_ref, rest = rest[0], rest[1], rest[2:]
    (
        input_ref,
        gain_row,
        query_ref,
        key_ref,
        value_ref,
        grad_ref,
        sum_ref,
        delta_ref,
        query_turned,
        key_turned,
        value_turned,
        allowed_ref,
        centre_ref,
        kept,
        load_sem,
        weight_sem,
        store_sem,
        part_sem,
    ) = rest
    head_dim = HEAD_DIM
    rows, width = input_ref.shape
    block = rows // slots
    mid = group * head_dim
    steps = weight_sem.shape[0]
    chunk = width // steps
    weights = ((query_hbm, query_ref, mid, 0), (key_hbm, key_ref, head_dim, mid))
    weights += ((value_hbm, value_ref, head_dim, mid + head_dim),)

    def fetch(step, which):
        lines = pl.ds(step * chunk, chunk)
        source, kept_ref = weights[which][:2]
        return pltpu.make_async_copy(
            source.at[lines, :], kept_ref.at[lines, :], weight_sem.at[step, which]
        )

    input_load = pltpu.make_async_copy(input_hbm, input_ref, load_sem.at[0])
    grad_load = pltpu.make_async_copy(grad_hbm, grad_ref, load_sem.at[1])
    input_load.start()
    for step in range(steps):
        for which in range(3):
            fetch(step, which).start()
    grad_load.start()
    gain_row[...] = gain_ref[...].reshape(1, width)

    first_count = lax.axis_index("branch") * slots
    parents = parent_ref[...].reshape(1, rows)
    for slot in range(slots):
        allowed_ref[slot] = ancestor_mask(parents[:, slot * block : (slot + 1) * block])
    inverse = inverse_ref[...]
    input_load.wait()
    stores = []
    if columns:
        start = pl.multiple_of(lax.axis_index("tensor") * columns, 128)
        stores.append(
            pltpu.make_async_copy(
                input_ref.at[:, pl.ds(start, columns)], column_hbm, store_sem.at[0]
            )
        )
        stores[0].start()
        column_gain_ref[...] = gain_row[:, pl.ds(start, columns)]
    else:
        column_gain_ref[...] = jnp.zeros_like(column_gain_ref)

    for step in range(steps):
        lines = slice(step * chunk, (step + 1) * chunk)
        gain = 1.0 + gain_row[:, lines]
        normed = (input_ref[:, lines].astype(jnp.float32) * inverse * gain).astype(jnp.bfloat16)
        for which, (_, kept_ref, wide, place) in enumerate(weights):
            fetch(step, which).wait()
            term = nn_dot(normed, kept_ref[lines, :])
            for h in range(kv_local):
                part = term[:, h * wide : (h + 1) * wide]
                if step > 0:
                    part = part + sum_ref[h, :, place : place + wide]
                sum_ref[h, :, place : place + wide] = part
    grad_load.wait()
    scale = head_dim ** (-0.5)
    centre_ref[...] = jnp.zeros_like(centre_ref)

    def attend(h, carry):
        for slot in range(slots):
            lines = slice(slot * block, (slot + 1) * block)
            live = (
                lax.broadcasted_iota(jnp.int32, (block, mid), 0) < count_ref[first_count + slot]
            )
            columns = pl.ds(pl.multiple_of(h * mid, mid), mid)
            grad_rows = jnp.where(live, grad_ref[lines, columns].astype(jnp.float32), 0.0)
            pair = [slice(g * head_dim, (g + 1) * head_dim) for g in range(group)]
            grads = jnp.concatenate([grad_rows[:, p] for p in pair], axis=0).astype(jnp.bfloat16)
            queries = jnp.concatenate([sum_ref[h, lines, p] for p in pair], axis=0)
            queries = queries.astype(jnp.bfloat16)
            keys = sum_ref[h, lines, mid : mid + head_dim].astype(jnp.bfloat16)
            values = sum_ref[h, lines, mid + head_dim :].astype(jnp.bfloat16)
            allowed = jnp.concatenate([allowed_ref[slot]] * group, axis=0)
            bounded = jnp.tanh(nt_dot(queries, keys) * (scale / softcap_limit))
            weighted = allowed * jnp.exp(softcap_limit * bounded)
            probabilities = weighted * (1.0 / jnp.sum(weighted, axis=-1, keepdims=True))
            d_probs = nt_dot(grads, values)
            d_scores = probabilities * (
                d_probs - jnp.sum(probabilities * d_probs, axis=-1, keepdims=True)
            )
            d_raw = (d_scores * (1.0 - bounded * bounded) * scale).astype(jnp.bfloat16)
            prob_half = probabilities.astype(jnp.bfloat16)
            d_query = nn_dot(d_raw, keys)
            d_key = tn_dot(d_raw, queries)
            d_value = tn_dot(prob_half, grads)
            places = [
                (d_query[g * block : (g + 1) * block], query_turned, h * mid + g * head_dim)
                for g in range(group)
            ]
            places += [(d_key, key_turned, h * head_dim), (d_value, value_turned, h * head_dim)]
            product = None
            for which, (part, turned_ref, start) in enumerate(places):
                half = part.astype(jnp.bfloat16)
                line = which * rows + slot * block
                delta_ref[h, line : line + block, :] = half
                spot = pl.ds(pl.multiple_of(start, head_dim), head_dim)
                turned_ref[spot, lines] = half.T
                term = half.astype(jnp.float32) * sum_ref[
                    h, lines, which * head_dim : (which + 1) * head_dim
                ]
                product = term if product is None else product + term
            centre_ref[lines, :] += jnp.sum(product, axis=-1, keepdims=True)
        return carry

    lax.fori_loop(0, kv_local, attend, 0)
    lasts = []
    for share, out in zip(shares, delta_hbm):
        for place, block_index in enumerate(share):
            h, which = divmod(block_index, group + 2)
            lasts.append(
                pltpu.make_async_copy(
                    delta_ref.at[h, pl.ds(which * rows, rows), :],
                    out.at[pl.ds(place * rows, rows), :],
                    store_sem.at[1 + len(lasts)],
                )
            )
    for which, turned_ref in enumerate((query_turned, key_turned, value_turned)):
        lasts.append(
            pltpu.make_async_copy(turned_ref, turned_hbm[which], store_sem.at[1 + len(lasts)])
        )
    for store in lasts:
        store.start()

    centre = jnp.broadcast_to(centre_ref[...], (rows, 128)).T[:CENTRE_ROWS].astype(jnp.bfloat16)
    centre_out[...] = centre
    span = width // blocks
    cuts = 2
    cut_lines = span // cuts
    parts = [
        pltpu.make_async_copy(kept.at[place], part_hbm[place], part_sem.at[place])
        for place in range(ready)
    ]

    def project_back(step, carry):
        place, cut = step // cuts, lax.rem(step, cuts)
        lines = pl.ds(pl.multiple_of(order(place) * span + cut * cut_lines, 16), cut_lines)
        total = nn_dot(query_ref[lines, :], query_turned[...])
        total += nn_dot(key_ref[lines, :], key_turned[...])
        total += nn_dot(value_ref[lines, :], value_turned[...])
        spot = pl.ds(pl.multiple_of(cut * cut_lines, 16), cut_lines)
        kept[place, spot, :] = total.astype(jnp.bfloat16)
        for which, part in enumerate(parts):

            @pl.when((place == which) & (cut == cuts - 1))
            def _():
                kept[which, span:, :] = centre
                part.start()

        return carry

    lax.fori_loop(0, ready * cuts, project_back, 0)
    for store in stores + lasts + parts:
        store.wait()


def attention_backward(
    layer_input,
    inverse,
    norm_gain,
    w_query,
    w_key,
    w_value,
    head_grad,
    parents,
    counts,
    slots,
    order,
    blocks,
    ready,
    shares,
):
    rows, width = layer_input.shape
    kv_local = w_key.shape[1] // HEAD_DIM
    group = w_query.shape[1] // w_key.shape[1]
    span = (group + 2) * HEAD_DIM
    stack = (group + 2) * rows
    column_width = width // blocks
    cut = column_width % 128 == 0
    wide = column_width if cut else 128
    steps = 2 if width % 512 == 0 else 1
    part_shape = (column_width + CENTRE_ROWS, rows)
    hbm = pl.BlockSpec(memory_space=pl.ANY)
    vmem = pl.BlockSpec(memory_space=pltpu.VMEM)
    half = lambda *shape: jax.ShapeDtypeStruct(shape, jnp.bfloat16)
    out = pl.pallas_call(
        functools.partial(
            attention_kernel,
            slots,
            group,
            kv_local,
            order,
            blocks,
            ready,
            wide if cut else 0,
            shares,
        ),
        out_shape=tuple(half(len(share) * rows, HEAD_DIM) for share in shares)
        + (half(*part_shape),) * ready
        + tuple(half(w.shape[1], rows) for w in (w_query, w_key, w_value))
        + (half(CENTRE_ROWS, rows),)
        + (half(rows, wide), jax.ShapeDtypeStruct((1, wide), jnp.float32)),
        in_specs=[pl.BlockSpec(memory_space=pltpu.SMEM), vmem, vmem, vmem] + [hbm] * 5,
        out_specs=(hbm,) * (len(shares) + ready + 3) + (vmem, hbm, vmem),
        scratch_shapes=[
            pltpu.VMEM((rows, width), jnp.bfloat16),
            pltpu.VMEM((1, width), jnp.float32),
            pltpu.VMEM(w_query.shape, jnp.bfloat16),
            pltpu.VMEM(w_key.shape, jnp.bfloat16),
            pltpu.VMEM(w_value.shape, jnp.bfloat16),
            pltpu.VMEM(head_grad.shape, jnp.bfloat16),
            pltpu.VMEM((kv_local, rows, span), jnp.float32),
            pltpu.VMEM((kv_local, stack, HEAD_DIM), jnp.bfloat16),
            pltpu.VMEM((w_query.shape[1], rows), jnp.bfloat16),
            pltpu.VMEM((w_key.shape[1], rows), jnp.bfloat16),
            pltpu.VMEM((w_value.shape[1], rows), jnp.bfloat16),
            pltpu.VMEM((slots, rows // slots, rows // slots), jnp.float32),
            pltpu.VMEM((rows, 1), jnp.float32),
            pltpu.VMEM((ready, *part_shape), jnp.bfloat16),
            pltpu.SemaphoreType.DMA((2,)),
            pltpu.SemaphoreType.DMA((steps, 3)),
            pltpu.SemaphoreType.DMA((4 + kv_local * (group + 2),)),
            pltpu.SemaphoreType.DMA((ready,)),
        ],
        compiler_params=pltpu.CompilerParams(vmem_limit_bytes=VMEM_LIMIT),
        cost_estimate=small_cost(),
        name="attention",
    )(counts, parents, inverse, norm_gain, layer_input, w_query, w_key, w_value, head_grad)
    deltas, out = out[: len(shares)], out[len(shares) :]
    parts, turned, centre = out[:ready], out[ready : ready + 3], out[ready + 3]
    if cut:
        input_cut, gain_cut = out[-2], out[-1]
    else:
        start = lax.axis_index("tensor") * column_width
        input_cut = lax.dynamic_slice_in_dim(layer_input, start, column_width, 1)
        gain_cut = lax.dynamic_slice_in_dim(norm_gain, start, column_width, 0)
        gain_cut = gain_cut.reshape(1, column_width)
    return deltas, parts, turned, centre, input_cut, gain_cut


def back_kernel(centre_ref, *refs):
    turned_refs, weight_refs, out_refs = refs[:3], refs[3:6], refs[6:]
    piece, cut = pl.program_id(0), pl.program_id(1)
    lines = weight_refs[0].shape[0]
    total = None
    for weight_ref, turned_ref in zip(weight_refs, turned_refs):
        term = nn_dot(weight_ref[...], turned_ref[...])
        total = term if total is None else total + term
    total = total.astype(jnp.bfloat16)
    start = pl.multiple_of(cut * lines, 16)
    depth = out_refs[0].shape[0] - CENTRE_ROWS
    for place, out_ref in enumerate(out_refs):

        @pl.when(piece == place)
        def _():
            out_ref[pl.ds(start, lines), :] = total
            out_ref[depth:, :] = centre_ref[...]


def back_project(order, first, pieces, turned, centre, weights, blocks):
    rows = centre.shape[1]
    depth = weights[0].shape[0] // blocks
    cuts = 2
    whole = lambda i, j: (0, 0)
    return pl.pallas_call(
        back_kernel,
        out_shape=(jax.ShapeDtypeStruct((depth + CENTRE_ROWS, rows), jnp.bfloat16),) * pieces,
        grid=(pieces, cuts),
        in_specs=[pl.BlockSpec(x.shape, whole) for x in (centre, *turned)]
        + [
            pl.BlockSpec((depth // cuts, w.shape[1]), lambda i, j: (order(first + i) * cuts + j, 0))
            for w in weights
        ],
        out_specs=(pl.BlockSpec((depth + CENTRE_ROWS, rows), whole),) * pieces,
        compiler_params=pltpu.CompilerParams(vmem_limit_bytes=VMEM_LIMIT),
        cost_estimate=small_cost(),
        name="back",
    )(centre, *turned, *weights)


def weight_kernel(outs, sources, *refs):
    turned_hbm, delta_hbm = refs[:sources], refs[sources : 2 * sources]
    out_hbm, token_ref = refs[-10:-7], refs[-7]
    turned_ref, delta_ref, kept, turned_sem, delta_sem, store_sem = refs[-6:]
    token_ref[...] = jnp.zeros_like(token_ref)
    rows = turned_ref.shape[2]
    loads = []
    for place in range(sources):
        loads.append(
            pltpu.make_async_copy(
                turned_hbm[place], turned_ref.at[place], turned_sem.at[place]
            )
        )
        loads.append(
            pltpu.make_async_copy(delta_hbm[place], delta_ref.at[place], delta_sem.at[place])
        )
    for load in loads:
        load.start()
    for load in loads:
        load.wait()
    stores = [
        pltpu.make_async_copy(
            kept.at[block],
            out_hbm[which].at[:, pl.ds(column * HEAD_DIM, HEAD_DIM)],
            store_sem.at[block],
        )
        for block, (which, column) in enumerate(outs)
    ]

    def fill(block, carry):
        lines = pl.ds(pl.multiple_of(block * rows, rows), rows)
        total = None
        for place in range(sources):
            term = nn_dot(turned_ref[place], delta_ref[place, lines, :])
            total = term if total is None else total + term
        kept[block] = total
        for which, store in enumerate(stores):

            @pl.when(block == which)
            def _():
                store.start()

        return carry

    lax.fori_loop(0, len(outs), fill, 0)
    for store in stores:
        store.wait()


def weight_gradients(turned, deltas, share, kv_local, group, before):
    depth, rows = turned[0].shape
    sources = len(turned)
    outs = []
    for block in share:
        h, which = divmod(block, group + 2)
        outs.append((0, h * group + which) if which < group else (which - group + 1, h))
    kept = list(before) if before is not None else []
    hbm = pl.BlockSpec(memory_space=pl.ANY)
    return pl.pallas_call(
        functools.partial(weight_kernel, outs, sources),
        out_shape=(
            jax.ShapeDtypeStruct((depth, kv_local * group * HEAD_DIM), jnp.float32),
            jax.ShapeDtypeStruct((depth, kv_local * HEAD_DIM), jnp.float32),
            jax.ShapeDtypeStruct((depth, kv_local * HEAD_DIM), jnp.float32),
            jax.ShapeDtypeStruct((8, 128), jnp.float32),
        ),
        in_specs=[hbm] * (2 * sources + len(kept)),
        out_specs=(hbm,) * 3 + (pl.BlockSpec(memory_space=pltpu.VMEM),),
        input_output_aliases={2 * sources + i: i for i in range(len(kept))},
        scratch_shapes=[
            pltpu.VMEM((sources, depth, rows), jnp.bfloat16),
            pltpu.VMEM((sources, len(share) * rows, HEAD_DIM), jnp.bfloat16),
            pltpu.VMEM((len(share), depth, HEAD_DIM), jnp.float32),
            pltpu.SemaphoreType.DMA((sources,)),
            pltpu.SemaphoreType.DMA((sources,)),
            pltpu.SemaphoreType.DMA((len(share),)),
        ],
        compiler_params=pltpu.CompilerParams(vmem_limit_bytes=VMEM_LIMIT),
        cost_estimate=small_cost(),
        name="weights",
    )(*turned, *deltas, *kept)


def gate_kernel(*refs):
    del refs


def gate(arrays, tokens):
    hbm = pl.BlockSpec(memory_space=pl.ANY)
    return pl.pallas_call(
        gate_kernel,
        out_shape=tuple(jax.ShapeDtypeStruct(x.shape, x.dtype) for x in arrays),
        in_specs=[hbm] * (len(arrays) + len(tokens)),
        out_specs=(hbm,) * len(arrays),
        input_output_aliases={i: i for i in range(len(arrays))},
        compiler_params=pltpu.CompilerParams(vmem_limit_bytes=VMEM_LIMIT),
        cost_estimate=small_cost(),
        name="gate",
    )(*arrays, *tokens)


def join_kernel(inner_ref, other_ref, end_ref, *rest):
    out_ref, token_ref = rest[-2:]
    token_ref[...] = jnp.zeros_like(token_ref)
    index = lax.axis_index("tensor")
    inner = (index > 0) & (index < lax.axis_size("tensor") - 1)

    @pl.when(inner)
    def _():
        out_ref[...] = (
            inner_ref[...].astype(jnp.float32) + other_ref[...].astype(jnp.float32)
        ).astype(jnp.bfloat16)

    @pl.when(jnp.logical_not(inner))
    def _():
        out_ref[...] = end_ref[...]


def join(inner_part, other, end_part, tokens):
    vmem = pl.BlockSpec(memory_space=pltpu.VMEM)
    return pl.pallas_call(
        join_kernel,
        out_shape=(
            jax.ShapeDtypeStruct(end_part.shape, end_part.dtype),
            jax.ShapeDtypeStruct((8, 128), jnp.float32),
        ),
        in_specs=[vmem] * 3 + [pl.BlockSpec(memory_space=pl.ANY)] * len(tokens),
        out_specs=(vmem, vmem),
        compiler_params=pltpu.CompilerParams(vmem_limit_bytes=VMEM_LIMIT),
        cost_estimate=small_cost(),
        name="join",
    )(inner_part, other, end_part, *tokens)


def add_parts(for_ends, for_inner, part_refs):
    index = lax.axis_index("tensor")
    ends = ((index == 0) | (index == lax.axis_size("tensor") - 1)).astype(jnp.float32)
    total = None
    for place, part_ref in enumerate(part_refs):
        part = part_ref[...].astype(jnp.float32)
        if place < for_ends:
            part = part * ends
        elif place < for_ends + for_inner:
            part = part * (1.0 - ends)
        total = part if total is None else total + part
    return total


def gain_kernel(add, count, input_ref, inverse_ref, *refs):
    part_refs, (sum_ref, total_ref) = refs[:count], refs[-2:]

    @pl.when(pl.program_id(0) == 0)
    def _():
        sum_ref[...] = jnp.zeros_like(sum_ref)

    d_normed = add(part_refs).T
    total_ref[...] = d_normed
    scaled = input_ref[...].astype(jnp.float32) * inverse_ref[...]
    sum_ref[...] += jnp.sum(d_normed * scaled, axis=0, keepdims=True)


def gain_sums(add, input_columns, inverse, parts, token):
    rows, wide = input_columns.shape
    some = 128
    return pl.pallas_call(
        functools.partial(gain_kernel, add, len(parts)),
        out_shape=(
            jax.ShapeDtypeStruct((1, wide), jnp.float32),
            jax.ShapeDtypeStruct((rows, wide), jnp.float32),
        ),
        grid=(rows // some,),
        in_specs=[
            pl.BlockSpec((some, wide), lambda i: (i, 0)),
            pl.BlockSpec((some, 1), lambda i: (i, 0)),
        ]
        + [pl.BlockSpec((wide, some), lambda i: (0, i))] * len(parts)
        + [pl.BlockSpec(memory_space=pl.ANY)],
        out_specs=(
            pl.BlockSpec((1, wide), lambda i: (0, 0)),
            pl.BlockSpec((some, wide), lambda i: (i, 0)),
        ),
        compiler_params=pltpu.CompilerParams(vmem_limit_bytes=VMEM_LIMIT),
        cost_estimate=small_cost(),
        name="gains",
    )(input_columns, inverse, *parts, token)


def finish_kernel(width, add, total_ref, input_ref, gain_ref, inverse_ref, *refs):
    centre_refs, out_ref = refs[:-1], refs[-1]
    centre = add(centre_refs).T[:, :1] * (1.0 / width)
    inverse = inverse_ref[...]
    scaled = input_ref[...].astype(jnp.float32) * inverse
    out_ref[...] = (
        inverse * ((1.0 + gain_ref[...]) * total_ref[...] - scaled * centre)
    ).astype(jnp.bfloat16)


def finish(width, add, total, input_columns, gain_columns, inverse, parts):
    rows, wide = input_columns.shape
    some = 128
    row_block = pl.BlockSpec((some, wide), lambda i: (i, 0))
    return pl.pallas_call(
        functools.partial(finish_kernel, width, add),
        out_shape=jax.ShapeDtypeStruct((rows, wide), jnp.bfloat16),
        grid=(rows // some,),
        in_specs=[
            row_block,
            row_block,
            pl.BlockSpec((1, wide), lambda i: (0, 0)),
            pl.BlockSpec((some, 1), lambda i: (i, 0)),
        ]
        + [pl.BlockSpec((CENTRE_ROWS, some), lambda i: (wide // CENTRE_ROWS, i))] * len(parts),
        out_specs=row_block,
        compiler_params=pltpu.CompilerParams(vmem_limit_bytes=VMEM_LIMIT),
        cost_estimate=small_cost(),
        name="finish",
    )(total, input_columns, gain_columns, inverse, *parts)


def total_kernel(*refs):
    total = (refs[0][...] + refs[1][...]) + (refs[2][...] + refs[3][...])
    refs[-1][...] = total.reshape(refs[-1].shape)


def total_of_four(arrays, token):
    whole = pl.BlockSpec(arrays[0].shape, lambda i: (0, 0))
    wide = arrays[0].shape[1]
    return pl.pallas_call(
        total_kernel,
        out_shape=jax.ShapeDtypeStruct((wide,), arrays[0].dtype),
        grid=(1,),
        in_specs=[whole] * 4 + [pl.BlockSpec(memory_space=pl.ANY)],
        out_specs=pl.BlockSpec((wide,), lambda i: (0,)),
        compiler_params=pltpu.CompilerParams(vmem_limit_bytes=VMEM_LIMIT),
        cost_estimate=small_cost(),
        name="total",
    )(*arrays, token)


def branch_send(array, chips, shift, swap):
    pairs = [
        (c * 2 + k, ((c + shift) % chips) * 2 + (k ^ swap)) for c in range(chips) for k in range(2)
    ]
    return lax.ppermute(array, "branch", pairs)


def pick(table, index):
    chosen = table[-1]
    for place in range(len(table) - 2, -1, -1):
        chosen = jnp.where(index == place, table[place], chosen)
    return chosen


def scatter_order(total):
    index = lax.axis_index("tensor")
    if total != 4:
        return lambda place: lax.rem(index + place + 1, total)
    table = [[3, 0, 3, 0], [0, 2, 1, 3], [2, 3, 0, 1], [1, 1, 2, 2]]
    here = [pick(row, index) for row in table]
    return lambda place: pick(here, place)


def scatter_begin(parts, total):
    if total != 4:
        return [
            lax.ppermute(part, "tensor", [(t, (t + shift) % total) for t in range(total)])
            for shift, part in zip(range(1, total), parts[:-1])
        ]
    from_first = lax.ppermute(parts[0], "tensor", [(0, 1), (1, 0), (2, 3), (3, 2)])
    from_inner = lax.ppermute(parts[1], "tensor", [(1, 2), (2, 1)])
    from_ends = lax.ppermute(parts[2], "tensor", [(0, 2), (3, 1)])
    return from_first, from_inner, from_ends


def scatter_end(parts, arrived, total):
    if total != 4:
        return [parts[-1], *arrived], 0, 0, arrived[0]
    from_first, from_inner, from_ends = arrived
    joined, token = join(parts[2], from_first, parts[3], (from_inner, from_ends))
    from_joined = lax.ppermute(joined, "tensor", [(1, 3), (2, 0), (0, 1), (3, 2)])
    return [from_first, parts[1], parts[3], from_inner, from_ends, from_joined], 2, 1, token


def local(layer_input, norm_gain, w_query, w_key, w_value, head_grad, parents, row_counts):
    branch_total = lax.axis_size("branch")
    tensor_total = lax.axis_size("tensor")
    slots = row_counts.shape[0] // branch_total
    rows, width = layer_input.shape
    column_width = width // tensor_total
    chips = branch_total // 2
    group = w_query.shape[1] // w_key.shape[1]
    kv_local = w_key.shape[1] // HEAD_DIM
    offsets = [(shift, swap) for shift in range(chips) for swap in range(2)]
    blocks = list(range(kv_local * (group + 2)))
    early = blocks[: group + 2] + [h * (group + 2) + group for h in range(1, kv_local)]
    shares = [early, [block for block in blocks if block not in early]]
    shares = [share for share in shares if share]

    def targets():
        index = lax.axis_index("branch")
        chip, core = index // 2, index % 2
        return [lax.rem(chip + s, chips) * 2 + lax.rem(core + e, 2) for s, e in offsets]

    inverse, pieces = normalize(layer_input, norm_gain, targets, branch_total, rows // slots)
    near = branch_send(pieces[1], chips, 0, 1)
    direct = [branch_send(pieces[2 * s], chips, s, 0) for s in range(1, chips)]
    across = [branch_send(pieces[2 * s + 1], chips, s, 1) for s in range(1, chips)]
    turned = [pieces[0]] + direct + [near] + across
    order = lambda place: scatter_order(tensor_total)(place)
    ready = min(3, tensor_total)
    deltas, parts, delta_turned, centre, input_columns, gain_columns = attention_backward(
        layer_input,
        inverse,
        norm_gain,
        w_query,
        w_key,
        w_value,
        head_grad,
        parents,
        row_counts,
        slots,
        order,
        tensor_total,
        ready,
        shares,
    )
    if ready < tensor_total:
        weights = (w_query, w_key, w_value)
        parts += back_project(
            order, ready, tensor_total - ready, delta_turned, centre, weights, tensor_total
        )
    arrived = scatter_begin(parts, tensor_total)

    (first,) = gate(deltas[:1], (near, *direct, *across))
    sent = [branch_send(first, chips, s, 0) for s in range(1, chips)]
    parts, for_ends, for_inner, met = scatter_end(parts, arrived, tensor_total)
    *sent, first = gate((*sent, first), parts[2:3])
    others = gate(deltas[1:], (sent[0],)) if deltas[1:] else ()
    weights, tokens = None, []
    for share, delta in zip(shares, (first, *others)):
        if tokens:
            sent = [branch_send(delta, chips, s, 0) for s in range(1, chips)]
            delta, *sent = gate((delta, *sent), ())
        gathered = [delta] + sent
        gathered += [branch_send(part, chips, 0, 1) for part in gathered]
        *weights, token = weight_gradients(turned, gathered, share, kv_local, group, weights)
        tokens.append(token)

    add = functools.partial(add_parts, for_ends, for_inner)
    gain_sum, total = gain_sums(add, input_columns, inverse, parts, tokens[-1])
    grad_input = finish(width, add, total, input_columns, gain_columns, inverse, parts)
    if chips == 2:
        sums = [gain_sum] + [branch_send(gain_sum, chips, s, e) for s, e in offsets[1:]]
        grad_gain = total_of_four(sums, tokens[-1])
    else:
        grad_gain = lax.psum(gain_sum, "branch").reshape(column_width)
    return (grad_input, *weights, grad_gain)


def solution(mesh):
    placed = (
        P(("parts", "branch"), None),
        P(),
        P(None, "tensor"),
        P(None, "tensor"),
        P(None, "tensor"),
        P(("parts", "branch"), "tensor"),
        P(("parts", "branch")),
        P("parts"),
    )
    return jax.shard_map(
        local,
        mesh=mesh,
        in_specs=placed,
        out_specs=(
            P(("parts", "branch"), "tensor"),
            P(("parts", "branch"), "tensor"),
            P(("parts", "branch"), "tensor"),
            P(("parts", "branch"), "tensor"),
            P(("parts", "tensor")),
        ),
        check_vma=False,
    )
```

```python
import functools

import jax
import jax.numpy as jnp
from jax import lax
from jax.experimental import pallas as pl
from jax.experimental.pallas import tpu as pltpu
from jax.sharding import PartitionSpec as P

HEAD_DIM = 256
MIB = 1024 * 1024
CENTRE_ROWS = 16
VMEM_LIMIT = 64 * MIB


epsilon = 1e-06
softcap_limit = 50.0


def nn_dot(left, right):
    return lax.dot_general(
        left, right, (((1,), (0,)), ((), ())), preferred_element_type=jnp.float32
    )


def nt_dot(left, right):
    return lax.dot_general(
        left, right, (((1,), (1,)), ((), ())), preferred_element_type=jnp.float32
    )


def tn_dot(left, right):
    return lax.dot_general(
        left, right, (((0,), (0,)), ((), ())), preferred_element_type=jnp.float32
    )


def small_cost():
    return pl.CostEstimate(flops=1000000, bytes_accessed=100000, transcendentals=0)


def norm_kernel(targets, input_ref, gain_ref, inverse_ref, *rest):
    piece_refs, turned = rest[:-1], rest[-1]
    rows, width = input_ref.shape
    values = input_ref[...].astype(jnp.float32)
    inverse = lax.rsqrt(jnp.mean(values * values, axis=-1, keepdims=True) + epsilon)
    inverse_ref[...] = inverse
    gain = gain_ref[...].reshape(1, width)
    turned[...] = (values * inverse * (1.0 + gain)).astype(jnp.bfloat16).T
    depth = width // len(piece_refs)
    for target, piece_ref in zip(targets(), piece_refs):
        start = pl.multiple_of(target * depth, 16)
        piece_ref[...] = turned[pl.ds(start, depth), :]


def normalize(layer_input, norm_gain, targets, pieces, block):
    rows, width = layer_input.shape
    depth = width // pieces
    out = pl.pallas_call(
        functools.partial(norm_kernel, targets),
        out_shape=(jax.ShapeDtypeStruct((rows, 1), jnp.float32),)
        + (jax.ShapeDtypeStruct((depth, rows), jnp.bfloat16),) * pieces,
        grid=(rows // block,),
        in_specs=[
            pl.BlockSpec((block, width), lambda i: (i, 0)),
            pl.BlockSpec((width,), lambda i: (0,)),
        ],
        out_specs=(pl.BlockSpec((block, 1), lambda i: (i, 0)),)
        + (pl.BlockSpec((depth, block), lambda i: (0, i)),) * pieces,
        scratch_shapes=[pltpu.VMEM((width, block), jnp.bfloat16)],
        compiler_params=pltpu.CompilerParams(vmem_limit_bytes=VMEM_LIMIT),
        cost_estimate=small_cost(),
        name="norm",
    )(layer_input, norm_gain)
    return out[0], out[1:]


def ancestor_mask(parent_row):
    rows = parent_row.shape[1]
    row = lax.broadcasted_iota(jnp.int32, (rows, rows), 0)
    column = lax.broadcasted_iota(jnp.int32, (rows, rows), 1)
    reached = jnp.where((parent_row == row) | (row == column), 1.0, 0.0)
    for squaring in range(rows.bit_length() - 1):
        halfway = reached.astype(jnp.bfloat16)
        reached = jnp.minimum(nn_dot(halfway, halfway), 1.0)
    return reached.T


def attention_kernel(
    slots,
    group,
    kv_local,
    order,
    blocks,
    ready,
    columns,
    shares,
    count_ref,
    parent_ref,
    inverse_ref,
    gain_ref,
    input_hbm,
    query_hbm,
    key_hbm,
    value_hbm,
    grad_hbm,
    *rest,
):
    delta_hbm, rest = rest[: len(shares)], rest[len(shares) :]
    part_hbm, rest = rest[:ready], rest[ready:]
    turned_hbm, centre_out, rest = rest[:3], rest[3], rest[4:]
    column_hbm, column_gain_ref, rest = rest[0], rest[1], rest[2:]
    (
        input_ref,
        gain_row,
        query_ref,
        key_ref,
        value_ref,
        grad_ref,
        sum_ref,
        delta_ref,
        query_turned,
        key_turned,
        value_turned,
        allowed_ref,
        centre_ref,
        kept,
        load_sem,
        weight_sem,
        store_sem,
        part_sem,
    ) = rest
    head_dim = HEAD_DIM
    rows, width = input_ref.shape
    block = rows // slots
    mid = group * head_dim
    steps = weight_sem.shape[0]
    chunk = width // steps
    weights = ((query_hbm, query_ref, mid, 0), (key_hbm, key_ref, head_dim, mid))
    weights += ((value_hbm, value_ref, head_dim, mid + head_dim),)

    def fetch(step, which):
        lines = pl.ds(step * chunk, chunk)
        source, kept_ref = weights[which][:2]
        return pltpu.make_async_copy(
            source.at[lines, :], kept_ref.at[lines, :], weight_sem.at[step, which]
        )

    input_load = pltpu.make_async_copy(input_hbm, input_ref, load_sem.at[0])
    grad_load = pltpu.make_async_copy(grad_hbm, grad_ref, load_sem.at[1])
    input_load.start()
    for step in range(steps):
        for which in range(3):
            fetch(step, which).start()
    grad_load.start()
    gain_row[...] = gain_ref[...].reshape(1, width)

    first_count = lax.axis_index("branch") * slots
    parents = parent_ref[...].reshape(1, rows)
    for slot in range(slots):
        allowed_ref[slot] = ancestor_mask(parents[:, slot * block : (slot + 1) * block])
    inverse = inverse_ref[...]
    input_load.wait()
    stores = []
    if columns:
        start = pl.multiple_of(lax.axis_index("tensor") * columns, 128)
        stores.append(
            pltpu.make_async_copy(
                input_ref.at[:, pl.ds(start, columns)], column_hbm, store_sem.at[0]
            )
        )
        stores[0].start()
        column_gain_ref[...] = gain_row[:, pl.ds(start, columns)]
    else:
        column_gain_ref[...] = jnp.zeros_like(column_gain_ref)

    for step in range(steps):
        lines = slice(step * chunk, (step + 1) * chunk)
        gain = 1.0 + gain_row[:, lines]
        normed = (input_ref[:, lines].astype(jnp.float32) * inverse * gain).astype(jnp.bfloat16)
        for which, (_, kept_ref, wide, place) in enumerate(weights):
            fetch(step, which).wait()
            term = nn_dot(normed, kept_ref[lines, :])
            for h in range(kv_local):
                part = term[:, h * wide : (h + 1) * wide]
                if step > 0:
                    part = part + sum_ref[h, :, place : place + wide]
                sum_ref[h, :, place : place + wide] = part
    grad_load.wait()
    scale = head_dim ** (-0.5)
    centre_ref[...] = jnp.zeros_like(centre_ref)

    def attend(h, carry):
        for slot in range(slots):
            lines = slice(slot * block, (slot + 1) * block)
            live = (
                lax.broadcasted_iota(jnp.int32, (block, mid), 0) < count_ref[first_count + slot]
            )
            columns = pl.ds(pl.multiple_of(h * mid, mid), mid)
            grad_rows = jnp.where(live, grad_ref[lines, columns].astype(jnp.float32), 0.0)
            pair = [slice(g * head_dim, (g + 1) * head_dim) for g in range(group)]
            grads = jnp.concatenate([grad_rows[:, p] for p in pair], axis=0).astype(jnp.bfloat16)
            queries = jnp.concatenate([sum_ref[h, lines, p] for p in pair], axis=0)
            queries = queries.astype(jnp.bfloat16)
            keys = sum_ref[h, lines, mid : mid + head_dim].astype(jnp.bfloat16)
            values = sum_ref[h, lines, mid + head_dim :].astype(jnp.bfloat16)
            allowed = jnp.concatenate([allowed_ref[slot]] * group, axis=0)
            bounded = jnp.tanh(nt_dot(queries, keys) * (scale / softcap_limit))
            weighted = allowed * jnp.exp(softcap_limit * bounded)
            probabilities = weighted * (1.0 / jnp.sum(weighted, axis=-1, keepdims=True))
            d_probs = nt_dot(grads, values)
            d_scores = probabilities * (
                d_probs - jnp.sum(probabilities * d_probs, axis=-1, keepdims=True)
            )
            d_raw = (d_scores * (1.0 - bounded * bounded) * scale).astype(jnp.bfloat16)
            prob_half = probabilities.astype(jnp.bfloat16)
            d_query = nn_dot(d_raw, keys)
            d_key = tn_dot(d_raw, queries)
            d_value = tn_dot(prob_half, grads)
            places = [
                (d_query[g * block : (g + 1) * block], query_turned, h * mid + g * head_dim)
                for g in range(group)
            ]
            places += [(d_key, key_turned, h * head_dim), (d_value, value_turned, h * head_dim)]
            product = None
            for which, (part, turned_ref, start) in enumerate(places):
                half = part.astype(jnp.bfloat16)
                line = which * rows + slot * block
                delta_ref[h, line : line + block, :] = half
                spot = pl.ds(pl.multiple_of(start, head_dim), head_dim)
                turned_ref[spot, lines] = half.T
                term = half.astype(jnp.float32) * sum_ref[
                    h, lines, which * head_dim : (which + 1) * head_dim
                ]
                product = term if product is None else product + term
            centre_ref[lines, :] += jnp.sum(product, axis=-1, keepdims=True)
        return carry

    lax.fori_loop(0, kv_local, attend, 0)
    lasts = []
    for share, out in zip(shares, delta_hbm):
        for place, block_index in enumerate(share):
            h, which = divmod(block_index, group + 2)
            lasts.append(
                pltpu.make_async_copy(
                    delta_ref.at[h, pl.ds(which * rows, rows), :],
                    out.at[pl.ds(place * rows, rows), :],
                    store_sem.at[1 + len(lasts)],
                )
            )
    for which, turned_ref in enumerate((query_turned, key_turned, value_turned)):
        lasts.append(
            pltpu.make_async_copy(turned_ref, turned_hbm[which], store_sem.at[1 + len(lasts)])
        )
    for store in lasts:
        store.start()

    centre = jnp.broadcast_to(centre_ref[...], (rows, 128)).T[:CENTRE_ROWS].astype(jnp.bfloat16)
    centre_out[...] = centre
    span = width // blocks
    cuts = 2
    cut_lines = span // cuts
    parts = [
        pltpu.make_async_copy(kept.at[place], part_hbm[place], part_sem.at[place])
        for place in range(ready)
    ]

    def project_back(step, carry):
        place, cut = step // cuts, lax.rem(step, cuts)
        lines = pl.ds(pl.multiple_of(order(place) * span + cut * cut_lines, 16), cut_lines)
        total = nn_dot(query_ref[lines, :], query_turned[...])
        total += nn_dot(key_ref[lines, :], key_turned[...])
        total += nn_dot(value_ref[lines, :], value_turned[...])
        spot = pl.ds(pl.multiple_of(cut * cut_lines, 16), cut_lines)
        kept[place, spot, :] = total.astype(jnp.bfloat16)
        for which, part in enumerate(parts):

            @pl.when((place == which) & (cut == cuts - 1))
            def _():
                kept[which, span:, :] = centre
                part.start()

        return carry

    lax.fori_loop(0, ready * cuts, project_back, 0)
    for store in stores + lasts + parts:
        store.wait()


def attention_backward(
    layer_input,
    inverse,
    norm_gain,
    w_query,
    w_key,
    w_value,
    head_grad,
    parents,
    counts,
    slots,
    order,
    blocks,
    ready,
    shares,
):
    rows, width = layer_input.shape
    kv_local = w_key.shape[1] // HEAD_DIM
    group = w_query.shape[1] // w_key.shape[1]
    span = (group + 2) * HEAD_DIM
    stack = (group + 2) * rows
    column_width = width // blocks
    cut = column_width % 128 == 0
    wide = column_width if cut else 128
    steps = 2 if width % 512 == 0 else 1
    part_shape = (column_width + CENTRE_ROWS, rows)
    hbm = pl.BlockSpec(memory_space=pl.ANY)
    vmem = pl.BlockSpec(memory_space=pltpu.VMEM)
    half = lambda *shape: jax.ShapeDtypeStruct(shape, jnp.bfloat16)
    out = pl.pallas_call(
        functools.partial(
            attention_kernel,
            slots,
            group,
            kv_local,
            order,
            blocks,
            ready,
            wide if cut else 0,
            shares,
        ),
        out_shape=tuple(half(len(share) * rows, HEAD_DIM) for share in shares)
        + (half(*part_shape),) * ready
        + tuple(half(w.shape[1], rows) for w in (w_query, w_key, w_value))
        + (half(CENTRE_ROWS, rows),)
        + (half(rows, wide), jax.ShapeDtypeStruct((1, wide), jnp.float32)),
        in_specs=[pl.BlockSpec(memory_space=pltpu.SMEM), vmem, vmem, vmem] + [hbm] * 5,
        out_specs=(hbm,) * (len(shares) + ready + 3) + (vmem, hbm, vmem),
        scratch_shapes=[
            pltpu.VMEM((rows, width), jnp.bfloat16),
            pltpu.VMEM((1, width), jnp.float32),
            pltpu.VMEM(w_query.shape, jnp.bfloat16),
            pltpu.VMEM(w_key.shape, jnp.bfloat16),
            pltpu.VMEM(w_value.shape, jnp.bfloat16),
            pltpu.VMEM(head_grad.shape, jnp.bfloat16),
            pltpu.VMEM((kv_local, rows, span), jnp.float32),
            pltpu.VMEM((kv_local, stack, HEAD_DIM), jnp.bfloat16),
            pltpu.VMEM((w_query.shape[1], rows), jnp.bfloat16),
            pltpu.VMEM((w_key.shape[1], rows), jnp.bfloat16),
            pltpu.VMEM((w_value.shape[1], rows), jnp.bfloat16),
            pltpu.VMEM((slots, rows // slots, rows // slots), jnp.float32),
            pltpu.VMEM((rows, 1), jnp.float32),
            pltpu.VMEM((ready, *part_shape), jnp.bfloat16),
            pltpu.SemaphoreType.DMA((2,)),
            pltpu.SemaphoreType.DMA((steps, 3)),
            pltpu.SemaphoreType.DMA((4 + kv_local * (group + 2),)),
            pltpu.SemaphoreType.DMA((ready,)),
        ],
        compiler_params=pltpu.CompilerParams(vmem_limit_bytes=VMEM_LIMIT),
        cost_estimate=small_cost(),
        name="attention",
    )(counts, parents, inverse, norm_gain, layer_input, w_query, w_key, w_value, head_grad)
    deltas, out = out[: len(shares)], out[len(shares) :]
    parts, turned, centre = out[:ready], out[ready : ready + 3], out[ready + 3]
    if cut:
        input_cut, gain_cut = out[-2], out[-1]
    else:
        start = lax.axis_index("tensor") * column_width
        input_cut = lax.dynamic_slice_in_dim(layer_input, start, column_width, 1)
        gain_cut = lax.dynamic_slice_in_dim(norm_gain, start, column_width, 0)
        gain_cut = gain_cut.reshape(1, column_width)
    return deltas, parts, turned, centre, input_cut, gain_cut


def back_kernel(centre_ref, *refs):
    turned_refs, weight_refs, out_refs = refs[:3], refs[3:6], refs[6:]
    piece, cut = pl.program_id(0), pl.program_id(1)
    lines = weight_refs[0].shape[0]
    total = None
    for weight_ref, turned_ref in zip(weight_refs, turned_refs):
        term = nn_dot(weight_ref[...], turned_ref[...])
        total = term if total is None else total + term
    total = total.astype(jnp.bfloat16)
    start = pl.multiple_of(cut * lines, 16)
    depth = out_refs[0].shape[0] - CENTRE_ROWS
    for place, out_ref in enumerate(out_refs):

        @pl.when(piece == place)
        def _():
            out_ref[pl.ds(start, lines), :] = total
            out_ref[depth:, :] = centre_ref[...]


def back_project(order, first, pieces, turned, centre, weights, blocks):
    rows = centre.shape[1]
    depth = weights[0].shape[0] // blocks
    cuts = 2
    whole = lambda i, j: (0, 0)
    return pl.pallas_call(
        back_kernel,
        out_shape=(jax.ShapeDtypeStruct((depth + CENTRE_ROWS, rows), jnp.bfloat16),) * pieces,
        grid=(pieces, cuts),
        in_specs=[pl.BlockSpec(x.shape, whole) for x in (centre, *turned)]
        + [
            pl.BlockSpec((depth // cuts, w.shape[1]), lambda i, j: (order(first + i) * cuts + j, 0))
            for w in weights
        ],
        out_specs=(pl.BlockSpec((depth + CENTRE_ROWS, rows), whole),) * pieces,
        compiler_params=pltpu.CompilerParams(vmem_limit_bytes=VMEM_LIMIT),
        cost_estimate=small_cost(),
        name="back",
    )(centre, *turned, *weights)


def weight_kernel(outs, sources, *refs):
    turned_hbm, delta_hbm = refs[:sources], refs[sources : 2 * sources]
    out_hbm, token_ref = refs[-10:-7], refs[-7]
    turned_ref, delta_ref, kept, turned_sem, delta_sem, store_sem = refs[-6:]
    token_ref[...] = jnp.zeros_like(token_ref)
    rows = turned_ref.shape[2]
    loads = []
    for place in range(sources):
        loads.append(
            pltpu.make_async_copy(
                turned_hbm[place], turned_ref.at[place], turned_sem.at[place]
            )
        )
    for load in loads:
        load.start()

    def fetch(block, place):
        lines = pl.ds(pl.multiple_of(block * rows, rows), rows)
        return pltpu.make_async_copy(
            delta_hbm[place].at[lines, :], delta_ref.at[place, lines, :], delta_sem.at[block, place]
        )

    for block in range(len(outs)):
        for place in range(sources):
            fetch(block, place).start()
    for load in loads:
        load.wait()
    stores = [
        pltpu.make_async_copy(
            kept.at[block],
            out_hbm[which].at[:, pl.ds(column * HEAD_DIM, HEAD_DIM)],
            store_sem.at[block],
        )
        for block, (which, column) in enumerate(outs)
    ]

    def fill(block, carry):
        lines = pl.ds(pl.multiple_of(block * rows, rows), rows)
        total = None
        for place in range(sources):
            fetch(block, place).wait()
        for place in range(sources):
            term = nn_dot(turned_ref[place], delta_ref[place, lines, :])
            total = term if total is None else total + term
        kept[block] = total
        for which, store in enumerate(stores):

            @pl.when(block == which)
            def _():
                store.start()

        return carry

    lax.fori_loop(0, len(outs), fill, 0)
    for store in stores:
        store.wait()


def weight_gradients(turned, deltas, share, kv_local, group, before):
    depth, rows = turned[0].shape
    sources = len(turned)
    outs = []
    for block in share:
        h, which = divmod(block, group + 2)
        outs.append((0, h * group + which) if which < group else (which - group + 1, h))
    kept = list(before) if before is not None else []
    hbm = pl.BlockSpec(memory_space=pl.ANY)
    return pl.pallas_call(
        functools.partial(weight_kernel, outs, sources),
        out_shape=(
            jax.ShapeDtypeStruct((depth, kv_local * group * HEAD_DIM), jnp.float32),
            jax.ShapeDtypeStruct((depth, kv_local * HEAD_DIM), jnp.float32),
            jax.ShapeDtypeStruct((depth, kv_local * HEAD_DIM), jnp.float32),
            jax.ShapeDtypeStruct((8, 128), jnp.float32),
        ),
        in_specs=[hbm] * (2 * sources + len(kept)),
        out_specs=(hbm,) * 3 + (pl.BlockSpec(memory_space=pltpu.VMEM),),
        input_output_aliases={2 * sources + i: i for i in range(len(kept))},
        scratch_shapes=[
            pltpu.VMEM((sources, depth, rows), jnp.bfloat16),
            pltpu.VMEM((sources, len(share) * rows, HEAD_DIM), jnp.bfloat16),
            pltpu.VMEM((len(share), depth, HEAD_DIM), jnp.float32),
            pltpu.SemaphoreType.DMA((sources,)),
            pltpu.SemaphoreType.DMA((len(share), sources)),
            pltpu.SemaphoreType.DMA((len(share),)),
        ],
        compiler_params=pltpu.CompilerParams(vmem_limit_bytes=VMEM_LIMIT),
        cost_estimate=small_cost(),
        name="weights",
    )(*turned, *deltas, *kept)


def gate_kernel(*refs):
    del refs


def gate(arrays, tokens):
    hbm = pl.BlockSpec(memory_space=pl.ANY)
    return pl.pallas_call(
        gate_kernel,
        out_shape=tuple(jax.ShapeDtypeStruct(x.shape, x.dtype) for x in arrays),
        in_specs=[hbm] * (len(arrays) + len(tokens)),
        out_specs=(hbm,) * len(arrays),
        input_output_aliases={i: i for i in range(len(arrays))},
        compiler_params=pltpu.CompilerParams(vmem_limit_bytes=VMEM_LIMIT),
        cost_estimate=small_cost(),
        name="gate",
    )(*arrays, *tokens)


def join_kernel(inner_ref, other_ref, end_ref, *rest):
    out_ref = rest[-1]
    index = lax.axis_index("tensor")
    inner = (index > 0) & (index < lax.axis_size("tensor") - 1)

    @pl.when(inner)
    def _():
        out_ref[...] = (
            inner_ref[...].astype(jnp.float32) + other_ref[...].astype(jnp.float32)
        ).astype(jnp.bfloat16)

    @pl.when(jnp.logical_not(inner))
    def _():
        out_ref[...] = end_ref[...]


def join(inner_part, other, end_part, tokens):
    vmem = pl.BlockSpec(memory_space=pltpu.VMEM)
    return pl.pallas_call(
        join_kernel,
        out_shape=jax.ShapeDtypeStruct(end_part.shape, end_part.dtype),
        in_specs=[vmem] * 3 + [pl.BlockSpec(memory_space=pl.ANY)] * len(tokens),
        out_specs=vmem,
        compiler_params=pltpu.CompilerParams(vmem_limit_bytes=VMEM_LIMIT),
        cost_estimate=small_cost(),
        name="join",
    )(inner_part, other, end_part, *tokens)


def add_parts(for_ends, for_inner, part_refs):
    index = lax.axis_index("tensor")
    ends = ((index == 0) | (index == lax.axis_size("tensor") - 1)).astype(jnp.float32)
    total = None
    for place, part_ref in enumerate(part_refs):
        part = part_ref[...].astype(jnp.float32)
        if place < for_ends:
            part = part * ends
        elif place < for_ends + for_inner:
            part = part * (1.0 - ends)
        total = part if total is None else total + part
    return total


def gain_kernel(add, count, input_ref, inverse_ref, *refs):
    part_refs, (sum_ref, total_ref) = refs[:count], refs[-2:]

    @pl.when(pl.program_id(0) == 0)
    def _():
        sum_ref[...] = jnp.zeros_like(sum_ref)

    d_normed = add(part_refs).T
    total_ref[...] = d_normed
    scaled = input_ref[...].astype(jnp.float32) * inverse_ref[...]
    sum_ref[...] += jnp.sum(d_normed * scaled, axis=0, keepdims=True)


def gain_sums(add, input_columns, inverse, parts, token):
    rows, wide = input_columns.shape
    some = 128
    return pl.pallas_call(
        functools.partial(gain_kernel, add, len(parts)),
        out_shape=(
            jax.ShapeDtypeStruct((1, wide), jnp.float32),
            jax.ShapeDtypeStruct((rows, wide), jnp.float32),
        ),
        grid=(rows // some,),
        in_specs=[
            pl.BlockSpec((some, wide), lambda i: (i, 0)),
            pl.BlockSpec((some, 1), lambda i: (i, 0)),
        ]
        + [pl.BlockSpec((wide, some), lambda i: (0, i))] * len(parts)
        + [pl.BlockSpec(memory_space=pl.ANY)],
        out_specs=(
            pl.BlockSpec((1, wide), lambda i: (0, 0)),
            pl.BlockSpec((some, wide), lambda i: (i, 0)),
        ),
        compiler_params=pltpu.CompilerParams(vmem_limit_bytes=VMEM_LIMIT),
        cost_estimate=small_cost(),
        name="gains",
    )(input_columns, inverse, *parts, token)


def finish_kernel(width, add, total_ref, input_ref, gain_ref, inverse_ref, *refs):
    centre_refs, out_ref = refs[:-1], refs[-1]
    centre = add(centre_refs).T[:, :1] * (1.0 / width)
    inverse = inverse_ref[...]
    scaled = input_ref[...].astype(jnp.float32) * inverse
    out_ref[...] = (
        inverse * ((1.0 + gain_ref[...]) * total_ref[...] - scaled * centre)
    ).astype(jnp.bfloat16)


def finish(width, add, total, input_columns, gain_columns, inverse, parts):
    rows, wide = input_columns.shape
    some = 128
    row_block = pl.BlockSpec((some, wide), lambda i: (i, 0))
    return pl.pallas_call(
        functools.partial(finish_kernel, width, add),
        out_shape=jax.ShapeDtypeStruct((rows, wide), jnp.bfloat16),
        grid=(rows // some,),
        in_specs=[
            row_block,
            row_block,
            pl.BlockSpec((1, wide), lambda i: (0, 0)),
            pl.BlockSpec((some, 1), lambda i: (i, 0)),
        ]
        + [pl.BlockSpec((CENTRE_ROWS, some), lambda i: (wide // CENTRE_ROWS, i))] * len(parts),
        out_specs=row_block,
        compiler_params=pltpu.CompilerParams(vmem_limit_bytes=VMEM_LIMIT),
        cost_estimate=small_cost(),
        name="finish",
    )(total, input_columns, gain_columns, inverse, *parts)


def total_kernel(*refs):
    total = (refs[0][...] + refs[1][...]) + (refs[2][...] + refs[3][...])
    refs[-1][...] = total.reshape(refs[-1].shape)


def total_of_four(arrays, token):
    whole = pl.BlockSpec(arrays[0].shape, lambda i: (0, 0))
    wide = arrays[0].shape[1]
    return pl.pallas_call(
        total_kernel,
        out_shape=jax.ShapeDtypeStruct((wide,), arrays[0].dtype),
        grid=(1,),
        in_specs=[whole] * 4 + [pl.BlockSpec(memory_space=pl.ANY)],
        out_specs=pl.BlockSpec((wide,), lambda i: (0,)),
        compiler_params=pltpu.CompilerParams(vmem_limit_bytes=VMEM_LIMIT),
        cost_estimate=small_cost(),
        name="total",
    )(*arrays, token)


def branch_send(array, chips, shift, swap):
    pairs = [
        (c * 2 + k, ((c + shift) % chips) * 2 + (k ^ swap)) for c in range(chips) for k in range(2)
    ]
    return lax.ppermute(array, "branch", pairs)


def pick(table, index):
    chosen = table[-1]
    for place in range(len(table) - 2, -1, -1):
        chosen = jnp.where(index == place, table[place], chosen)
    return chosen


def scatter_order(total):
    index = lax.axis_index("tensor")
    if total != 4:
        return lambda place: lax.rem(index + place + 1, total)
    table = [[3, 0, 3, 0], [0, 2, 1, 3], [2, 3, 0, 1], [1, 1, 2, 2]]
    here = [pick(row, index) for row in table]
    return lambda place: pick(here, place)


def scatter_begin(parts, total):
    if total != 4:
        return [
            lax.ppermute(part, "tensor", [(t, (t + shift) % total) for t in range(total)])
            for shift, part in zip(range(1, total), parts[:-1])
        ]
    from_first = lax.ppermute(parts[0], "tensor", [(0, 1), (1, 0), (2, 3), (3, 2)])
    from_inner = lax.ppermute(parts[1], "tensor", [(1, 2), (2, 1)])
    from_ends = lax.ppermute(parts[2], "tensor", [(0, 2), (3, 1)])
    return from_first, from_inner, from_ends


def scatter_end(parts, arrived, total, tokens):
    if total != 4:
        return [parts[-1], *arrived], 0, 0
    from_first, from_inner, from_ends = arrived
    joined = join(parts[2], from_first, parts[3], (from_inner, from_ends, *tokens))
    from_joined = lax.ppermute(joined, "tensor", [(1, 3), (2, 0), (0, 1), (3, 2)])
    return [from_first, parts[1], parts[3], from_inner, from_ends, from_joined], 2, 1


def local(layer_input, norm_gain, w_query, w_key, w_value, head_grad, parents, row_counts):
    branch_total = lax.axis_size("branch")
    tensor_total = lax.axis_size("tensor")
    slots = row_counts.shape[0] // branch_total
    rows, width = layer_input.shape
    column_width = width // tensor_total
    chips = branch_total // 2
    group = w_query.shape[1] // w_key.shape[1]
    kv_local = w_key.shape[1] // HEAD_DIM
    offsets = [(shift, swap) for shift in range(chips) for swap in range(2)]
    blocks = list(range(kv_local * (group + 2)))
    early = len(blocks) * 3 // 8
    shares = [blocks[:early], blocks[early:]]
    shares = [share for share in shares if share]

    def targets():
        index = lax.axis_index("branch")
        chip, core = index // 2, index % 2
        return [lax.rem(chip + s, chips) * 2 + lax.rem(core + e, 2) for s, e in offsets]

    inverse, pieces = normalize(layer_input, norm_gain, targets, branch_total, rows // slots)
    near = branch_send(pieces[1], chips, 0, 1)
    direct = [branch_send(pieces[2 * s], chips, s, 0) for s in range(1, chips)]
    across = [branch_send(pieces[2 * s + 1], chips, s, 1) for s in range(1, chips)]
    turned = [pieces[0]] + direct + [near] + across
    order = lambda place: scatter_order(tensor_total)(place)
    ready = min(3, tensor_total)
    deltas, parts, delta_turned, centre, input_columns, gain_columns = attention_backward(
        layer_input,
        inverse,
        norm_gain,
        w_query,
        w_key,
        w_value,
        head_grad,
        parents,
        row_counts,
        slots,
        order,
        tensor_total,
        ready,
        shares,
    )
    if ready < tensor_total:
        weights = (w_query, w_key, w_value)
        parts += back_project(
            order, ready, tensor_total - ready, delta_turned, centre, weights, tensor_total
        )
    arrived = scatter_begin(parts, tensor_total)

    deltas = gate(deltas, (near, *direct, *across))
    sent = [[branch_send(delta, chips, s, 0) for s in range(1, chips)] for delta in deltas]
    weights, tokens = None, []
    for share, delta, arrivals in zip(shares, deltas, sent):
        delta, *arrivals = gate((delta, *arrivals), () if tokens else (*parts[3:4], *arrived[:2]))
        gathered = [delta] + arrivals
        gathered += [branch_send(part, chips, 0, 1) for part in gathered]
        *weights, token = weight_gradients(turned, gathered, share, kv_local, group, weights)
        tokens.append(token)
    parts, for_ends, for_inner = scatter_end(parts, arrived, tensor_total, tokens[:1])

    add = functools.partial(add_parts, for_ends, for_inner)
    gain_sum, total = gain_sums(add, input_columns, inverse, parts, tokens[-1])
    grad_input = finish(width, add, total, input_columns, gain_columns, inverse, parts)
    if chips == 2:
        sums = [gain_sum] + [branch_send(gain_sum, chips, s, e) for s, e in offsets[1:]]
        grad_gain = total_of_four(sums, tokens[-1])
    else:
        grad_gain = lax.psum(gain_sum, "branch").reshape(column_width)
    return (grad_input, *weights, grad_gain)


def solution(mesh):
    placed = (
        P(("parts", "branch"), None),
        P(),
        P(None, "tensor"),
        P(None, "tensor"),
        P(None, "tensor"),
        P(("parts", "branch"), "tensor"),
        P(("parts", "branch")),
        P("parts"),
    )
    return jax.shard_map(
        local,
        mesh=mesh,
        in_specs=placed,
        out_specs=(
            P(("parts", "branch"), "tensor"),
            P(("parts", "branch"), "tensor"),
            P(("parts", "branch"), "tensor"),
            P(("parts", "branch"), "tensor"),
            P(("parts", "tensor")),
        ),
        check_vma=False,
    )
```

```python
import functools

import jax
import jax.numpy as jnp
from jax import lax
from jax.experimental import pallas as pl
from jax.experimental.pallas import tpu as pltpu
from jax.sharding import PartitionSpec as P

HEAD_DIM = 256
MIB = 1024 * 1024
CENTRE_ROWS = 16
VMEM_LIMIT = 64 * MIB


epsilon = 1e-06
softcap_limit = 50.0


def nn_dot(left, right):
    return lax.dot_general(
        left, right, (((1,), (0,)), ((), ())), preferred_element_type=jnp.float32
    )


def nt_dot(left, right):
    return lax.dot_general(
        left, right, (((1,), (1,)), ((), ())), preferred_element_type=jnp.float32
    )


def tn_dot(left, right):
    return lax.dot_general(
        left, right, (((0,), (0,)), ((), ())), preferred_element_type=jnp.float32
    )


def small_cost():
    return pl.CostEstimate(flops=1000000, bytes_accessed=100000, transcendentals=0)


def norm_kernel(targets, input_ref, gain_ref, inverse_ref, *rest):
    piece_refs, turned = rest[:-1], rest[-1]
    rows, width = input_ref.shape
    values = input_ref[...].astype(jnp.float32)
    inverse = lax.rsqrt(jnp.mean(values * values, axis=-1, keepdims=True) + epsilon)
    inverse_ref[...] = inverse
    gain = gain_ref[...].reshape(1, width)
    turned[...] = (values * inverse * (1.0 + gain)).astype(jnp.bfloat16).T
    depth = width // len(piece_refs)
    for target, piece_ref in zip(targets(), piece_refs):
        start = pl.multiple_of(target * depth, 16)
        piece_ref[...] = turned[pl.ds(start, depth), :]


def normalize(layer_input, norm_gain, targets, pieces, block):
    rows, width = layer_input.shape
    depth = width // pieces
    out = pl.pallas_call(
        functools.partial(norm_kernel, targets),
        out_shape=(jax.ShapeDtypeStruct((rows, 1), jnp.float32),)
        + (jax.ShapeDtypeStruct((depth, rows), jnp.bfloat16),) * pieces,
        grid=(rows // block,),
        in_specs=[
            pl.BlockSpec((block, width), lambda i: (i, 0)),
            pl.BlockSpec((width,), lambda i: (0,)),
        ],
        out_specs=(pl.BlockSpec((block, 1), lambda i: (i, 0)),)
        + (pl.BlockSpec((depth, block), lambda i: (0, i)),) * pieces,
        scratch_shapes=[pltpu.VMEM((width, block), jnp.bfloat16)],
        compiler_params=pltpu.CompilerParams(vmem_limit_bytes=VMEM_LIMIT),
        cost_estimate=small_cost(),
        name="norm",
    )(layer_input, norm_gain)
    return out[0], out[1:]


def ancestor_mask(parent_row):
    rows = parent_row.shape[1]
    row = lax.broadcasted_iota(jnp.int32, (rows, rows), 0)
    column = lax.broadcasted_iota(jnp.int32, (rows, rows), 1)
    reached = jnp.where((parent_row == row) | (row == column), 1.0, 0.0)
    for squaring in range(rows.bit_length() - 1):
        halfway = reached.astype(jnp.bfloat16)
        reached = jnp.minimum(nn_dot(halfway, halfway), 1.0)
    return reached.T


def attention_kernel(
    slots,
    group,
    kv_local,
    order,
    blocks,
    ready,
    columns,
    shares,
    count_ref,
    parent_ref,
    inverse_ref,
    gain_ref,
    input_hbm,
    query_hbm,
    key_hbm,
    value_hbm,
    grad_hbm,
    *rest,
):
    delta_hbm, rest = rest[: len(shares)], rest[len(shares) :]
    part_hbm, rest = rest[:ready], rest[ready:]
    turned_hbm, centre_out, rest = rest[:3], rest[3], rest[4:]
    column_hbm, column_gain_ref, rest = rest[0], rest[1], rest[2:]
    (
        input_ref,
        gain_row,
        query_ref,
        key_ref,
        value_ref,
        grad_ref,
        sum_ref,
        delta_ref,
        query_turned,
        key_turned,
        value_turned,
        allowed_ref,
        centre_ref,
        kept,
        load_sem,
        weight_sem,
        store_sem,
        part_sem,
    ) = rest
    head_dim = HEAD_DIM
    rows, width = input_ref.shape
    block = rows // slots
    mid = group * head_dim
    steps = weight_sem.shape[0]
    chunk = width // steps
    weights = ((query_hbm, query_ref, mid, 0), (key_hbm, key_ref, head_dim, mid))
    weights += ((value_hbm, value_ref, head_dim, mid + head_dim),)

    def fetch(step, which):
        lines = pl.ds(step * chunk, chunk)
        source, kept_ref = weights[which][:2]
        return pltpu.make_async_copy(
            source.at[lines, :], kept_ref.at[lines, :], weight_sem.at[step, which]
        )

    input_load = pltpu.make_async_copy(input_hbm, input_ref, load_sem.at[0])
    grad_load = pltpu.make_async_copy(grad_hbm, grad_ref, load_sem.at[1])
    input_load.start()
    for step in range(steps):
        for which in range(3):
            fetch(step, which).start()
    grad_load.start()
    gain_row[...] = gain_ref[...].reshape(1, width)

    first_count = lax.axis_index("branch") * slots
    parents = parent_ref[...].reshape(1, rows)
    for slot in range(slots):
        allowed_ref[slot] = ancestor_mask(parents[:, slot * block : (slot + 1) * block])
    inverse = inverse_ref[...]
    input_load.wait()
    stores = []
    if columns:
        start = pl.multiple_of(lax.axis_index("tensor") * columns, 128)
        stores.append(
            pltpu.make_async_copy(
                input_ref.at[:, pl.ds(start, columns)], column_hbm, store_sem.at[0]
            )
        )
        stores[0].start()
        column_gain_ref[...] = gain_row[:, pl.ds(start, columns)]
    else:
        column_gain_ref[...] = jnp.zeros_like(column_gain_ref)

    for step in range(steps):
        lines = slice(step * chunk, (step + 1) * chunk)
        gain = 1.0 + gain_row[:, lines]
        normed = (input_ref[:, lines].astype(jnp.float32) * inverse * gain).astype(jnp.bfloat16)
        for which, (_, kept_ref, wide, place) in enumerate(weights):
            fetch(step, which).wait()
            term = nn_dot(normed, kept_ref[lines, :])
            for h in range(kv_local):
                part = term[:, h * wide : (h + 1) * wide]
                if step > 0:
                    part = part + sum_ref[h, :, place : place + wide]
                sum_ref[h, :, place : place + wide] = part
    grad_load.wait()
    scale = head_dim ** (-0.5)
    centre_ref[...] = jnp.zeros_like(centre_ref)

    def attend(h, carry):
        for slot in range(slots):
            lines = slice(slot * block, (slot + 1) * block)
            live = (
                lax.broadcasted_iota(jnp.int32, (block, mid), 0) < count_ref[first_count + slot]
            )
            columns = pl.ds(pl.multiple_of(h * mid, mid), mid)
            grad_rows = jnp.where(live, grad_ref[lines, columns].astype(jnp.float32), 0.0)
            pair = [slice(g * head_dim, (g + 1) * head_dim) for g in range(group)]
            grads = jnp.concatenate([grad_rows[:, p] for p in pair], axis=0).astype(jnp.bfloat16)
            queries = jnp.concatenate([sum_ref[h, lines, p] for p in pair], axis=0)
            queries = queries.astype(jnp.bfloat16)
            keys = sum_ref[h, lines, mid : mid + head_dim].astype(jnp.bfloat16)
            values = sum_ref[h, lines, mid + head_dim :].astype(jnp.bfloat16)
            allowed = jnp.concatenate([allowed_ref[slot]] * group, axis=0)
            bounded = jnp.tanh(nt_dot(queries, keys) * (scale / softcap_limit))
            weighted = allowed * jnp.exp(softcap_limit * bounded)
            probabilities = weighted * (1.0 / jnp.sum(weighted, axis=-1, keepdims=True))
            d_probs = nt_dot(grads, values)
            d_scores = probabilities * (
                d_probs - jnp.sum(probabilities * d_probs, axis=-1, keepdims=True)
            )
            d_raw = (d_scores * (1.0 - bounded * bounded) * scale).astype(jnp.bfloat16)
            prob_half = probabilities.astype(jnp.bfloat16)
            d_query = nn_dot(d_raw, keys)
            d_key = tn_dot(d_raw, queries)
            d_value = tn_dot(prob_half, grads)
            places = [
                (d_query[g * block : (g + 1) * block], query_turned, h * mid + g * head_dim)
                for g in range(group)
            ]
            places += [(d_key, key_turned, h * head_dim), (d_value, value_turned, h * head_dim)]
            product = None
            for which, (part, turned_ref, start) in enumerate(places):
                half = part.astype(jnp.bfloat16)
                line = which * rows + slot * block
                delta_ref[h, line : line + block, :] = half
                spot = pl.ds(pl.multiple_of(start, head_dim), head_dim)
                turned_ref[spot, lines] = half.T
                term = half.astype(jnp.float32) * sum_ref[
                    h, lines, which * head_dim : (which + 1) * head_dim
                ]
                product = term if product is None else product + term
            centre_ref[lines, :] += jnp.sum(product, axis=-1, keepdims=True)
        return carry

    lax.fori_loop(0, kv_local, attend, 0)
    lasts = []
    for share, out in zip(shares, delta_hbm):
        for place, block_index in enumerate(share):
            h, which = divmod(block_index, group + 2)
            lasts.append(
                pltpu.make_async_copy(
                    delta_ref.at[h, pl.ds(which * rows, rows), :],
                    out.at[pl.ds(place * rows, rows), :],
                    store_sem.at[1 + len(lasts)],
                )
            )
    for which, turned_ref in enumerate((query_turned, key_turned, value_turned)):
        lasts.append(
            pltpu.make_async_copy(turned_ref, turned_hbm[which], store_sem.at[1 + len(lasts)])
        )
    for store in lasts:
        store.start()

    centre = jnp.broadcast_to(centre_ref[...], (rows, 128)).T[:CENTRE_ROWS].astype(jnp.bfloat16)
    centre_out[...] = centre
    span = width // blocks
    cuts = 2
    cut_lines = span // cuts
    parts = [
        pltpu.make_async_copy(kept.at[place], part_hbm[place], part_sem.at[place])
        for place in range(ready)
    ]

    def project_back(step, carry):
        place, cut = step // cuts, lax.rem(step, cuts)
        lines = pl.ds(pl.multiple_of(order(place) * span + cut * cut_lines, 16), cut_lines)
        total = nn_dot(query_ref[lines, :], query_turned[...])
        total += nn_dot(key_ref[lines, :], key_turned[...])
        total += nn_dot(value_ref[lines, :], value_turned[...])
        spot = pl.ds(pl.multiple_of(cut * cut_lines, 16), cut_lines)
        kept[place, spot, :] = total.astype(jnp.bfloat16)
        for which, part in enumerate(parts):

            @pl.when((place == which) & (cut == cuts - 1))
            def _():
                kept[which, span:, :] = centre
                part.start()

        return carry

    lax.fori_loop(0, ready * cuts, project_back, 0)
    for store in stores + lasts + parts:
        store.wait()


def attention_backward(
    layer_input,
    inverse,
    norm_gain,
    w_query,
    w_key,
    w_value,
    head_grad,
    parents,
    counts,
    slots,
    order,
    blocks,
    ready,
    shares,
):
    rows, width = layer_input.shape
    kv_local = w_key.shape[1] // HEAD_DIM
    group = w_query.shape[1] // w_key.shape[1]
    span = (group + 2) * HEAD_DIM
    stack = (group + 2) * rows
    column_width = width // blocks
    cut = column_width % 128 == 0
    wide = column_width if cut else 128
    steps = 2 if width % 512 == 0 else 1
    part_shape = (column_width + CENTRE_ROWS, rows)
    hbm = pl.BlockSpec(memory_space=pl.ANY)
    vmem = pl.BlockSpec(memory_space=pltpu.VMEM)
    half = lambda *shape: jax.ShapeDtypeStruct(shape, jnp.bfloat16)
    out = pl.pallas_call(
        functools.partial(
            attention_kernel,
            slots,
            group,
            kv_local,
            order,
            blocks,
            ready,
            wide if cut else 0,
            shares,
        ),
        out_shape=tuple(half(len(share) * rows, HEAD_DIM) for share in shares)
        + (half(*part_shape),) * ready
        + tuple(half(w.shape[1], rows) for w in (w_query, w_key, w_value))
        + (half(CENTRE_ROWS, rows),)
        + (half(rows, wide), jax.ShapeDtypeStruct((1, wide), jnp.float32)),
        in_specs=[pl.BlockSpec(memory_space=pltpu.SMEM), vmem, vmem, vmem] + [hbm] * 5,
        out_specs=(hbm,) * (len(shares) + ready + 3) + (vmem, hbm, vmem),
        scratch_shapes=[
            pltpu.VMEM((rows, width), jnp.bfloat16),
            pltpu.VMEM((1, width), jnp.float32),
            pltpu.VMEM(w_query.shape, jnp.bfloat16),
            pltpu.VMEM(w_key.shape, jnp.bfloat16),
            pltpu.VMEM(w_value.shape, jnp.bfloat16),
            pltpu.VMEM(head_grad.shape, jnp.bfloat16),
            pltpu.VMEM((kv_local, rows, span), jnp.float32),
            pltpu.VMEM((kv_local, stack, HEAD_DIM), jnp.bfloat16),
            pltpu.VMEM((w_query.shape[1], rows), jnp.bfloat16),
            pltpu.VMEM((w_key.shape[1], rows), jnp.bfloat16),
            pltpu.VMEM((w_value.shape[1], rows), jnp.bfloat16),
            pltpu.VMEM((slots, rows // slots, rows // slots), jnp.float32),
            pltpu.VMEM((rows, 1), jnp.float32),
            pltpu.VMEM((ready, *part_shape), jnp.bfloat16),
            pltpu.SemaphoreType.DMA((2,)),
            pltpu.SemaphoreType.DMA((steps, 3)),
            pltpu.SemaphoreType.DMA((4 + kv_local * (group + 2),)),
            pltpu.SemaphoreType.DMA((ready,)),
        ],
        compiler_params=pltpu.CompilerParams(vmem_limit_bytes=VMEM_LIMIT),
        cost_estimate=small_cost(),
        name="attention",
    )(counts, parents, inverse, norm_gain, layer_input, w_query, w_key, w_value, head_grad)
    deltas, out = out[: len(shares)], out[len(shares) :]
    parts, turned, centre = out[:ready], out[ready : ready + 3], out[ready + 3]
    if cut:
        input_cut, gain_cut = out[-2], out[-1]
    else:
        start = lax.axis_index("tensor") * column_width
        input_cut = lax.dynamic_slice_in_dim(layer_input, start, column_width, 1)
        gain_cut = lax.dynamic_slice_in_dim(norm_gain, start, column_width, 0)
        gain_cut = gain_cut.reshape(1, column_width)
    return deltas, parts, turned, centre, input_cut, gain_cut


def back_kernel(centre_ref, *refs):
    turned_refs, weight_refs, out_refs = refs[:3], refs[3:6], refs[6:]
    piece, cut = pl.program_id(0), pl.program_id(1)
    lines = weight_refs[0].shape[0]
    total = None
    for weight_ref, turned_ref in zip(weight_refs, turned_refs):
        term = nn_dot(weight_ref[...], turned_ref[...])
        total = term if total is None else total + term
    total = total.astype(jnp.bfloat16)
    start = pl.multiple_of(cut * lines, 16)
    depth = out_refs[0].shape[0] - CENTRE_ROWS
    for place, out_ref in enumerate(out_refs):

        @pl.when(piece == place)
        def _():
            out_ref[pl.ds(start, lines), :] = total
            out_ref[depth:, :] = centre_ref[...]


def back_project(order, first, pieces, turned, centre, weights, blocks):
    rows = centre.shape[1]
    depth = weights[0].shape[0] // blocks
    cuts = 2
    whole = lambda i, j: (0, 0)
    return pl.pallas_call(
        back_kernel,
        out_shape=(jax.ShapeDtypeStruct((depth + CENTRE_ROWS, rows), jnp.bfloat16),) * pieces,
        grid=(pieces, cuts),
        in_specs=[pl.BlockSpec(x.shape, whole) for x in (centre, *turned)]
        + [
            pl.BlockSpec((depth // cuts, w.shape[1]), lambda i, j: (order(first + i) * cuts + j, 0))
            for w in weights
        ],
        out_specs=(pl.BlockSpec((depth + CENTRE_ROWS, rows), whole),) * pieces,
        compiler_params=pltpu.CompilerParams(vmem_limit_bytes=VMEM_LIMIT),
        cost_estimate=small_cost(),
        name="back",
    )(centre, *turned, *weights)


def weight_kernel(outs, sources, *refs):
    turned_hbm, delta_hbm = refs[:sources], refs[sources : 2 * sources]
    out_hbm, token_ref = refs[-10:-7], refs[-7]
    turned_ref, delta_ref, kept, turned_sem, delta_sem, store_sem = refs[-6:]
    token_ref[...] = jnp.zeros_like(token_ref)
    rows = turned_ref.shape[2]
    loads = []
    for place in range(sources):
        loads.append(
            pltpu.make_async_copy(
                turned_hbm[place], turned_ref.at[place], turned_sem.at[place]
            )
        )
    for load in loads:
        load.start()

    def fetch(block, place):
        lines = pl.ds(pl.multiple_of(block * rows, rows), rows)
        return pltpu.make_async_copy(
            delta_hbm[place].at[lines, :], delta_ref.at[place, lines, :], delta_sem.at[block, place]
        )

    for block in range(len(outs)):
        for place in range(sources):
            fetch(block, place).start()
    for load in loads:
        load.wait()
    stores = [
        pltpu.make_async_copy(
            kept.at[block],
            out_hbm[which].at[:, pl.ds(column * HEAD_DIM, HEAD_DIM)],
            store_sem.at[block],
        )
        for block, (which, column) in enumerate(outs)
    ]

    def fill(block, carry):
        lines = pl.ds(pl.multiple_of(block * rows, rows), rows)
        total = None
        for place in range(sources):
            fetch(block, place).wait()
        for place in range(sources):
            term = nn_dot(turned_ref[place], delta_ref[place, lines, :])
            total = term if total is None else total + term
        kept[block] = total
        for which, store in enumerate(stores):

            @pl.when(block == which)
            def _():
                store.start()

        return carry

    lax.fori_loop(0, len(outs), fill, 0)
    for store in stores:
        store.wait()


def weight_gradients(turned, deltas, share, kv_local, group, before):
    depth, rows = turned[0].shape
    sources = len(turned)
    outs = []
    for block in share:
        h, which = divmod(block, group + 2)
        outs.append((0, h * group + which) if which < group else (which - group + 1, h))
    kept = list(before) if before is not None else []
    hbm = pl.BlockSpec(memory_space=pl.ANY)
    return pl.pallas_call(
        functools.partial(weight_kernel, outs, sources),
        out_shape=(
            jax.ShapeDtypeStruct((depth, kv_local * group * HEAD_DIM), jnp.float32),
            jax.ShapeDtypeStruct((depth, kv_local * HEAD_DIM), jnp.float32),
            jax.ShapeDtypeStruct((depth, kv_local * HEAD_DIM), jnp.float32),
            jax.ShapeDtypeStruct((8, 128), jnp.float32),
        ),
        in_specs=[hbm] * (2 * sources + len(kept)),
        out_specs=(hbm,) * 3 + (pl.BlockSpec(memory_space=pltpu.VMEM),),
        input_output_aliases={2 * sources + i: i for i in range(len(kept))},
        scratch_shapes=[
            pltpu.VMEM((sources, depth, rows), jnp.bfloat16),
            pltpu.VMEM((sources, len(share) * rows, HEAD_DIM), jnp.bfloat16),
            pltpu.VMEM((len(share), depth, HEAD_DIM), jnp.float32),
            pltpu.SemaphoreType.DMA((sources,)),
            pltpu.SemaphoreType.DMA((len(share), sources)),
            pltpu.SemaphoreType.DMA((len(share),)),
        ],
        compiler_params=pltpu.CompilerParams(vmem_limit_bytes=VMEM_LIMIT),
        cost_estimate=small_cost(),
        name="weights",
    )(*turned, *deltas, *kept)


def gate_kernel(*refs):
    del refs


def gate(arrays, tokens):
    hbm = pl.BlockSpec(memory_space=pl.ANY)
    return pl.pallas_call(
        gate_kernel,
        out_shape=tuple(jax.ShapeDtypeStruct(x.shape, x.dtype) for x in arrays),
        in_specs=[hbm] * (len(arrays) + len(tokens)),
        out_specs=(hbm,) * len(arrays),
        input_output_aliases={i: i for i in range(len(arrays))},
        compiler_params=pltpu.CompilerParams(vmem_limit_bytes=VMEM_LIMIT),
        cost_estimate=small_cost(),
        name="gate",
    )(*arrays, *tokens)


def join_kernel(inner_ref, other_ref, end_ref, *rest):
    out_ref, token_ref = rest[-2:]
    token_ref[...] = jnp.zeros_like(token_ref)
    index = lax.axis_index("tensor")
    inner = (index > 0) & (index < lax.axis_size("tensor") - 1)

    @pl.when(inner)
    def _():
        out_ref[...] = (
            inner_ref[...].astype(jnp.float32) + other_ref[...].astype(jnp.float32)
        ).astype(jnp.bfloat16)

    @pl.when(jnp.logical_not(inner))
    def _():
        out_ref[...] = end_ref[...]


def join(inner_part, other, end_part, tokens):
    vmem = pl.BlockSpec(memory_space=pltpu.VMEM)
    return pl.pallas_call(
        join_kernel,
        out_shape=(
            jax.ShapeDtypeStruct(end_part.shape, end_part.dtype),
            jax.ShapeDtypeStruct((8, 128), jnp.float32),
        ),
        in_specs=[vmem] * 3 + [pl.BlockSpec(memory_space=pl.ANY)] * len(tokens),
        out_specs=(vmem, vmem),
        compiler_params=pltpu.CompilerParams(vmem_limit_bytes=VMEM_LIMIT),
        cost_estimate=small_cost(),
        name="join",
    )(inner_part, other, end_part, *tokens)


def add_parts(for_ends, for_inner, part_refs):
    index = lax.axis_index("tensor")
    ends = ((index == 0) | (index == lax.axis_size("tensor") - 1)).astype(jnp.float32)
    total = None
    for place, part_ref in enumerate(part_refs):
        part = part_ref[...].astype(jnp.float32)
        if place < for_ends:
            part = part * ends
        elif place < for_ends + for_inner:
            part = part * (1.0 - ends)
        total = part if total is None else total + part
    return total


def gain_kernel(add, count, input_ref, inverse_ref, *refs):
    part_refs, (sum_ref, total_ref) = refs[:count], refs[-2:]

    @pl.when(pl.program_id(0) == 0)
    def _():
        sum_ref[...] = jnp.zeros_like(sum_ref)

    d_normed = add(part_refs).T
    total_ref[...] = d_normed
    scaled = input_ref[...].astype(jnp.float32) * inverse_ref[...]
    sum_ref[...] += jnp.sum(d_normed * scaled, axis=0, keepdims=True)


def gain_sums(add, input_columns, inverse, parts, token):
    rows, wide = input_columns.shape
    some = 128
    return pl.pallas_call(
        functools.partial(gain_kernel, add, len(parts)),
        out_shape=(
            jax.ShapeDtypeStruct((1, wide), jnp.float32),
            jax.ShapeDtypeStruct((rows, wide), jnp.float32),
        ),
        grid=(rows // some,),
        in_specs=[
            pl.BlockSpec((some, wide), lambda i: (i, 0)),
            pl.BlockSpec((some, 1), lambda i: (i, 0)),
        ]
        + [pl.BlockSpec((wide, some), lambda i: (0, i))] * len(parts)
        + [pl.BlockSpec(memory_space=pl.ANY)],
        out_specs=(
            pl.BlockSpec((1, wide), lambda i: (0, 0)),
            pl.BlockSpec((some, wide), lambda i: (i, 0)),
        ),
        compiler_params=pltpu.CompilerParams(vmem_limit_bytes=VMEM_LIMIT),
        cost_estimate=small_cost(),
        name="gains",
    )(input_columns, inverse, *parts, token)


def finish_kernel(width, add, total_ref, input_ref, gain_ref, inverse_ref, *refs):
    centre_refs, out_ref = refs[:-1], refs[-1]
    centre = add(centre_refs).T[:, :1] * (1.0 / width)
    inverse = inverse_ref[...]
    scaled = input_ref[...].astype(jnp.float32) * inverse
    out_ref[...] = (
        inverse * ((1.0 + gain_ref[...]) * total_ref[...] - scaled * centre)
    ).astype(jnp.bfloat16)


def finish(width, add, total, input_columns, gain_columns, inverse, parts):
    rows, wide = input_columns.shape
    some = 128
    row_block = pl.BlockSpec((some, wide), lambda i: (i, 0))
    return pl.pallas_call(
        functools.partial(finish_kernel, width, add),
        out_shape=jax.ShapeDtypeStruct((rows, wide), jnp.bfloat16),
        grid=(rows // some,),
        in_specs=[
            row_block,
            row_block,
            pl.BlockSpec((1, wide), lambda i: (0, 0)),
            pl.BlockSpec((some, 1), lambda i: (i, 0)),
        ]
        + [pl.BlockSpec((CENTRE_ROWS, some), lambda i: (wide // CENTRE_ROWS, i))] * len(parts),
        out_specs=row_block,
        compiler_params=pltpu.CompilerParams(vmem_limit_bytes=VMEM_LIMIT),
        cost_estimate=small_cost(),
        name="finish",
    )(total, input_columns, gain_columns, inverse, *parts)


def total_kernel(*refs):
    total = (refs[0][...] + refs[1][...]) + (refs[2][...] + refs[3][...])
    refs[-1][...] = total.reshape(refs[-1].shape)


def total_of_four(arrays, token):
    whole = pl.BlockSpec(arrays[0].shape, lambda i: (0, 0))
    wide = arrays[0].shape[1]
    return pl.pallas_call(
        total_kernel,
        out_shape=jax.ShapeDtypeStruct((wide,), arrays[0].dtype),
        grid=(1,),
        in_specs=[whole] * 4 + [pl.BlockSpec(memory_space=pl.ANY)],
        out_specs=pl.BlockSpec((wide,), lambda i: (0,)),
        compiler_params=pltpu.CompilerParams(vmem_limit_bytes=VMEM_LIMIT),
        cost_estimate=small_cost(),
        name="total",
    )(*arrays, token)


def branch_send(array, chips, shift, swap):
    pairs = [
        (c * 2 + k, ((c + shift) % chips) * 2 + (k ^ swap)) for c in range(chips) for k in range(2)
    ]
    return lax.ppermute(array, "branch", pairs)


def pick(table, index):
    chosen = table[-1]
    for place in range(len(table) - 2, -1, -1):
        chosen = jnp.where(index == place, table[place], chosen)
    return chosen


def scatter_order(total):
    index = lax.axis_index("tensor")
    if total != 4:
        return lambda place: lax.rem(index + place + 1, total)
    table = [[3, 0, 3, 0], [0, 2, 1, 3], [2, 3, 0, 1], [1, 1, 2, 2]]
    here = [pick(row, index) for row in table]
    return lambda place: pick(here, place)


def scatter_begin(parts, total):
    if total != 4:
        return [
            lax.ppermute(part, "tensor", [(t, (t + shift) % total) for t in range(total)])
            for shift, part in zip(range(1, total), parts[:-1])
        ]
    from_first = lax.ppermute(parts[0], "tensor", [(0, 1), (1, 0), (2, 3), (3, 2)])
    from_inner = lax.ppermute(parts[1], "tensor", [(1, 2), (2, 1)])
    from_ends = lax.ppermute(parts[2], "tensor", [(0, 2), (3, 1)])
    return from_first, from_inner, from_ends


def scatter_end(parts, arrived, total):
    if total != 4:
        return [parts[-1], *arrived], 0, 0, arrived[0]
    from_first, from_inner, from_ends = arrived
    joined, token = join(parts[2], from_first, parts[3], (from_inner, from_ends))
    from_joined = lax.ppermute(joined, "tensor", [(1, 3), (2, 0), (0, 1), (3, 2)])
    return [from_first, parts[1], parts[3], from_inner, from_ends, from_joined], 2, 1, token


def local(layer_input, norm_gain, w_query, w_key, w_value, head_grad, parents, row_counts):
    branch_total = lax.axis_size("branch")
    tensor_total = lax.axis_size("tensor")
    slots = row_counts.shape[0] // branch_total
    rows, width = layer_input.shape
    column_width = width // tensor_total
    chips = branch_total // 2
    group = w_query.shape[1] // w_key.shape[1]
    kv_local = w_key.shape[1] // HEAD_DIM
    offsets = [(shift, swap) for shift in range(chips) for swap in range(2)]
    blocks = list(range(kv_local * (group + 2)))
    early = blocks[: group + 2] + [h * (group + 2) + group for h in range(1, kv_local)]
    shares = [early, [block for block in blocks if block not in early]]
    shares = [share for share in shares if share]

    def targets():
        index = lax.axis_index("branch")
        chip, core = index // 2, index % 2
        return [lax.rem(chip + s, chips) * 2 + lax.rem(core + e, 2) for s, e in offsets]

    inverse, pieces = normalize(layer_input, norm_gain, targets, branch_total, rows // slots)
    near = branch_send(pieces[1], chips, 0, 1)
    direct = [branch_send(pieces[2 * s], chips, s, 0) for s in range(1, chips)]
    across = [branch_send(pieces[2 * s + 1], chips, s, 1) for s in range(1, chips)]
    turned = [pieces[0]] + direct + [near] + across
    order = lambda place: scatter_order(tensor_total)(place)
    ready = min(3, tensor_total)
    deltas, parts, delta_turned, centre, input_columns, gain_columns = attention_backward(
        layer_input,
        inverse,
        norm_gain,
        w_query,
        w_key,
        w_value,
        head_grad,
        parents,
        row_counts,
        slots,
        order,
        tensor_total,
        ready,
        shares,
    )
    if ready < tensor_total:
        weights = (w_query, w_key, w_value)
        parts += back_project(
            order, ready, tensor_total - ready, delta_turned, centre, weights, tensor_total
        )
    arrived = scatter_begin(parts, tensor_total)

    (first,) = gate(deltas[:1], (near, *direct, *across))
    sent = [branch_send(first, chips, s, 0) for s in range(1, chips)]
    parts, for_ends, for_inner, met = scatter_end(parts, arrived, tensor_total)
    *sent, first = gate((*sent, first), parts[2:3])
    others = gate(deltas[1:], (sent[0],)) if deltas[1:] else ()
    weights, tokens = None, []
    for share, delta in zip(shares, (first, *others)):
        if tokens:
            sent = [branch_send(delta, chips, s, 0) for s in range(1, chips)]
            delta, *sent = gate((delta, *sent), (parts[-1], tokens[0]))
        gathered = [delta] + sent
        gathered += [branch_send(part, chips, 0, 1) for part in gathered]
        *weights, token = weight_gradients(turned, gathered, share, kv_local, group, weights)
        tokens.append(token)

    add = functools.partial(add_parts, for_ends, for_inner)
    gain_sum, total = gain_sums(add, input_columns, inverse, parts, tokens[0])
    grad_input = finish(width, add, total, input_columns, gain_columns, inverse, parts)
    if chips == 2:
        sums = [gain_sum] + [branch_send(gain_sum, chips, s, e) for s, e in offsets[1:]]
        grad_gain = total_of_four(sums, tokens[-1])
    else:
        grad_gain = lax.psum(gain_sum, "branch").reshape(column_width)
    return (grad_input, *weights, grad_gain)


def solution(mesh):
    placed = (
        P(("parts", "branch"), None),
        P(),
        P(None, "tensor"),
        P(None, "tensor"),
        P(None, "tensor"),
        P(("parts", "branch"), "tensor"),
        P(("parts", "branch")),
        P("parts"),
    )
    return jax.shard_map(
        local,
        mesh=mesh,
        in_specs=placed,
        out_specs=(
            P(("parts", "branch"), "tensor"),
            P(("parts", "branch"), "tensor"),
            P(("parts", "branch"), "tensor"),
            P(("parts", "branch"), "tensor"),
            P(("parts", "tensor")),
        ),
        check_vma=False,
    )
```

```python
import functools

import jax
import jax.numpy as jnp
from jax import lax
from jax.experimental import pallas as pl
from jax.experimental.pallas import tpu as pltpu
from jax.sharding import PartitionSpec as P

HEAD_DIM = 256
MIB = 1024 * 1024
CENTRE_ROWS = 16
VMEM_LIMIT = 64 * MIB


epsilon = 1e-06
softcap_limit = 50.0


def nn_dot(left, right):
    return lax.dot_general(
        left, right, (((1,), (0,)), ((), ())), preferred_element_type=jnp.float32
    )


def nt_dot(left, right):
    return lax.dot_general(
        left, right, (((1,), (1,)), ((), ())), preferred_element_type=jnp.float32
    )


def tn_dot(left, right):
    return lax.dot_general(
        left, right, (((0,), (0,)), ((), ())), preferred_element_type=jnp.float32
    )


def small_cost():
    return pl.CostEstimate(flops=1000000, bytes_accessed=100000, transcendentals=0)


def norm_kernel(targets, input_ref, gain_ref, inverse_ref, *rest):
    piece_refs, turned = rest[:-1], rest[-1]
    rows, width = input_ref.shape
    values = input_ref[...].astype(jnp.float32)
    inverse = lax.rsqrt(jnp.mean(values * values, axis=-1, keepdims=True) + epsilon)
    inverse_ref[...] = inverse
    gain = gain_ref[...].reshape(1, width)
    turned[...] = (values * inverse * (1.0 + gain)).astype(jnp.bfloat16).T
    depth = width // len(piece_refs)
    for target, piece_ref in zip(targets(), piece_refs):
        start = pl.multiple_of(target * depth, 16)
        piece_ref[...] = turned[pl.ds(start, depth), :]


def normalize(layer_input, norm_gain, targets, pieces, block):
    rows, width = layer_input.shape
    depth = width // pieces
    out = pl.pallas_call(
        functools.partial(norm_kernel, targets),
        out_shape=(jax.ShapeDtypeStruct((rows, 1), jnp.float32),)
        + (jax.ShapeDtypeStruct((depth, rows), jnp.bfloat16),) * pieces,
        grid=(rows // block,),
        in_specs=[
            pl.BlockSpec((block, width), lambda i: (i, 0)),
            pl.BlockSpec((width,), lambda i: (0,)),
        ],
        out_specs=(pl.BlockSpec((block, 1), lambda i: (i, 0)),)
        + (pl.BlockSpec((depth, block), lambda i: (0, i)),) * pieces,
        scratch_shapes=[pltpu.VMEM((width, block), jnp.bfloat16)],
        compiler_params=pltpu.CompilerParams(vmem_limit_bytes=VMEM_LIMIT),
        cost_estimate=small_cost(),
        name="norm",
    )(layer_input, norm_gain)
    return out[0], out[1:]


def ancestor_mask(parent_row):
    rows = parent_row.shape[1]
    row = lax.broadcasted_iota(jnp.int32, (rows, rows), 0)
    column = lax.broadcasted_iota(jnp.int32, (rows, rows), 1)
    reached = jnp.where((parent_row == row) | (row == column), 1.0, 0.0)
    for squaring in range(rows.bit_length() - 1):
        halfway = reached.astype(jnp.bfloat16)
        reached = jnp.minimum(nn_dot(halfway, halfway), 1.0)
    return reached.T


def attention_kernel(
    slots,
    group,
    kv_local,
    order,
    blocks,
    ready,
    columns,
    shares,
    count_ref,
    parent_ref,
    inverse_ref,
    gain_ref,
    input_hbm,
    query_hbm,
    key_hbm,
    value_hbm,
    grad_hbm,
    *rest,
):
    delta_hbm, rest = rest[: len(shares)], rest[len(shares) :]
    part_hbm, rest = rest[:ready], rest[ready:]
    turned_hbm, centre_out, rest = rest[:3], rest[3], rest[4:]
    column_hbm, column_gain_ref, rest = rest[0], rest[1], rest[2:]
    (
        input_ref,
        gain_row,
        query_ref,
        key_ref,
        value_ref,
        grad_ref,
        sum_ref,
        delta_ref,
        query_turned,
        key_turned,
        value_turned,
        allowed_ref,
        centre_ref,
        kept,
        load_sem,
        weight_sem,
        store_sem,
        part_sem,
    ) = rest
    head_dim = HEAD_DIM
    rows, width = input_ref.shape
    block = rows // slots
    mid = group * head_dim
    steps = weight_sem.shape[0]
    chunk = width // steps
    weights = ((query_hbm, query_ref, mid, 0), (key_hbm, key_ref, head_dim, mid))
    weights += ((value_hbm, value_ref, head_dim, mid + head_dim),)

    def fetch(step, which):
        lines = pl.ds(step * chunk, chunk)
        source, kept_ref = weights[which][:2]
        return pltpu.make_async_copy(
            source.at[lines, :], kept_ref.at[lines, :], weight_sem.at[step, which]
        )

    input_load = pltpu.make_async_copy(input_hbm, input_ref, load_sem.at[0])
    grad_load = pltpu.make_async_copy(grad_hbm, grad_ref, load_sem.at[1])
    input_load.start()
    for step in range(steps):
        for which in range(3):
            fetch(step, which).start()
    grad_load.start()
    gain_row[...] = gain_ref[...].reshape(1, width)

    first_count = lax.axis_index("branch") * slots
    parents = parent_ref[...].reshape(1, rows)
    for slot in range(slots):
        allowed_ref[slot] = ancestor_mask(parents[:, slot * block : (slot + 1) * block])
    inverse = inverse_ref[...]
    input_load.wait()
    stores = []
    if columns:
        start = pl.multiple_of(lax.axis_index("tensor") * columns, 128)
        stores.append(
            pltpu.make_async_copy(
                input_ref.at[:, pl.ds(start, columns)], column_hbm, store_sem.at[0]
            )
        )
        stores[0].start()
        column_gain_ref[...] = gain_row[:, pl.ds(start, columns)]
    else:
        column_gain_ref[...] = jnp.zeros_like(column_gain_ref)

    for step in range(steps):
        lines = slice(step * chunk, (step + 1) * chunk)
        gain = 1.0 + gain_row[:, lines]
        normed = (input_ref[:, lines].astype(jnp.float32) * inverse * gain).astype(jnp.bfloat16)
        for which, (_, kept_ref, wide, place) in enumerate(weights):
            fetch(step, which).wait()
            term = nn_dot(normed, kept_ref[lines, :])
            for h in range(kv_local):
                part = term[:, h * wide : (h + 1) * wide]
                if step > 0:
                    part = part + sum_ref[h, :, place : place + wide]
                sum_ref[h, :, place : place + wide] = part
    grad_load.wait()
    scale = head_dim ** (-0.5)
    centre_ref[...] = jnp.zeros_like(centre_ref)

    def attend(h, carry):
        for slot in range(slots):
            lines = slice(slot * block, (slot + 1) * block)
            live = (
                lax.broadcasted_iota(jnp.int32, (block, mid), 0) < count_ref[first_count + slot]
            )
            columns = pl.ds(pl.multiple_of(h * mid, mid), mid)
            grad_rows = jnp.where(live, grad_ref[lines, columns].astype(jnp.float32), 0.0)
            pair = [slice(g * head_dim, (g + 1) * head_dim) for g in range(group)]
            grads = jnp.concatenate([grad_rows[:, p] for p in pair], axis=0).astype(jnp.bfloat16)
            queries = jnp.concatenate([sum_ref[h, lines, p] for p in pair], axis=0)
            queries = queries.astype(jnp.bfloat16)
            keys = sum_ref[h, lines, mid : mid + head_dim].astype(jnp.bfloat16)
            values = sum_ref[h, lines, mid + head_dim :].astype(jnp.bfloat16)
            allowed = jnp.concatenate([allowed_ref[slot]] * group, axis=0)
            bounded = jnp.tanh(nt_dot(queries, keys) * (scale / softcap_limit))
            weighted = allowed * jnp.exp(softcap_limit * bounded)
            probabilities = weighted * (1.0 / jnp.sum(weighted, axis=-1, keepdims=True))
            d_probs = nt_dot(grads, values)
            d_scores = probabilities * (
                d_probs - jnp.sum(probabilities * d_probs, axis=-1, keepdims=True)
            )
            d_raw = (d_scores * (1.0 - bounded * bounded) * scale).astype(jnp.bfloat16)
            prob_half = probabilities.astype(jnp.bfloat16)
            d_query = nn_dot(d_raw, keys)
            d_key = tn_dot(d_raw, queries)
            d_value = tn_dot(prob_half, grads)
            places = [
                (d_query[g * block : (g + 1) * block], query_turned, h * mid + g * head_dim)
                for g in range(group)
            ]
            places += [(d_key, key_turned, h * head_dim), (d_value, value_turned, h * head_dim)]
            product = None
            for which, (part, turned_ref, start) in enumerate(places):
                half = part.astype(jnp.bfloat16)
                line = which * rows + slot * block
                delta_ref[h, line : line + block, :] = half
                spot = pl.ds(pl.multiple_of(start, head_dim), head_dim)
                turned_ref[spot, lines] = half.T
                term = half.astype(jnp.float32) * sum_ref[
                    h, lines, which * head_dim : (which + 1) * head_dim
                ]
                product = term if product is None else product + term
            centre_ref[lines, :] += jnp.sum(product, axis=-1, keepdims=True)
        return carry

    lax.fori_loop(0, kv_local, attend, 0)
    lasts = []
    for share, out in zip(shares, delta_hbm):
        for place, block_index in enumerate(share):
            h, which = divmod(block_index, group + 2)
            lasts.append(
                pltpu.make_async_copy(
                    delta_ref.at[h, pl.ds(which * rows, rows), :],
                    out.at[pl.ds(place * rows, rows), :],
                    store_sem.at[1 + len(lasts)],
                )
            )
    for which, turned_ref in enumerate((query_turned, key_turned, value_turned)):
        lasts.append(
            pltpu.make_async_copy(turned_ref, turned_hbm[which], store_sem.at[1 + len(lasts)])
        )
    for store in lasts:
        store.start()

    centre = jnp.broadcast_to(centre_ref[...], (rows, 128)).T[:CENTRE_ROWS].astype(jnp.bfloat16)
    centre_out[...] = centre
    span = width // blocks
    cuts = 2
    cut_lines = span // cuts
    parts = [
        pltpu.make_async_copy(kept.at[place], part_hbm[place], part_sem.at[place])
        for place in range(ready)
    ]

    def project_back(step, carry):
        place, cut = step // cuts, lax.rem(step, cuts)
        lines = pl.ds(pl.multiple_of(order(place) * span + cut * cut_lines, 16), cut_lines)
        total = nn_dot(query_ref[lines, :], query_turned[...])
        total += nn_dot(key_ref[lines, :], key_turned[...])
        total += nn_dot(value_ref[lines, :], value_turned[...])
        spot = pl.ds(pl.multiple_of(cut * cut_lines, 16), cut_lines)
        kept[place, spot, :] = total.astype(jnp.bfloat16)
        for which, part in enumerate(parts):

            @pl.when((place == which) & (cut == cuts - 1))
            def _():
                kept[which, span:, :] = centre
                part.start()

        return carry

    lax.fori_loop(0, ready * cuts, project_back, 0)
    for store in stores + lasts + parts:
        store.wait()


def attention_backward(
    layer_input,
    inverse,
    norm_gain,
    w_query,
    w_key,
    w_value,
    head_grad,
    parents,
    counts,
    slots,
    order,
    blocks,
    ready,
    shares,
):
    rows, width = layer_input.shape
    kv_local = w_key.shape[1] // HEAD_DIM
    group = w_query.shape[1] // w_key.shape[1]
    span = (group + 2) * HEAD_DIM
    stack = (group + 2) * rows
    column_width = width // blocks
    cut = column_width % 128 == 0
    wide = column_width if cut else 128
    steps = 2 if width % 512 == 0 else 1
    part_shape = (column_width + CENTRE_ROWS, rows)
    hbm = pl.BlockSpec(memory_space=pl.ANY)
    vmem = pl.BlockSpec(memory_space=pltpu.VMEM)
    half = lambda *shape: jax.ShapeDtypeStruct(shape, jnp.bfloat16)
    out = pl.pallas_call(
        functools.partial(
            attention_kernel,
            slots,
            group,
            kv_local,
            order,
            blocks,
            ready,
            wide if cut else 0,
            shares,
        ),
        out_shape=tuple(half(len(share) * rows, HEAD_DIM) for share in shares)
        + (half(*part_shape),) * ready
        + tuple(half(w.shape[1], rows) for w in (w_query, w_key, w_value))
        + (half(CENTRE_ROWS, rows),)
        + (half(rows, wide), jax.ShapeDtypeStruct((1, wide), jnp.float32)),
        in_specs=[pl.BlockSpec(memory_space=pltpu.SMEM), vmem, vmem, vmem] + [hbm] * 5,
        out_specs=(hbm,) * (len(shares) + ready + 3) + (vmem, hbm, vmem),
        scratch_shapes=[
            pltpu.VMEM((rows, width), jnp.bfloat16),
            pltpu.VMEM((1, width), jnp.float32),
            pltpu.VMEM(w_query.shape, jnp.bfloat16),
            pltpu.VMEM(w_key.shape, jnp.bfloat16),
            pltpu.VMEM(w_value.shape, jnp.bfloat16),
            pltpu.VMEM(head_grad.shape, jnp.bfloat16),
            pltpu.VMEM((kv_local, rows, span), jnp.float32),
            pltpu.VMEM((kv_local, stack, HEAD_DIM), jnp.bfloat16),
            pltpu.VMEM((w_query.shape[1], rows), jnp.bfloat16),
            pltpu.VMEM((w_key.shape[1], rows), jnp.bfloat16),
            pltpu.VMEM((w_value.shape[1], rows), jnp.bfloat16),
            pltpu.VMEM((slots, rows // slots, rows // slots), jnp.float32),
            pltpu.VMEM((rows, 1), jnp.float32),
            pltpu.VMEM((ready, *part_shape), jnp.bfloat16),
            pltpu.SemaphoreType.DMA((2,)),
            pltpu.SemaphoreType.DMA((steps, 3)),
            pltpu.SemaphoreType.DMA((4 + kv_local * (group + 2),)),
            pltpu.SemaphoreType.DMA((ready,)),
        ],
        compiler_params=pltpu.CompilerParams(vmem_limit_bytes=VMEM_LIMIT),
        cost_estimate=small_cost(),
        name="attention",
    )(counts, parents, inverse, norm_gain, layer_input, w_query, w_key, w_value, head_grad)
    deltas, out = out[: len(shares)], out[len(shares) :]
    parts, turned, centre = out[:ready], out[ready : ready + 3], out[ready + 3]
    if cut:
        input_cut, gain_cut = out[-2], out[-1]
    else:
        start = lax.axis_index("tensor") * column_width
        input_cut = lax.dynamic_slice_in_dim(layer_input, start, column_width, 1)
        gain_cut = lax.dynamic_slice_in_dim(norm_gain, start, column_width, 0)
        gain_cut = gain_cut.reshape(1, column_width)
    return deltas, parts, turned, centre, input_cut, gain_cut


def back_kernel(centre_ref, *refs):
    turned_refs, weight_refs, out_refs = refs[:3], refs[3:6], refs[6:]
    piece, cut = pl.program_id(0), pl.program_id(1)
    lines = weight_refs[0].shape[0]
    total = None
    for weight_ref, turned_ref in zip(weight_refs, turned_refs):
        term = nn_dot(weight_ref[...], turned_ref[...])
        total = term if total is None else total + term
    total = total.astype(jnp.bfloat16)
    start = pl.multiple_of(cut * lines, 16)
    depth = out_refs[0].shape[0] - CENTRE_ROWS
    for place, out_ref in enumerate(out_refs):

        @pl.when(piece == place)
        def _():
            out_ref[pl.ds(start, lines), :] = total
            out_ref[depth:, :] = centre_ref[...]


def back_project(order, first, pieces, turned, centre, weights, blocks):
    rows = centre.shape[1]
    depth = weights[0].shape[0] // blocks
    cuts = 2
    whole = lambda i, j: (0, 0)
    return pl.pallas_call(
        back_kernel,
        out_shape=(jax.ShapeDtypeStruct((depth + CENTRE_ROWS, rows), jnp.bfloat16),) * pieces,
        grid=(pieces, cuts),
        in_specs=[pl.BlockSpec(x.shape, whole) for x in (centre, *turned)]
        + [
            pl.BlockSpec((depth // cuts, w.shape[1]), lambda i, j: (order(first + i) * cuts + j, 0))
            for w in weights
        ],
        out_specs=(pl.BlockSpec((depth + CENTRE_ROWS, rows), whole),) * pieces,
        compiler_params=pltpu.CompilerParams(vmem_limit_bytes=VMEM_LIMIT),
        cost_estimate=small_cost(),
        name="back",
    )(centre, *turned, *weights)


def weight_kernel(outs, sources, *refs):
    turned_hbm, delta_hbm = refs[:sources], refs[sources : 2 * sources]
    out_hbm, token_ref = refs[-10:-7], refs[-7]
    turned_ref, delta_ref, kept, turned_sem, delta_sem, store_sem = refs[-6:]
    token_ref[...] = jnp.zeros_like(token_ref)
    rows = turned_ref.shape[2]
    loads = []
    for place in range(sources):
        loads.append(
            pltpu.make_async_copy(
                turned_hbm[place], turned_ref.at[place], turned_sem.at[place]
            )
        )
    for load in loads:
        load.start()

    def fetch(block, place):
        lines = pl.ds(pl.multiple_of(block * rows, rows), rows)
        return pltpu.make_async_copy(
            delta_hbm[place].at[lines, :], delta_ref.at[place, lines, :], delta_sem.at[block, place]
        )

    for block in range(len(outs)):
        for place in range(sources):
            fetch(block, place).start()
    for load in loads:
        load.wait()
    stores = [
        pltpu.make_async_copy(
            kept.at[block],
            out_hbm[which].at[:, pl.ds(column * HEAD_DIM, HEAD_DIM)],
            store_sem.at[block],
        )
        for block, (which, column) in enumerate(outs)
    ]

    def fill(block, carry):
        lines = pl.ds(pl.multiple_of(block * rows, rows), rows)
        total = None
        for place in range(sources):
            fetch(block, place).wait()
        for place in range(sources):
            term = nn_dot(turned_ref[place], delta_ref[place, lines, :])
            total = term if total is None else total + term
        kept[block] = total
        for which, store in enumerate(stores):

            @pl.when(block == which)
            def _():
                store.start()

        return carry

    lax.fori_loop(0, len(outs), fill, 0)
    for store in stores:
        store.wait()


def weight_gradients(turned, deltas, share, kv_local, group, before):
    depth, rows = turned[0].shape
    sources = len(turned)
    outs = []
    for block in share:
        h, which = divmod(block, group + 2)
        outs.append((0, h * group + which) if which < group else (which - group + 1, h))
    kept = list(before) if before is not None else []
    hbm = pl.BlockSpec(memory_space=pl.ANY)
    return pl.pallas_call(
        functools.partial(weight_kernel, outs, sources),
        out_shape=(
            jax.ShapeDtypeStruct((depth, kv_local * group * HEAD_DIM), jnp.float32),
            jax.ShapeDtypeStruct((depth, kv_local * HEAD_DIM), jnp.float32),
            jax.ShapeDtypeStruct((depth, kv_local * HEAD_DIM), jnp.float32),
            jax.ShapeDtypeStruct((8, 128), jnp.float32),
        ),
        in_specs=[hbm] * (2 * sources + len(kept)),
        out_specs=(hbm,) * 3 + (pl.BlockSpec(memory_space=pltpu.VMEM),),
        input_output_aliases={2 * sources + i: i for i in range(len(kept))},
        scratch_shapes=[
            pltpu.VMEM((sources, depth, rows), jnp.bfloat16),
            pltpu.VMEM((sources, len(share) * rows, HEAD_DIM), jnp.bfloat16),
            pltpu.VMEM((len(share), depth, HEAD_DIM), jnp.float32),
            pltpu.SemaphoreType.DMA((sources,)),
            pltpu.SemaphoreType.DMA((len(share), sources)),
            pltpu.SemaphoreType.DMA((len(share),)),
        ],
        compiler_params=pltpu.CompilerParams(vmem_limit_bytes=VMEM_LIMIT),
        cost_estimate=small_cost(),
        name="weights",
    )(*turned, *deltas, *kept)


def gate_kernel(*refs):
    del refs


def gate(arrays, tokens):
    hbm = pl.BlockSpec(memory_space=pl.ANY)
    return pl.pallas_call(
        gate_kernel,
        out_shape=tuple(jax.ShapeDtypeStruct(x.shape, x.dtype) for x in arrays),
        in_specs=[hbm] * (len(arrays) + len(tokens)),
        out_specs=(hbm,) * len(arrays),
        input_output_aliases={i: i for i in range(len(arrays))},
        compiler_params=pltpu.CompilerParams(vmem_limit_bytes=VMEM_LIMIT),
        cost_estimate=small_cost(),
        name="gate",
    )(*arrays, *tokens)


def join_kernel(inner_ref, other_ref, end_ref, *rest):
    out_ref, token_ref = rest[-2:]
    token_ref[...] = jnp.zeros_like(token_ref)
    index = lax.axis_index("tensor")
    inner = (index > 0) & (index < lax.axis_size("tensor") - 1)

    @pl.when(inner)
    def _():
        out_ref[...] = (
            inner_ref[...].astype(jnp.float32) + other_ref[...].astype(jnp.float32)
        ).astype(jnp.bfloat16)

    @pl.when(jnp.logical_not(inner))
    def _():
        out_ref[...] = end_ref[...]


def join(inner_part, other, end_part, tokens):
    vmem = pl.BlockSpec(memory_space=pltpu.VMEM)
    return pl.pallas_call(
        join_kernel,
        out_shape=(
            jax.ShapeDtypeStruct(end_part.shape, end_part.dtype),
            jax.ShapeDtypeStruct((8, 128), jnp.float32),
        ),
        in_specs=[vmem] * 3 + [pl.BlockSpec(memory_space=pl.ANY)] * len(tokens),
        out_specs=(vmem, vmem),
        compiler_params=pltpu.CompilerParams(vmem_limit_bytes=VMEM_LIMIT),
        cost_estimate=small_cost(),
        name="join",
    )(inner_part, other, end_part, *tokens)


def add_parts(for_ends, for_inner, part_refs):
    index = lax.axis_index("tensor")
    ends = ((index == 0) | (index == lax.axis_size("tensor") - 1)).astype(jnp.float32)
    total = None
    for place, part_ref in enumerate(part_refs):
        part = part_ref[...].astype(jnp.float32)
        if place < for_ends:
            part = part * ends
        elif place < for_ends + for_inner:
            part = part * (1.0 - ends)
        total = part if total is None else total + part
    return total


def gain_kernel(add, count, input_ref, inverse_ref, *refs):
    part_refs, (sum_ref, total_ref) = refs[:count], refs[-2:]

    @pl.when(pl.program_id(0) == 0)
    def _():
        sum_ref[...] = jnp.zeros_like(sum_ref)

    d_normed = add(part_refs).T
    total_ref[...] = d_normed
    scaled = input_ref[...].astype(jnp.float32) * inverse_ref[...]
    sum_ref[...] += jnp.sum(d_normed * scaled, axis=0, keepdims=True)


def gain_sums(add, input_columns, inverse, parts, token):
    rows, wide = input_columns.shape
    some = 128
    return pl.pallas_call(
        functools.partial(gain_kernel, add, len(parts)),
        out_shape=(
            jax.ShapeDtypeStruct((1, wide), jnp.float32),
            jax.ShapeDtypeStruct((rows, wide), jnp.float32),
        ),
        grid=(rows // some,),
        in_specs=[
            pl.BlockSpec((some, wide), lambda i: (i, 0)),
            pl.BlockSpec((some, 1), lambda i: (i, 0)),
        ]
        + [pl.BlockSpec((wide, some), lambda i: (0, i))] * len(parts)
        + [pl.BlockSpec(memory_space=pl.ANY)],
        out_specs=(
            pl.BlockSpec((1, wide), lambda i: (0, 0)),
            pl.BlockSpec((some, wide), lambda i: (i, 0)),
        ),
        compiler_params=pltpu.CompilerParams(vmem_limit_bytes=VMEM_LIMIT),
        cost_estimate=small_cost(),
        name="gains",
    )(input_columns, inverse, *parts, token)


def finish_kernel(width, add, total_ref, input_ref, gain_ref, inverse_ref, *refs):
    centre_refs, out_ref = refs[:-1], refs[-1]
    centre = add(centre_refs).T[:, :1] * (1.0 / width)
    inverse = inverse_ref[...]
    scaled = input_ref[...].astype(jnp.float32) * inverse
    out_ref[...] = (
        inverse * ((1.0 + gain_ref[...]) * total_ref[...] - scaled * centre)
    ).astype(jnp.bfloat16)


def finish(width, add, total, input_columns, gain_columns, inverse, parts):
    rows, wide = input_columns.shape
    some = 128
    row_block = pl.BlockSpec((some, wide), lambda i: (i, 0))
    return pl.pallas_call(
        functools.partial(finish_kernel, width, add),
        out_shape=jax.ShapeDtypeStruct((rows, wide), jnp.bfloat16),
        grid=(rows // some,),
        in_specs=[
            row_block,
            row_block,
            pl.BlockSpec((1, wide), lambda i: (0, 0)),
            pl.BlockSpec((some, 1), lambda i: (i, 0)),
        ]
        + [pl.BlockSpec((CENTRE_ROWS, some), lambda i: (wide // CENTRE_ROWS, i))] * len(parts),
        out_specs=row_block,
        compiler_params=pltpu.CompilerParams(vmem_limit_bytes=VMEM_LIMIT),
        cost_estimate=small_cost(),
        name="finish",
    )(total, input_columns, gain_columns, inverse, *parts)


def total_kernel(*refs):
    total = (refs[0][...] + refs[1][...]) + (refs[2][...] + refs[3][...])
    refs[-1][...] = total.reshape(refs[-1].shape)


def total_of_four(arrays, token):
    whole = pl.BlockSpec(arrays[0].shape, lambda i: (0, 0))
    wide = arrays[0].shape[1]
    return pl.pallas_call(
        total_kernel,
        out_shape=jax.ShapeDtypeStruct((wide,), arrays[0].dtype),
        grid=(1,),
        in_specs=[whole] * 4 + [pl.BlockSpec(memory_space=pl.ANY)],
        out_specs=pl.BlockSpec((wide,), lambda i: (0,)),
        compiler_params=pltpu.CompilerParams(vmem_limit_bytes=VMEM_LIMIT),
        cost_estimate=small_cost(),
        name="total",
    )(*arrays, token)


def branch_send(array, chips, shift, swap):
    pairs = [
        (c * 2 + k, ((c + shift) % chips) * 2 + (k ^ swap)) for c in range(chips) for k in range(2)
    ]
    return lax.ppermute(array, "branch", pairs)


def pick(table, index):
    chosen = table[-1]
    for place in range(len(table) - 2, -1, -1):
        chosen = jnp.where(index == place, table[place], chosen)
    return chosen


def scatter_order(total):
    index = lax.axis_index("tensor")
    if total != 4:
        return lambda place: lax.rem(index + place + 1, total)
    table = [[3, 0, 3, 0], [0, 2, 1, 3], [2, 3, 0, 1], [1, 1, 2, 2]]
    here = [pick(row, index) for row in table]
    return lambda place: pick(here, place)


def scatter_begin(parts, total):
    if total != 4:
        return [
            lax.ppermute(part, "tensor", [(t, (t + shift) % total) for t in range(total)])
            for shift, part in zip(range(1, total), parts[:-1])
        ]
    from_first = lax.ppermute(parts[0], "tensor", [(0, 1), (1, 0), (2, 3), (3, 2)])
    from_inner = lax.ppermute(parts[1], "tensor", [(1, 2), (2, 1)])
    from_ends = lax.ppermute(parts[2], "tensor", [(0, 2), (3, 1)])
    return from_first, from_inner, from_ends


def scatter_end(parts, arrived, total):
    if total != 4:
        return [parts[-1], *arrived], 0, 0, arrived[0]
    from_first, from_inner, from_ends = arrived
    joined, token = join(parts[2], from_first, parts[3], (from_inner, from_ends))
    from_joined = lax.ppermute(joined, "tensor", [(1, 3), (2, 0), (0, 1), (3, 2)])
    return [from_first, parts[1], parts[3], from_inner, from_ends, from_joined], 2, 1, token


def local(layer_input, norm_gain, w_query, w_key, w_value, head_grad, parents, row_counts):
    branch_total = lax.axis_size("branch")
    tensor_total = lax.axis_size("tensor")
    slots = row_counts.shape[0] // branch_total
    rows, width = layer_input.shape
    column_width = width // tensor_total
    chips = branch_total // 2
    group = w_query.shape[1] // w_key.shape[1]
    kv_local = w_key.shape[1] // HEAD_DIM
    offsets = [(shift, swap) for shift in range(chips) for swap in range(2)]
    shares = [list(range(kv_local * (group + 2)))]

    def targets():
        index = lax.axis_index("branch")
        chip, core = index // 2, index % 2
        return [lax.rem(chip + s, chips) * 2 + lax.rem(core + e, 2) for s, e in offsets]

    inverse, pieces = normalize(layer_input, norm_gain, targets, branch_total, rows // slots)
    near = branch_send(pieces[1], chips, 0, 1)
    direct = [branch_send(pieces[2 * s], chips, s, 0) for s in range(1, chips)]
    across = [branch_send(pieces[2 * s + 1], chips, s, 1) for s in range(1, chips)]
    turned = [pieces[0]] + direct + [near] + across
    order = lambda place: scatter_order(tensor_total)(place)
    ready = min(3, tensor_total)
    deltas, parts, delta_turned, centre, input_columns, gain_columns = attention_backward(
        layer_input,
        inverse,
        norm_gain,
        w_query,
        w_key,
        w_value,
        head_grad,
        parents,
        row_counts,
        slots,
        order,
        tensor_total,
        ready,
        shares,
    )
    if ready < tensor_total:
        weights = (w_query, w_key, w_value)
        parts += back_project(
            order, ready, tensor_total - ready, delta_turned, centre, weights, tensor_total
        )
    arrived = scatter_begin(parts, tensor_total)

    (delta,) = gate(deltas, (near, *direct, *across))
    sent = [branch_send(delta, chips, s, 0) for s in range(1, chips)]
    gathered = list(gate((delta, *sent), (parts[-1], *arrived)))
    parts, for_ends, for_inner, _ = scatter_end(parts, arrived, tensor_total)
    gathered += [branch_send(part, chips, 0, 1) for part in gathered]
    *weights, token = weight_gradients(turned, gathered, shares[0], kv_local, group, None)

    add = functools.partial(add_parts, for_ends, for_inner)
    gain_sum, total = gain_sums(add, input_columns, inverse, parts, token)
    grad_input = finish(width, add, total, input_columns, gain_columns, inverse, parts)
    if chips == 2:
        sums = [gain_sum] + [branch_send(gain_sum, chips, s, e) for s, e in offsets[1:]]
        grad_gain = total_of_four(sums, grad_input)
    else:
        grad_gain = lax.psum(gain_sum, "branch").reshape(column_width)
    return (grad_input, *weights, grad_gain)


def solution(mesh):
    placed = (
        P(("parts", "branch"), None),
        P(),
        P(None, "tensor"),
        P(None, "tensor"),
        P(None, "tensor"),
        P(("parts", "branch"), "tensor"),
        P(("parts", "branch")),
        P("parts"),
    )
    return jax.shard_map(
        local,
        mesh=mesh,
        in_specs=placed,
        out_specs=(
            P(("parts", "branch"), "tensor"),
            P(("parts", "branch"), "tensor"),
            P(("parts", "branch"), "tensor"),
            P(("parts", "branch"), "tensor"),
            P(("parts", "tensor")),
        ),
        check_vma=False,
    )
```

```python
import functools

import jax
import jax.numpy as jnp
from jax import lax
from jax.experimental import pallas as pl
from jax.experimental.pallas import tpu as pltpu
from jax.sharding import PartitionSpec as P

HEAD_DIM = 256
MIB = 1024 * 1024
CENTRE_ROWS = 16
VMEM_LIMIT = 64 * MIB


epsilon = 1e-06
softcap_limit = 50.0


def nn_dot(left, right):
    return lax.dot_general(
        left, right, (((1,), (0,)), ((), ())), preferred_element_type=jnp.float32
    )


def nt_dot(left, right):
    return lax.dot_general(
        left, right, (((1,), (1,)), ((), ())), preferred_element_type=jnp.float32
    )


def tn_dot(left, right):
    return lax.dot_general(
        left, right, (((0,), (0,)), ((), ())), preferred_element_type=jnp.float32
    )


def small_cost():
    return pl.CostEstimate(flops=1000000, bytes_accessed=100000, transcendentals=0)


def norm_kernel(targets, input_ref, gain_ref, inverse_ref, *rest):
    piece_refs, turned = rest[:-1], rest[-1]
    rows, width = input_ref.shape
    values = input_ref[...].astype(jnp.float32)
    inverse = lax.rsqrt(jnp.mean(values * values, axis=-1, keepdims=True) + epsilon)
    inverse_ref[...] = inverse
    gain = gain_ref[...].reshape(1, width)
    turned[...] = (values * inverse * (1.0 + gain)).astype(jnp.bfloat16).T
    depth = width // len(piece_refs)
    for target, piece_ref in zip(targets(), piece_refs):
        start = pl.multiple_of(target * depth, 16)
        piece_ref[...] = turned[pl.ds(start, depth), :]


def normalize(layer_input, norm_gain, targets, pieces, block):
    rows, width = layer_input.shape
    depth = width // pieces
    out = pl.pallas_call(
        functools.partial(norm_kernel, targets),
        out_shape=(jax.ShapeDtypeStruct((rows, 1), jnp.float32),)
        + (jax.ShapeDtypeStruct((depth, rows), jnp.bfloat16),) * pieces,
        grid=(rows // block,),
        in_specs=[
            pl.BlockSpec((block, width), lambda i: (i, 0)),
            pl.BlockSpec((width,), lambda i: (0,)),
        ],
        out_specs=(pl.BlockSpec((block, 1), lambda i: (i, 0)),)
        + (pl.BlockSpec((depth, block), lambda i: (0, i)),) * pieces,
        scratch_shapes=[pltpu.VMEM((width, block), jnp.bfloat16)],
        compiler_params=pltpu.CompilerParams(vmem_limit_bytes=VMEM_LIMIT),
        cost_estimate=small_cost(),
        name="norm",
    )(layer_input, norm_gain)
    return out[0], out[1:]


def ancestor_mask(parent_row):
    rows = parent_row.shape[1]
    row = lax.broadcasted_iota(jnp.int32, (rows, rows), 0)
    column = lax.broadcasted_iota(jnp.int32, (rows, rows), 1)
    reached = jnp.where((parent_row == row) | (row == column), 1.0, 0.0)
    for squaring in range(rows.bit_length() - 1):
        halfway = reached.astype(jnp.bfloat16)
        reached = jnp.minimum(nn_dot(halfway, halfway), 1.0)
    return reached.T


def attention_kernel(
    slots,
    group,
    kv_local,
    order,
    blocks,
    ready,
    columns,
    shares,
    count_ref,
    parent_ref,
    inverse_ref,
    gain_ref,
    input_hbm,
    query_hbm,
    key_hbm,
    value_hbm,
    grad_hbm,
    *rest,
):
    delta_hbm, rest = rest[: len(shares)], rest[len(shares) :]
    part_hbm, rest = rest[:ready], rest[ready:]
    turned_hbm, centre_out, rest = rest[:3], rest[3], rest[4:]
    column_hbm, column_gain_ref, rest = rest[0], rest[1], rest[2:]
    (
        input_ref,
        gain_row,
        query_ref,
        key_ref,
        value_ref,
        grad_ref,
        sum_ref,
        delta_ref,
        query_turned,
        key_turned,
        value_turned,
        allowed_ref,
        centre_ref,
        kept,
        load_sem,
        weight_sem,
        store_sem,
        part_sem,
    ) = rest
    head_dim = HEAD_DIM
    rows, width = input_ref.shape
    block = rows // slots
    mid = group * head_dim
    steps = weight_sem.shape[0]
    chunk = width // 7 if steps > 1 else width
    edges = [0] + [width - (steps - 1 - step) * 2 * chunk for step in range(steps)]
    weights = ((query_hbm, query_ref, mid, 0), (key_hbm, key_ref, head_dim, mid))
    weights += ((value_hbm, value_ref, head_dim, mid + head_dim),)

    def fetch(step, which):
        lines = pl.ds(edges[step], edges[step + 1] - edges[step])
        source, kept_ref = weights[which][:2]
        return pltpu.make_async_copy(
            source.at[lines, :], kept_ref.at[lines, :], weight_sem.at[step, which]
        )

    input_load = pltpu.make_async_copy(input_hbm, input_ref, load_sem.at[0])
    grad_load = pltpu.make_async_copy(grad_hbm, grad_ref, load_sem.at[1])
    input_load.start()
    for step in range(steps):
        for which in range(3):
            fetch(step, which).start()
    grad_load.start()
    gain_row[...] = gain_ref[...].reshape(1, width)

    first_count = lax.axis_index("branch") * slots
    parents = parent_ref[...].reshape(1, rows)
    for slot in range(slots):
        allowed_ref[slot] = ancestor_mask(parents[:, slot * block : (slot + 1) * block])
    inverse = inverse_ref[...]
    input_load.wait()
    stores = []
    if columns:
        start = pl.multiple_of(lax.axis_index("tensor") * columns, 128)
        stores.append(
            pltpu.make_async_copy(
                input_ref.at[:, pl.ds(start, columns)], column_hbm, store_sem.at[0]
            )
        )
        stores[0].start()
        column_gain_ref[...] = gain_row[:, pl.ds(start, columns)]
    else:
        column_gain_ref[...] = jnp.zeros_like(column_gain_ref)

    for step in range(steps):
        lines = slice(edges[step], edges[step + 1])
        gain = 1.0 + gain_row[:, lines]
        normed = (input_ref[:, lines].astype(jnp.float32) * inverse * gain).astype(jnp.bfloat16)
        for which, (_, kept_ref, wide, place) in enumerate(weights):
            fetch(step, which).wait()
            term = nn_dot(normed, kept_ref[lines, :])
            for h in range(kv_local):
                part = term[:, h * wide : (h + 1) * wide]
                if step > 0:
                    part = part + sum_ref[h, :, place : place + wide]
                sum_ref[h, :, place : place + wide] = part
    grad_load.wait()
    scale = head_dim ** (-0.5)
    centre_ref[...] = jnp.zeros_like(centre_ref)

    def attend(h):
        for slot in range(slots):
            lines = slice(slot * block, (slot + 1) * block)
            live = (
                lax.broadcasted_iota(jnp.int32, (block, mid), 0) < count_ref[first_count + slot]
            )
            columns = slice(h * mid, (h + 1) * mid)
            grad_rows = jnp.where(live, grad_ref[lines, columns].astype(jnp.float32), 0.0)
            pair = [slice(g * head_dim, (g + 1) * head_dim) for g in range(group)]
            grads = jnp.concatenate([grad_rows[:, p] for p in pair], axis=0).astype(jnp.bfloat16)
            queries = jnp.concatenate([sum_ref[h, lines, p] for p in pair], axis=0)
            queries = queries.astype(jnp.bfloat16)
            keys = sum_ref[h, lines, mid : mid + head_dim].astype(jnp.bfloat16)
            values = sum_ref[h, lines, mid + head_dim :].astype(jnp.bfloat16)
            allowed = jnp.concatenate([allowed_ref[slot]] * group, axis=0)
            bounded = jnp.tanh(nt_dot(queries, keys) * (scale / softcap_limit))
            weighted = allowed * jnp.exp(softcap_limit * bounded)
            probabilities = weighted * (1.0 / jnp.sum(weighted, axis=-1, keepdims=True))
            d_probs = nt_dot(grads, values)
            d_scores = probabilities * (
                d_probs - jnp.sum(probabilities * d_probs, axis=-1, keepdims=True)
            )
            d_raw = (d_scores * (1.0 - bounded * bounded) * scale).astype(jnp.bfloat16)
            prob_half = probabilities.astype(jnp.bfloat16)
            d_query = nn_dot(d_raw, keys)
            d_key = tn_dot(d_raw, queries)
            d_value = tn_dot(prob_half, grads)
            places = [
                (d_query[g * block : (g + 1) * block], query_turned, h * mid + g * head_dim)
                for g in range(group)
            ]
            places += [(d_key, key_turned, h * head_dim), (d_value, value_turned, h * head_dim)]
            product = None
            for which, (part, turned_ref, start) in enumerate(places):
                half = part.astype(jnp.bfloat16)
                line = which * rows + slot * block
                delta_ref[h, line : line + block, :] = half
                spot = slice(start, start + head_dim)
                turned_ref[spot, lines] = half.T
                term = half.astype(jnp.float32) * sum_ref[
                    h, lines, which * head_dim : (which + 1) * head_dim
                ]
                product = term if product is None else product + term
            centre_ref[lines, :] += jnp.sum(product, axis=-1, keepdims=True)

    for h in range(kv_local):
        attend(h)
    lasts = []
    for share, out in zip(shares, delta_hbm):
        for place, block_index in enumerate(share):
            h, which = divmod(block_index, group + 2)
            lasts.append(
                pltpu.make_async_copy(
                    delta_ref.at[h, pl.ds(which * rows, rows), :],
                    out.at[pl.ds(place * rows, rows), :],
                    store_sem.at[1 + len(lasts)],
                )
            )
    for which, turned_ref in enumerate((query_turned, key_turned, value_turned)):
        lasts.append(
            pltpu.make_async_copy(turned_ref, turned_hbm[which], store_sem.at[1 + len(lasts)])
        )
    for store in lasts:
        store.start()

    centre = jnp.broadcast_to(centre_ref[...], (rows, 128)).T[:CENTRE_ROWS].astype(jnp.bfloat16)
    centre_out[...] = centre
    span = width // blocks
    cuts = 2
    cut_lines = span // cuts
    parts = [
        pltpu.make_async_copy(kept.at[place], part_hbm[place], part_sem.at[place])
        for place in range(ready)
    ]

    def project_back(step, carry):
        place, cut = step // cuts, lax.rem(step, cuts)
        lines = pl.ds(pl.multiple_of(order(place) * span + cut * cut_lines, 16), cut_lines)
        total = nn_dot(query_ref[lines, :], query_turned[...])
        total += nn_dot(key_ref[lines, :], key_turned[...])
        total += nn_dot(value_ref[lines, :], value_turned[...])
        spot = pl.ds(pl.multiple_of(cut * cut_lines, 16), cut_lines)
        kept[place, spot, :] = total.astype(jnp.bfloat16)
        for which, part in enumerate(parts):

            @pl.when((place == which) & (cut == cuts - 1))
            def _():
                kept[which, span:, :] = centre
                part.start()

        return carry

    lax.fori_loop(0, ready * cuts, project_back, 0)
    for store in stores + lasts + parts:
        store.wait()


def attention_backward(
    layer_input,
    inverse,
    norm_gain,
    w_query,
    w_key,
    w_value,
    head_grad,
    parents,
    counts,
    slots,
    order,
    blocks,
    ready,
    shares,
):
    rows, width = layer_input.shape
    kv_local = w_key.shape[1] // HEAD_DIM
    group = w_query.shape[1] // w_key.shape[1]
    span = (group + 2) * HEAD_DIM
    stack = (group + 2) * rows
    column_width = width // blocks
    cut = column_width % 128 == 0
    wide = column_width if cut else 128
    steps = 4 if width % (7 * 256) == 0 else 1
    part_shape = (column_width + CENTRE_ROWS, rows)
    hbm = pl.BlockSpec(memory_space=pl.ANY)
    vmem = pl.BlockSpec(memory_space=pltpu.VMEM)
    half = lambda *shape: jax.ShapeDtypeStruct(shape, jnp.bfloat16)
    out = pl.pallas_call(
        functools.partial(
            attention_kernel,
            slots,
            group,
            kv_local,
            order,
            blocks,
            ready,
            wide if cut else 0,
            shares,
        ),
        out_shape=tuple(half(len(share) * rows, HEAD_DIM) for share in shares)
        + (half(*part_shape),) * ready
        + tuple(half(w.shape[1], rows) for w in (w_query, w_key, w_value))
        + (half(CENTRE_ROWS, rows),)
        + (half(rows, wide), jax.ShapeDtypeStruct((1, wide), jnp.float32)),
        in_specs=[pl.BlockSpec(memory_space=pltpu.SMEM), vmem, vmem, vmem] + [hbm] * 5,
        out_specs=(hbm,) * (len(shares) + ready + 3) + (vmem, hbm, vmem),
        scratch_shapes=[
            pltpu.VMEM((rows, width), jnp.bfloat16),
            pltpu.VMEM((1, width), jnp.float32),
            pltpu.VMEM(w_query.shape, jnp.bfloat16),
            pltpu.VMEM(w_key.shape, jnp.bfloat16),
            pltpu.VMEM(w_value.shape, jnp.bfloat16),
            pltpu.VMEM(head_grad.shape, jnp.bfloat16),
            pltpu.VMEM((kv_local, rows, span), jnp.float32),
            pltpu.VMEM((kv_local, stack, HEAD_DIM), jnp.bfloat16),
            pltpu.VMEM((w_query.shape[1], rows), jnp.bfloat16),
            pltpu.VMEM((w_key.shape[1], rows), jnp.bfloat16),
            pltpu.VMEM((w_value.shape[1], rows), jnp.bfloat16),
            pltpu.VMEM((slots, rows // slots, rows // slots), jnp.float32),
            pltpu.VMEM((rows, 1), jnp.float32),
            pltpu.VMEM((ready, *part_shape), jnp.bfloat16),
            pltpu.SemaphoreType.DMA((2,)),
            pltpu.SemaphoreType.DMA((steps, 3)),
            pltpu.SemaphoreType.DMA((4 + kv_local * (group + 2),)),
            pltpu.SemaphoreType.DMA((ready,)),
        ],
        compiler_params=pltpu.CompilerParams(vmem_limit_bytes=VMEM_LIMIT),
        cost_estimate=small_cost(),
        name="attention",
    )(counts, parents, inverse, norm_gain, layer_input, w_query, w_key, w_value, head_grad)
    deltas, out = out[: len(shares)], out[len(shares) :]
    parts, turned, centre = out[:ready], out[ready : ready + 3], out[ready + 3]
    if cut:
        input_cut, gain_cut = out[-2], out[-1]
    else:
        start = lax.axis_index("tensor") * column_width
        input_cut = lax.dynamic_slice_in_dim(layer_input, start, column_width, 1)
        gain_cut = lax.dynamic_slice_in_dim(norm_gain, start, column_width, 0)
        gain_cut = gain_cut.reshape(1, column_width)
    return deltas, parts, turned, centre, input_cut, gain_cut


def back_kernel(centre_ref, *refs):
    turned_refs, weight_refs, out_refs = refs[:3], refs[3:6], refs[6:]
    piece, cut = pl.program_id(0), pl.program_id(1)
    lines = weight_refs[0].shape[0]
    total = None
    for weight_ref, turned_ref in zip(weight_refs, turned_refs):
        term = nn_dot(weight_ref[...], turned_ref[...])
        total = term if total is None else total + term
    total = total.astype(jnp.bfloat16)
    start = pl.multiple_of(cut * lines, 16)
    depth = out_refs[0].shape[0] - CENTRE_ROWS
    for place, out_ref in enumerate(out_refs):

        @pl.when(piece == place)
        def _():
            out_ref[pl.ds(start, lines), :] = total
            out_ref[depth:, :] = centre_ref[...]


def back_project(order, first, pieces, turned, centre, weights, blocks):
    rows = centre.shape[1]
    depth = weights[0].shape[0] // blocks
    cuts = 2
    whole = lambda i, j: (0, 0)
    return pl.pallas_call(
        back_kernel,
        out_shape=(jax.ShapeDtypeStruct((depth + CENTRE_ROWS, rows), jnp.bfloat16),) * pieces,
        grid=(pieces, cuts),
        in_specs=[pl.BlockSpec(x.shape, whole) for x in (centre, *turned)]
        + [
            pl.BlockSpec((depth // cuts, w.shape[1]), lambda i, j: (order(first + i) * cuts + j, 0))
            for w in weights
        ],
        out_specs=(pl.BlockSpec((depth + CENTRE_ROWS, rows), whole),) * pieces,
        compiler_params=pltpu.CompilerParams(vmem_limit_bytes=VMEM_LIMIT),
        cost_estimate=small_cost(),
        name="back",
    )(centre, *turned, *weights)


def weight_kernel(outs, sources, *refs):
    turned_hbm, delta_hbm = refs[:sources], refs[sources : 2 * sources]
    out_hbm, token_ref = refs[-10:-7], refs[-7]
    turned_ref, delta_ref, kept, turned_sem, delta_sem, store_sem = refs[-6:]
    token_ref[...] = jnp.zeros_like(token_ref)
    rows = turned_ref.shape[2]
    loads = []
    for place in range(sources):
        loads.append(
            pltpu.make_async_copy(
                turned_hbm[place], turned_ref.at[place], turned_sem.at[place]
            )
        )
    for load in loads:
        load.start()

    def fetch(block, place):
        lines = pl.ds(pl.multiple_of(block * rows, rows), rows)
        return pltpu.make_async_copy(
            delta_hbm[place].at[lines, :], delta_ref.at[place, lines, :], delta_sem.at[block, place]
        )

    for block in range(len(outs)):
        for place in range(sources):
            fetch(block, place).start()
    for load in loads:
        load.wait()
    stores = [
        pltpu.make_async_copy(
            kept.at[block],
            out_hbm[which].at[:, pl.ds(column * HEAD_DIM, HEAD_DIM)],
            store_sem.at[block],
        )
        for block, (which, column) in enumerate(outs)
    ]

    def fill(block, carry):
        lines = pl.ds(pl.multiple_of(block * rows, rows), rows)
        total = None
        for place in range(sources):
            fetch(block, place).wait()
        for place in range(sources):
            term = nn_dot(turned_ref[place], delta_ref[place, lines, :])
            total = term if total is None else total + term
        kept[block] = total
        for which, store in enumerate(stores):

            @pl.when(block == which)
            def _():
                store.start()

        return carry

    lax.fori_loop(0, len(outs), fill, 0)
    for store in stores:
        store.wait()


def weight_gradients(turned, deltas, share, kv_local, group, before):
    depth, rows = turned[0].shape
    sources = len(turned)
    outs = []
    for block in share:
        h, which = divmod(block, group + 2)
        outs.append((0, h * group + which) if which < group else (which - group + 1, h))
    kept = list(before) if before is not None else []
    hbm = pl.BlockSpec(memory_space=pl.ANY)
    return pl.pallas_call(
        functools.partial(weight_kernel, outs, sources),
        out_shape=(
            jax.ShapeDtypeStruct((depth, kv_local * group * HEAD_DIM), jnp.float32),
            jax.ShapeDtypeStruct((depth, kv_local * HEAD_DIM), jnp.float32),
            jax.ShapeDtypeStruct((depth, kv_local * HEAD_DIM), jnp.float32),
            jax.ShapeDtypeStruct((8, 128), jnp.float32),
        ),
        in_specs=[hbm] * (2 * sources + len(kept)),
        out_specs=(hbm,) * 3 + (pl.BlockSpec(memory_space=pltpu.VMEM),),
        input_output_aliases={2 * sources + i: i for i in range(len(kept))},
        scratch_shapes=[
            pltpu.VMEM((sources, depth, rows), jnp.bfloat16),
            pltpu.VMEM((sources, len(share) * rows, HEAD_DIM), jnp.bfloat16),
            pltpu.VMEM((len(share), depth, HEAD_DIM), jnp.float32),
            pltpu.SemaphoreType.DMA((sources,)),
            pltpu.SemaphoreType.DMA((len(share), sources)),
            pltpu.SemaphoreType.DMA((len(share),)),
        ],
        compiler_params=pltpu.CompilerParams(vmem_limit_bytes=VMEM_LIMIT),
        cost_estimate=small_cost(),
        name="weights",
    )(*turned, *deltas, *kept)


def gate_kernel(*refs):
    del refs


def gate(arrays, tokens):
    hbm = pl.BlockSpec(memory_space=pl.ANY)
    return pl.pallas_call(
        gate_kernel,
        out_shape=tuple(jax.ShapeDtypeStruct(x.shape, x.dtype) for x in arrays),
        in_specs=[hbm] * (len(arrays) + len(tokens)),
        out_specs=(hbm,) * len(arrays),
        input_output_aliases={i: i for i in range(len(arrays))},
        compiler_params=pltpu.CompilerParams(vmem_limit_bytes=VMEM_LIMIT),
        cost_estimate=small_cost(),
        name="gate",
    )(*arrays, *tokens)


def join_kernel(inner_ref, other_ref, end_ref, *rest):
    out_ref, token_ref = rest[-2:]
    token_ref[...] = jnp.zeros_like(token_ref)
    index = lax.axis_index("tensor")
    inner = (index > 0) & (index < lax.axis_size("tensor") - 1)

    @pl.when(inner)
    def _():
        out_ref[...] = (
            inner_ref[...].astype(jnp.float32) + other_ref[...].astype(jnp.float32)
        ).astype(jnp.bfloat16)

    @pl.when(jnp.logical_not(inner))
    def _():
        out_ref[...] = end_ref[...]


def join(inner_part, other, end_part, tokens):
    lines, rows = end_part.shape
    cuts = 3 if lines % 48 == 0 else 1
    some = pl.BlockSpec((lines // cuts, rows), lambda i: (i, 0))
    return pl.pallas_call(
        join_kernel,
        out_shape=(
            jax.ShapeDtypeStruct(end_part.shape, end_part.dtype),
            jax.ShapeDtypeStruct((8, 128), jnp.float32),
        ),
        grid=(cuts,),
        in_specs=[some] * 3 + [pl.BlockSpec(memory_space=pl.ANY)] * len(tokens),
        out_specs=(some, pl.BlockSpec((8, 128), lambda i: (0, 0))),
        compiler_params=pltpu.CompilerParams(vmem_limit_bytes=VMEM_LIMIT),
        cost_estimate=small_cost(),
        name="join",
    )(inner_part, other, end_part, *tokens)


def add_parts(for_ends, for_inner, part_refs):
    index = lax.axis_index("tensor")
    ends = ((index == 0) | (index == lax.axis_size("tensor") - 1)).astype(jnp.float32)
    total = None
    for place, part_ref in enumerate(part_refs):
        part = part_ref[...].astype(jnp.float32)
        if place < for_ends:
            part = part * ends
        elif place < for_ends + for_inner:
            part = part * (1.0 - ends)
        total = part if total is None else total + part
    return total


def gain_kernel(add, count, input_ref, inverse_ref, *refs):
    part_refs, (sum_ref, total_ref) = refs[:count], refs[-2:]

    @pl.when(pl.program_id(0) == 0)
    def _():
        sum_ref[...] = jnp.zeros_like(sum_ref)

    d_normed = add(part_refs).T
    total_ref[...] = d_normed
    scaled = input_ref[...].astype(jnp.float32) * inverse_ref[...]
    sum_ref[...] += jnp.sum(d_normed * scaled, axis=0, keepdims=True)


def gain_sums(add, input_columns, inverse, parts, token):
    rows, wide = input_columns.shape
    some = 128
    return pl.pallas_call(
        functools.partial(gain_kernel, add, len(parts)),
        out_shape=(
            jax.ShapeDtypeStruct((1, wide), jnp.float32),
            jax.ShapeDtypeStruct((rows, wide), jnp.float32),
        ),
        grid=(rows // some,),
        in_specs=[
            pl.BlockSpec((some, wide), lambda i: (i, 0)),
            pl.BlockSpec((some, 1), lambda i: (i, 0)),
        ]
        + [pl.BlockSpec((wide, some), lambda i: (0, i))] * len(parts)
        + [pl.BlockSpec(memory_space=pl.ANY)],
        out_specs=(
            pl.BlockSpec((1, wide), lambda i: (0, 0)),
            pl.BlockSpec((some, wide), lambda i: (i, 0)),
        ),
        compiler_params=pltpu.CompilerParams(vmem_limit_bytes=VMEM_LIMIT),
        cost_estimate=small_cost(),
        name="gains",
    )(input_columns, inverse, *parts, token)


def finish_kernel(width, add, total_ref, input_ref, gain_ref, inverse_ref, *refs):
    centre_refs, out_ref = refs[:-1], refs[-1]
    centre = add(centre_refs).T[:, :1] * (1.0 / width)
    inverse = inverse_ref[...]
    scaled = input_ref[...].astype(jnp.float32) * inverse
    out_ref[...] = (
        inverse * ((1.0 + gain_ref[...]) * total_ref[...] - scaled * centre)
    ).astype(jnp.bfloat16)


def finish(width, add, total, input_columns, gain_columns, inverse, parts):
    rows, wide = input_columns.shape
    some = 128
    row_block = pl.BlockSpec((some, wide), lambda i: (i, 0))
    return pl.pallas_call(
        functools.partial(finish_kernel, width, add),
        out_shape=jax.ShapeDtypeStruct((rows, wide), jnp.bfloat16),
        grid=(rows // some,),
        in_specs=[
            row_block,
            row_block,
            pl.BlockSpec((1, wide), lambda i: (0, 0)),
            pl.BlockSpec((some, 1), lambda i: (i, 0)),
        ]
        + [pl.BlockSpec((CENTRE_ROWS, some), lambda i: (wide // CENTRE_ROWS, i))] * len(parts),
        out_specs=row_block,
        compiler_params=pltpu.CompilerParams(vmem_limit_bytes=VMEM_LIMIT),
        cost_estimate=small_cost(),
        name="finish",
    )(total, input_columns, gain_columns, inverse, *parts)


def total_kernel(*refs):
    total = (refs[0][...] + refs[1][...]) + (refs[2][...] + refs[3][...])
    refs[-1][...] = total.reshape(refs[-1].shape)


def total_of_four(arrays, token):
    whole = pl.BlockSpec(arrays[0].shape, lambda i: (0, 0))
    wide = arrays[0].shape[1]
    return pl.pallas_call(
        total_kernel,
        out_shape=jax.ShapeDtypeStruct((wide,), arrays[0].dtype),
        grid=(1,),
        in_specs=[whole] * 4 + [pl.BlockSpec(memory_space=pl.ANY)],
        out_specs=pl.BlockSpec((wide,), lambda i: (0,)),
        compiler_params=pltpu.CompilerParams(vmem_limit_bytes=VMEM_LIMIT),
        cost_estimate=small_cost(),
        name="total",
    )(*arrays, token)


def branch_send(array, chips, shift, swap):
    pairs = [
        (c * 2 + k, ((c + shift) % chips) * 2 + (k ^ swap)) for c in range(chips) for k in range(2)
    ]
    return lax.ppermute(array, "branch", pairs)


def pick(table, index):
    chosen = table[-1]
    for place in range(len(table) - 2, -1, -1):
        chosen = jnp.where(index == place, table[place], chosen)
    return chosen


def scatter_order(total):
    index = lax.axis_index("tensor")
    if total != 4:
        return lambda place: lax.rem(index + place + 1, total)
    table = [[3, 0, 3, 0], [0, 2, 1, 3], [2, 3, 0, 1], [1, 1, 2, 2]]
    here = [pick(row, index) for row in table]
    return lambda place: pick(here, place)


def scatter_begin(parts, total):
    if total != 4:
        return [
            lax.ppermute(part, "tensor", [(t, (t + shift) % total) for t in range(total)])
            for shift, part in zip(range(1, total), parts[:-1])
        ]
    from_first = lax.ppermute(parts[0], "tensor", [(0, 1), (1, 0), (2, 3), (3, 2)])
    from_inner = lax.ppermute(parts[1], "tensor", [(1, 2), (2, 1)])
    from_ends = lax.ppermute(parts[2], "tensor", [(0, 2), (3, 1)])
    return from_first, from_inner, from_ends


def scatter_end(parts, arrived, total):
    if total != 4:
        return [parts[-1], *arrived], 0, 0, arrived[0]
    from_first, from_inner, from_ends = arrived
    joined, token = join(parts[2], from_first, parts[3], (from_inner, from_ends))
    from_joined = lax.ppermute(joined, "tensor", [(1, 3), (2, 0), (0, 1), (3, 2)])
    return [from_first, parts[1], parts[3], from_inner, from_ends, from_joined], 2, 1, token


def local(layer_input, norm_gain, w_query, w_key, w_value, head_grad, parents, row_counts):
    branch_total = lax.axis_size("branch")
    tensor_total = lax.axis_size("tensor")
    slots = row_counts.shape[0] // branch_total
    rows, width = layer_input.shape
    column_width = width // tensor_total
    chips = branch_total // 2
    group = w_query.shape[1] // w_key.shape[1]
    kv_local = w_key.shape[1] // HEAD_DIM
    offsets = [(shift, swap) for shift in range(chips) for swap in range(2)]
    shares = [list(range(kv_local * (group + 2)))]

    def targets():
        index = lax.axis_index("branch")
        chip, core = index // 2, index % 2
        return [lax.rem(chip + s, chips) * 2 + lax.rem(core + e, 2) for s, e in offsets]

    inverse, pieces = normalize(layer_input, norm_gain, targets, branch_total, rows // slots)
    near = branch_send(pieces[1], chips, 0, 1)
    direct = [branch_send(pieces[2 * s], chips, s, 0) for s in range(1, chips)]
    across = [branch_send(pieces[2 * s + 1], chips, s, 1) for s in range(1, chips)]
    turned = [pieces[0]] + direct + [near] + across
    order = lambda place: scatter_order(tensor_total)(place)
    ready = min(3, tensor_total)
    deltas, parts, delta_turned, centre, input_columns, gain_columns = attention_backward(
        layer_input,
        inverse,
        norm_gain,
        w_query,
        w_key,
        w_value,
        head_grad,
        parents,
        row_counts,
        slots,
        order,
        tensor_total,
        ready,
        shares,
    )
    if ready < tensor_total:
        weights = (w_query, w_key, w_value)
        parts += back_project(
            order, ready, tensor_total - ready, delta_turned, centre, weights, tensor_total
        )
    arrived = scatter_begin(parts, tensor_total)

    (delta,) = gate(deltas, (near, *direct, *across))
    sent = [branch_send(delta, chips, s, 0) for s in range(1, chips)]
    gathered = list(gate((delta, *sent), (parts[-1], *arrived)))
    parts, for_ends, for_inner, _ = scatter_end(parts, arrived, tensor_total)
    gathered += [branch_send(part, chips, 0, 1) for part in gathered]
    *weights, token = weight_gradients(turned, gathered, shares[0], kv_local, group, None)

    add = functools.partial(add_parts, for_ends, for_inner)
    gain_sum, total = gain_sums(add, input_columns, inverse, parts, token)
    grad_input = finish(width, add, total, input_columns, gain_columns, inverse, parts)
    if chips == 2:
        sums = [gain_sum] + [branch_send(gain_sum, chips, s, e) for s, e in offsets[1:]]
        grad_gain = total_of_four(sums, grad_input)
    else:
        grad_gain = lax.psum(gain_sum, "branch").reshape(column_width)
    return (grad_input, *weights, grad_gain)


def solution(mesh):
    placed = (
        P(("parts", "branch"), None),
        P(),
        P(None, "tensor"),
        P(None, "tensor"),
        P(None, "tensor"),
        P(("parts", "branch"), "tensor"),
        P(("parts", "branch")),
        P("parts"),
    )
    return jax.shard_map(
        local,
        mesh=mesh,
        in_specs=placed,
        out_specs=(
            P(("parts", "branch"), "tensor"),
            P(("parts", "branch"), "tensor"),
            P(("parts", "branch"), "tensor"),
            P(("parts", "branch"), "tensor"),
            P(("parts", "tensor")),
        ),
        check_vma=False,
    )
```
